256 devices in a mesh: seq: 32 (over y_lo, z, core), band: 8 (over x, y_hi).
Axes of the slice: x: 4, y: 4 (y_hi: 2, y_lo: 2; y = y_hi * 2 + y_lo), z: 8, core: 2. Of those that a mesh axis runs over, the one named last changes fastest.
Arguments:
- tokens: bfloat16 [32, 1024, 768], P('seq', 'band'), may hold values from -6 to 6
- image_ids: int32 [32, 1024], P('seq', 'band'), may hold values from 0 to 3, as said below
- ln1_gain: bfloat16 [768], P(('seq', 'band')), may hold values from 0.25 to 1.75
- ln1_bias: bfloat16 [768], P(('seq', 'band')), may hold values from -1.75 to 1.75
- w_qkv: bfloat16 [768, 2304], P(('seq', 'band')), may hold values from -0.21875 to 0.21875
- qv_bias: bfloat16 [1536], P(('seq', 'band')), may hold values from -3 to 3
- w_out: bfloat16 [768, 768], P(('seq', 'band')), may hold values from -3.5 to 3.5
- out_bias: bfloat16 [768], P(('seq', 'band')), may hold values from -1.75 to 1.75
- ln2_gain: bfloat16 [768], P(('seq', 'band')), may hold values from 0.25 to 1.75
- ln2_bias: bfloat16 [768], P(('seq', 'band')), may hold values from -1.75 to 1.75
- w_up: bfloat16 [768, 3072], P(('seq', 'band')), may hold values from -0.21875 to 0.21875
- up_bias: bfloat16 [3072], P(('seq', 'band')), may hold values from -3 to 3
- w_down: bfloat16 [3072, 768], P(('seq', 'band')), may hold values from -0.109375 to 0.109375
- down_bias: bfloat16 [768], P(('seq', 'band')), may hold values from -1.75 to 1.75
- cotangent: bfloat16 [32, 1024, 768], P('seq', 'band'), may hold values from -6 to 6
Outputs:
- output: bfloat16 [32, 1024, 768], P('seq', 'band')
- tokens_grad: bfloat16 [32, 1024, 768], P('seq', 'band')
- ln1_gain_grad: float32 [768], P(('seq', 'band'))
- ln1_bias_grad: float32 [768], P(('seq', 'band'))
- w_qkv_grad: float32 [768, 2304], P(('seq', 'band'))
- qv_bias_grad: float32 [1536], P(('seq', 'band'))
- w_out_grad: float32 [768, 768], P(('seq', 'band'))
- out_bias_grad: float32 [768], P(('seq', 'band'))
- ln2_gain_grad: float32 [768], P(('seq', 'band'))
- ln2_bias_grad: float32 [768], P(('seq', 'band'))
- w_up_grad: float32 [768, 3072], P(('seq', 'band'))
- up_bias_grad: float32 [3072], P(('seq', 'band'))
- w_down_grad: float32 [3072, 768], P(('seq', 'band'))
- down_bias_grad: float32 [768], P(('seq', 'band'))
The draws below stay inside these ranges and needn't reach their ends.
Inputs may be any that keep to these rules, and one draw needn't show every extreme that they name: `image_ids`: within a sequence the ids never fall. Each sequence is either one image of 1024 tokens with every id 0, or images of 256 tokens with ids 0, 1, 2, 3 in order; which sequences are which is drawn from the seed, and both kinds occur in every draw.
All inputs are finite; a program needn't handle non-finite values.
Results may differ from the reference program's by a relative error of at most 0.025.
Values may be sent and summed in bfloat16 or wider, within the bound.
No kernel may reach another device: no remote copies, remote signals or barrier semaphores. Data moves between devices by JAX's collectives and lax.ppermute only.
A program may use at most 192 MiB of HBM per device.

```python
import jax
import jax.numpy as jnp
from jax import lax

D = 768
HEADS = 16
HEAD_DIM = 48
FF = 3072
LEN = 1024
IMG = 256
SEQS = 32


def draw_image_ids(key, part):
    key = jax.random.fold_in(key, 7)
    key_flags, key_first, key_step = jax.random.split(key, 3)
    flags = jax.random.randint(key_flags, (SEQS,), 0, 2) == 0
    first = jax.random.randint(key_first, (), 0, SEQS)
    step = jax.random.randint(key_step, (), 1, SEQS)
    second = (first + step) % SEQS
    seq_rows = jnp.arange(SEQS)
    single = (flags | (seq_rows == first)) & (seq_rows != second)
    positions = jnp.arange(LEN)
    small_ids = (positions // IMG)[None, :]
    image_ids = jnp.where(single.reshape(SEQS, 1), 0, small_ids)
    return image_ids.astype(jnp.int32)


def with_spikes(drawn, stream_key, source, target, shards_of, factor):
    def block_of(position):
        return (jnp.arange(drawn.shape[position]) // (drawn.shape[position] // shards_of)).reshape((-1,) + (1,) * (drawn.ndim - 1 - position))

    one_side = jax.random.permutation(stream_key, shards_of)[block_of(target)]
    other_side = (block_of(target) + shards_of // 2) % shards_of
    return jnp.where((block_of(source) == one_side) | (block_of(source) == other_side), factor * drawn, drawn)


def levels(rng, extent, pieces, least, top_value):
    factor_of, own = 1.0, jax.random.fold_in(rng, 6)
    for position, shards_of in pieces:
        heights = jnp.exp(jax.random.uniform(jax.random.fold_in(own, position), (shards_of,), jnp.float32, least / len(pieces), top_value / len(pieces)))
        factor_of = factor_of * jnp.repeat(heights, extent[position] // shards_of).reshape([-1 if axis == position else 1 for axis in range(len(extent))])
    return factor_of


def centred(rng, extent, deviation, reach, pieces=(), dtype=jnp.bfloat16):
    drawn = jax.random.normal(rng, extent, jnp.float32) * deviation
    if len(pieces) > 0:
        drawn = levels(rng, extent, pieces, -0.22, 0.18) * drawn
    return jnp.clip(drawn, min=-reach, max=reach).astype(dtype)


def bell_draw_with(key, shape, width, bound, cuts, heavy, held_as=jnp.bfloat16):
    array = width * jax.random.normal(key, shape, jnp.float32)
    if cuts:
        array = array * levels(key, shape, cuts, -0.22, 0.18)
    return jnp.clip(with_spikes(array, jax.random.fold_in(key, 3), *heavy), -bound, bound).astype(held_as)


def setup_inputs(seed: int = 0) -> dict:
    key_of = jax.random.split(jax.random.key(seed), 16)
    return {
        "tokens": centred(key_of[0], (SEQS, LEN, D), 1.0, 6.0, ((0, 32), (1, 8))),
        "image_ids": draw_image_ids(jax.random.fold_in(key_of[15], 71), 0),
        "ln1_gain": jnp.clip(1.0 + 0.15 * jax.random.normal(key_of[2], (D,), jnp.float32), 0.25, 1.75).astype(jnp.bfloat16),
        "ln1_bias": centred(key_of[3], (D,), 0.3, 1.75, ((0, 256),)),
        "w_qkv": centred(key_of[4], (D, 3 * D), D ** -0.5, 0.21875, ((0, 256),)),
        "qv_bias": centred(key_of[5], (2 * D,), 0.5, 3.0, ((0, 256),)),
        "w_out": centred(key_of[6], (D, D), (max(D * 4 // LEN, 1)) ** -0.5, 3.5, ((0, 256),)),
        "out_bias": centred(key_of[7], (D,), 0.3, 1.75, ((0, 256),)),
        "ln2_gain": jnp.clip(1.0 + 0.15 * jax.random.normal(key_of[8], (D,), jnp.float32), 0.25, 1.75).astype(jnp.bfloat16),
        "ln2_bias": centred(key_of[9], (D,), 0.3, 1.75, ((0, 256),)),
        "w_up": centred(key_of[10], (D, FF), D ** -0.5, 0.21875, ((0, 256),)),
        "up_bias": centred(key_of[11], (FF,), 0.5, 3.0, ((0, 256),)),
        "w_down": centred(key_of[12], (FF, D), FF ** -0.5, 0.109375, ((0, 256),)),
        "down_bias": centred(key_of[13], (D,), 0.3, 1.75, ((0, 256),)),
        "cotangent": bell_draw_with(key_of[14], (SEQS, LEN, D), 1.0, 6.0, ((0, 32), (1, 8)), (0, 2, 32, 2.75)),
    }


@jax.custom_vjp
def low(v):
    return lax.optimization_barrier(v.astype(jnp.bfloat16)).astype(jnp.float32)

@jax.custom_vjp
def low_back(v):
    return v

def low_keep(v):
    return (low(v), None)

def low_pass(kept, grad):
    return (grad,)

def back_keep(v):
    return (v, None)

def back_low(kept, grad):
    return (low(grad),)
low.defvjp(low_keep, low_pass)
low_back.defvjp(back_keep, back_low)
NORM_EPS = 1e-05
MASK_FILL = -1e+30
HIGHEST_PREC = lax.Precision.HIGHEST

def layer_norm(values, norm_gain, offset):
    center = lax.optimization_barrier(jnp.mean(values, axis=-1, keepdims=True))
    centered = values - center
    spread = lax.optimization_barrier(jnp.mean(centered * centered, axis=-1, keepdims=True))
    return centered * lax.rsqrt(spread + NORM_EPS) * norm_gain + offset

def project(values, weight):
    return jnp.einsum('gld,de->gle', values, weight, precision=HIGHEST_PREC)

def block(params, inputs, group_ids):
    ln1_gain, ln1_bias, w_qkv, qv_bias, w_out, out_bias, ln2_gain, ln2_bias, w_up, up_bias, w_down, down_bias = params
    groups = inputs.shape[0]
    normed = low(layer_norm(inputs, ln1_gain, ln1_bias))
    qkv_mixed = project(normed, w_qkv)
    queries = low_back(low(qkv_mixed[..., :D] + qv_bias[:D]))
    keys_all = low_back(low(qkv_mixed[..., D:2 * D]))
    values_all = low_back(low(qkv_mixed[..., 2 * D:] + qv_bias[D:]))
    head_shape = (groups, LEN, HEADS, HEAD_DIM)
    scores = jnp.einsum('gqhe,gkhe->ghqk', queries.reshape(head_shape), keys_all.reshape(head_shape), precision=HIGHEST_PREC)
    scores = low_back(scores * HEAD_DIM ** (-0.5))
    same_image = (group_ids[:, :, None] == group_ids[:, None, :])[:, None]
    scores = jnp.where(same_image, scores, MASK_FILL)
    totals = jax.nn.logsumexp(scores, axis=-1, keepdims=True)
    weights = low(jnp.exp(scores - totals))
    attended = jnp.einsum('ghqk,gkhe->gqhe', weights, values_all.reshape(head_shape), precision=HIGHEST_PREC)
    attended = low_back(low(attended.reshape(groups, LEN, D)))
    residual = inputs + low_back(project(attended, w_out) + out_bias)
    normed2 = low(layer_norm(residual, ln2_gain, ln2_bias))
    up_values = low_back(project(normed2, w_up) + up_bias)
    hidden = low_back(low(jax.nn.gelu(up_values, approximate=False)))
    return residual + project(hidden, w_down) + down_bias

def reference(tokens, image_ids, ln1_gain, ln1_bias, w_qkv, qv_bias, w_out, out_bias, ln2_gain, ln2_bias, w_up, up_bias, w_down, down_bias, cotangent):
    params = tuple((weight.astype(jnp.float32) for weight in (ln1_gain, ln1_bias, w_qkv, qv_bias, w_out, out_bias, ln2_gain, ln2_bias, w_up, up_bias, w_down, down_bias)))
    inputs = tokens.astype(jnp.float32)

    def forward(param_set, layer_in):
        paired = layer_in.reshape(SEQS // 2, 2, LEN, D)
        paired_ids = image_ids.reshape(SEQS // 2, 2, LEN)
        step_block = jax.checkpoint(block)

        def one_group(operands):
            return step_block(param_set, operands[0], operands[1])
        results = lax.map(one_group, (paired, paired_ids))
        return results.reshape(SEQS, LEN, D)
    output, pullback = jax.vjp(forward, params, inputs)
    grads, input_grad = pullback(cotangent.astype(jnp.float32))
    return (output.astype(jnp.bfloat16), input_grad.astype(jnp.bfloat16), grads[0], grads[1], grads[2], grads[3], grads[4], grads[5], grads[6], grads[7], grads[8], grads[9], grads[10], grads[11])
```

```python
import math

import jax
import jax.numpy as jnp
import numpy as np
from jax import lax
from jax.experimental import pallas as pl
from jax.experimental.pallas import tpu as pltpu
from jax.sharding import Mesh, PartitionSpec as P

D = 768
HEADS = 16
HD = 48
FF = 3072
LEN = 1024
ROWS = 128
BLK = 256
EPS = 1e-05
SCALE = HD ** (-0.5)
BF = jnp.bfloat16
F32 = jnp.float32


def nn(a, b):
    return lax.dot_general(a, b, (((1,), (0,)), ((), ())), preferred_element_type=F32)


def nt(a, b):
    return lax.dot_general(a, b, (((1,), (1,)), ((), ())), preferred_element_type=F32)


def tn(a, b):
    return lax.dot_general(a, b, (((0,), (0,)), ((), ())), preferred_element_type=F32)


def turned(a):
    return a.astype(F32).T.astype(BF)


def attend_fwd_kernel(split_ref, x_ref, w_ref, bias_ref, gain_ref, off_ref, normed_ref, qkv_ref, att_ref, lse_ref):
    for r in range(LEN // BLK):
        rows = slice(r * BLK, (r + 1) * BLK)
        x = x_ref[rows, :].astype(F32)
        center = jnp.mean(x, axis=-1, keepdims=True)
        xc = x - center
        inv = lax.rsqrt(jnp.mean(xc * xc, axis=-1, keepdims=True) + EPS)
        normed = (xc * inv * gain_ref[...] + off_ref[...]).astype(BF)
        normed_ref[rows, :] = normed
        qkv_ref[:, rows] = (nt(w_ref[...], normed) + bias_ref[...]).astype(BF)

    def block(qb, keys):
        cols = slice(qb * BLK, (qb + 1) * BLK)
        kt = qkv_ref[HD : 2 * HD, keys]
        vt = qkv_ref[2 * HD : 3 * HD, keys]
        s = nn(turned(kt), qkv_ref[0:HD, cols]) * SCALE
        peak = jnp.max(s, axis=0, keepdims=True)
        e = jnp.exp(s - peak)
        total = jnp.sum(e, axis=0, keepdims=True)
        probs = (e * (1.0 / total)).astype(BF)
        lse_ref[:, cols] = peak + jnp.log(total)
        out = nn(vt, probs).astype(BF)
        att_ref[2 * qb, :, :] = out[:, :ROWS]
        att_ref[2 * qb + 1, :, :] = out[:, ROWS:]

    whole = split_ref[pl.program_id(0)] == 0

    @pl.when(whole)
    def _():
        for qb in range(LEN // BLK):
            block(qb, slice(0, LEN))

    @pl.when(jnp.logical_not(whole))
    def _():
        for qb in range(LEN // BLK):
            block(qb, slice(qb * BLK, (qb + 1) * BLK))


def attend_fwd(split, x2, w_head, bias, gain, off):
    full = lambda *shape: pl.BlockSpec(shape, lambda i, s: (0,) * len(shape))
    return pl.pallas_call(
        attend_fwd_kernel,
        grid_spec=pltpu.PrefetchScalarGridSpec(
            num_scalar_prefetch=1,
            grid=(2,),
            in_specs=[
                pl.BlockSpec((None, LEN, D), lambda i, s: (i, 0, 0)),
                full(3 * HD, D),
                full(3 * HD, 1),
                full(1, D),
                full(1, D),
            ],
            out_specs=[
                pl.BlockSpec((None, LEN, D), lambda i, s: (i, 0, 0)),
                pl.BlockSpec((None, 3 * HD, LEN), lambda i, s: (i, 0, 0)),
                pl.BlockSpec((8, HD, ROWS), lambda i, s: (0, 0, i)),
                pl.BlockSpec((None, 1, LEN), lambda i, s: (i, 0, 0)),
            ],
        ),
        out_shape=[
            jax.ShapeDtypeStruct((2, LEN, D), BF),
            jax.ShapeDtypeStruct((2, 3 * HD, LEN), BF),
            jax.ShapeDtypeStruct((8, HD, 2 * ROWS), BF),
            jax.ShapeDtypeStruct((2, 1, LEN), F32),
        ],
        compiler_params=pltpu.CompilerParams(vmem_limit_bytes=48 << 20),
        cost_estimate=pl.CostEstimate(flops=2 * 800_000_000, bytes_accessed=8_000_000, transcendentals=2 << 20),
        name="attend_fwd",
    )(split, x2, w_head, bias, gain, off)


def attend_bwd_kernel(split_ref, qkv_ref, lse_ref, datt_ref, normed_ref, w_ref, dnorm_ref, gw_ref, gb_ref, dqkv, acc):
    vt_all = qkv_ref[2 * HD : 3 * HD, :]
    d_out = jnp.concatenate([datt_ref[b] for b in range(8)], axis=1)

    def block(qb, keys, first):
        cols = slice(qb * BLK, (qb + 1) * BLK)
        qt = qkv_ref[0:HD, cols]
        kt = qkv_ref[HD : 2 * HD, keys]
        vt = qkv_ref[2 * HD : 3 * HD, keys]
        dt = d_out[:, cols]
        s = nn(turned(kt), qt) * SCALE
        probs = jnp.exp(s - lse_ref[:, cols])
        dp = nn(turned(vt), dt)
        delta = jnp.sum(probs * dp, axis=0, keepdims=True)
        ds = (probs * (dp - delta)).astype(BF)
        dqkv[0:HD, cols] = nn(kt, ds) * SCALE
        dk = nt(qt, ds) * SCALE
        dv = nt(dt, probs.astype(BF))
        if first:
            dqkv[HD : 2 * HD, keys] = dk
            dqkv[2 * HD : 3 * HD, keys] = dv
        else:
            dqkv[HD : 2 * HD, keys] += dk
            dqkv[2 * HD : 3 * HD, keys] += dv

    whole = split_ref[pl.program_id(0)] == 0

    @pl.when(whole)
    def _():
        for qb in range(LEN // BLK):
            block(qb, slice(0, LEN), qb == 0)

    @pl.when(jnp.logical_not(whole))
    def _():
        for qb in range(LEN // BLK):
            block(qb, slice(qb * BLK, (qb + 1) * BLK), True)

    d_b = dqkv[...].astype(BF)
    gw = nn(d_b, normed_ref[...])
    gb = jnp.sum(d_b.astype(F32), axis=1, keepdims=True)
    first_seq = pl.program_id(0) == 0

    @pl.when(first_seq)
    def _():
        acc[...] = gw
        gb_ref[...] = gb

    @pl.when(jnp.logical_not(first_seq))
    def _():
        gw_ref[...] = (acc[...] + gw).astype(BF)
        gb_ref[...] += gb

    dnorm_ref[...] = nn(turned(dqkv[...]), w_ref[...]).astype(BF)


def attend_bwd(split, qkv, lse, datt, normed, w_head):
    full = lambda *shape: pl.BlockSpec(shape, lambda i, s: (0,) * len(shape))
    return pl.pallas_call(
        attend_bwd_kernel,
        grid_spec=pltpu.PrefetchScalarGridSpec(
            num_scalar_prefetch=1,
            grid=(2,),
            in_specs=[
                pl.BlockSpec((None, 3 * HD, LEN), lambda i, s: (i, 0, 0)),
                pl.BlockSpec((None, 1, LEN), lambda i, s: (i, 0, 0)),
                pl.BlockSpec((8, HD, ROWS), lambda i, s: (0, 0, i)),
                pl.BlockSpec((None, LEN, D), lambda i, s: (i, 0, 0)),
                full(3 * HD, D),
            ],
            out_specs=[
                pl.BlockSpec((None, LEN, D), lambda i, s: (i, 0, 0)),
                full(3 * HD, D),
                full(3 * HD, 1),
            ],
            scratch_shapes=[pltpu.VMEM((3 * HD, LEN), F32), pltpu.VMEM((3 * HD, D), F32)],
        ),
        out_shape=[
            jax.ShapeDtypeStruct((2, LEN, D), BF),
            jax.ShapeDtypeStruct((3 * HD, D), BF),
            jax.ShapeDtypeStruct((3 * HD, 1), F32),
        ],
        compiler_params=pltpu.CompilerParams(vmem_limit_bytes=48 << 20),
        cost_estimate=pl.CostEstimate(flops=2 * 1_600_000_000, bytes_accessed=9_000_000, transcendentals=2 << 20),
        name="attend_bwd",
    )(split, qkv, lse, datt, normed, w_head)


TILE = 256


def mlp_kernel(n2_ref, cot_ref, wu_ref, wd_ref, ub_ref, out_ref, dn_ref, gu_ref, gd_ref, gb_ref):
    j = pl.program_id(0)
    up = nn(n2_ref[...], wu_ref[...]) + ub_ref[...]
    cdf = 0.5 * (1.0 + lax.erf(up * 2.0 ** (-0.5)))
    hidden = (up * cdf).astype(BF)
    dh = nt(cot_ref[...], wd_ref[...]).astype(BF).astype(F32)
    slope = cdf + up * jnp.exp(-0.5 * up * up) * (2.0 * math.pi) ** (-0.5)
    d_up = (dh * slope).astype(BF)
    gb_ref[...] = jnp.sum(d_up.astype(F32), axis=0, keepdims=True)
    gd_ref[...] = tn(hidden, cot_ref[...]).astype(BF)
    gu_ref[...] = tn(n2_ref[...], d_up).astype(BF)
    out = nn(hidden, wd_ref[...])
    dn = nt(d_up, wu_ref[...])

    @pl.when(j == 0)
    def _():
        out_ref[...] = out
        dn_ref[...] = dn

    @pl.when(j > 0)
    def _():
        out_ref[...] += out
        dn_ref[...] += dn


def mlp(n2, cot, wu, wd, ub):
    rows, half = n2.shape[0], wu.shape[1]
    full = lambda *shape: pl.BlockSpec(shape, lambda j: (0,) * len(shape))
    return pl.pallas_call(
        mlp_kernel,
        grid=(half // TILE,),
        in_specs=[
            full(rows, D),
            full(rows, D),
            pl.BlockSpec((D, TILE), lambda j: (0, j)),
            pl.BlockSpec((TILE, D), lambda j: (j, 0)),
            pl.BlockSpec((1, TILE), lambda j: (0, j)),
        ],
        out_specs=[
            full(rows, D),
            full(rows, D),
            pl.BlockSpec((D, TILE), lambda j: (0, j)),
            pl.BlockSpec((TILE, D), lambda j: (j, 0)),
            pl.BlockSpec((1, TILE), lambda j: (0, j)),
        ],
        out_shape=[
            jax.ShapeDtypeStruct((rows, D), F32),
            jax.ShapeDtypeStruct((rows, D), F32),
            jax.ShapeDtypeStruct((D, half), BF),
            jax.ShapeDtypeStruct((half, D), BF),
            jax.ShapeDtypeStruct((1, half), F32),
        ],
        compiler_params=pltpu.CompilerParams(vmem_limit_bytes=48 << 20),
        cost_estimate=pl.CostEstimate(flops=12 * rows * D * half, bytes_accessed=12_000_000, transcendentals=2 * rows * half),
        name="mlp",
    )(n2, cot, wu, wd, ub)


AXES = ("yl", "z", "c", "x", "yh")
SEQ = ("yl", "z", "c")
BAND = ("x", "yh")
LINE = ("yl", "z")


def swap_core(v):
    return lax.ppermute(v, "c", [(0, 1), (1, 0)])


def swap_yl(v):
    return lax.ppermute(v, "yl", [(0, 1), (1, 0)])


def swap_both(v):
    return lax.ppermute(v, ("yl", "c"), [(0, 3), (1, 2), (2, 1), (3, 0)])


def exchange(v, axes):
    return lax.all_to_all(v, axes, 0, 0, tiled=True)


def by_core(c, own, other):
    return jnp.stack([jnp.where(c == 0, own, other), jnp.where(c == 0, other, own)])


def halves(c, whole, axis):
    first, second = jnp.split(whole, 2, axis=axis)
    return jnp.where(c == 0, first, second), jnp.where(c == 0, second, first)


def joined(c, own, other, axis):
    return jnp.concatenate([jnp.where(c == 0, own, other), jnp.where(c == 0, other, own)], axis=axis)


def norm_parts(values):
    center = jnp.mean(values, axis=-1, keepdims=True)
    centered = values - center
    inverse = lax.rsqrt(jnp.mean(centered * centered, axis=-1, keepdims=True) + EPS)
    return centered * inverse, inverse


def norm_back(d, unit, inverse, gain):
    dg = d * gain
    return inverse * (dg - jnp.mean(dg, axis=-1, keepdims=True) - unit * jnp.mean(dg * unit, axis=-1, keepdims=True))


def per_device(
    tokens, image_ids, ln1_gain, ln1_bias, w_qkv, qv_bias, w_out, out_bias,
    ln2_gain, ln2_bias, w_up, up_bias, w_down, down_bias, cotangent,
):
    c = lax.axis_index("c")
    yl = lax.axis_index("yl")
    z = lax.axis_index("z")
    band = lax.axis_index(BAND)
    aligned = c == yl
    x = tokens[0]
    cot = cotangent[0]

    qkv_heads = w_qkv.reshape(3, 3, HEADS, HD).transpose(0, 2, 1, 3).reshape(3, HEADS * 3 * HD)
    qkv_own, qkv_other = halves(c, qkv_heads, 1)
    up_own, up_other = halves(c, w_up, 1)
    ids_mark = jnp.broadcast_to(jnp.max(image_ids).astype(BF), (3, 1))
    small = jnp.concatenate(
        [v[:, None] for v in (ln1_gain, ln1_bias, out_bias, ln2_gain, ln2_bias, down_bias)]
        + [qv_bias.reshape(3, 2), up_bias.reshape(3, 4), ids_mark, jnp.zeros((3, 3), BF)],
        axis=1,
    )
    rows = jnp.concatenate([w_out, w_down], axis=0)
    cols_other = jnp.concatenate([qkv_other, up_other, small], axis=1)
    cols_got = swap_core(cols_other)
    rows_core, rows_yl, rows_both = swap_core(rows), swap_yl(rows), swap_both(rows)
    rows_same = jnp.where(aligned, rows, rows_yl)
    rows_cross = jnp.where(aligned, rows_core, rows_both)
    rows2 = by_core(c, rows_same, rows_cross)
    nq, nu = qkv_own.shape[1], up_own.shape[1]
    qkv2 = by_core(c, qkv_own, cols_got[:, :nq])
    up2 = by_core(c, up_own, cols_got[:, nq : nq + nu])
    small2 = by_core(c, small, cols_got[:, nq + nu :])

    head_cols = qkv2.reshape(6, 8, 3 * HD).transpose(1, 0, 2).reshape(8, 6 * 3 * HD)
    one = jnp.concatenate([x.reshape(-1), rows2.reshape(-1), small2.reshape(-1)])
    n_one = one.shape[0]
    width = -(-(n_one + head_cols.shape[1]) // 1024) * 1024
    sent = jnp.concatenate(
        [
            jnp.broadcast_to(one[None], (8, n_one)),
            head_cols,
            jnp.zeros((8, width - n_one - head_cols.shape[1]), BF),
        ],
        axis=1,
    ).reshape(8, width // 128, 128)
    got = exchange(sent, BAND).reshape(8, width)
    at = ROWS * D
    tokens_all = got[:, :at].reshape(LEN, D)
    rows_all = got[:, at : at + 30 * D].reshape(8, 2, 15, D)
    at += 30 * D
    small_all = got[:, at : at + 96].reshape(8, 2, 3, 16)
    at += 96
    head_all = got[:, at : at + 6 * 3 * HD].reshape(8, 2, 3, 3 * HD)

    rows_block = jnp.concatenate(
        [
            rows_all[:, :, :3].transpose(1, 0, 2, 3).reshape(48, D),
            rows_all[:, :, 3:].transpose(1, 0, 2, 3).reshape(192, D),
        ],
        axis=0,
    )
    rows_full = lax.all_gather(rows_block, "z", axis=0)
    w_out_c = rows_full[:, :48].reshape(8 * 48, D)
    w_down_c = rows_full[:, 48:].reshape(8 * 192, D)

    head_block = head_all.transpose(1, 0, 2, 3).reshape(48 * 3 * HD)
    small_block = small_all.transpose(1, 0, 2, 3).reshape(48 * 16)
    line = jnp.concatenate([head_block, small_block, up2.reshape(-1)])
    line_width = -(-line.shape[0] // 1024) * 1024
    line = jnp.pad(line, (0, line_width - line.shape[0])).reshape(1, line_width // 128, 128)
    line_got = exchange(jnp.broadcast_to(line, (16,) + line.shape[1:]), LINE).reshape(16, line_width)
    at = 48 * 3 * HD
    w_head = line_got[:, :at].reshape(D, 3 * HD)
    small_full = line_got[:, at : at + 768].reshape(D, 16)
    at += 768
    up_block = line_got[:, at : at + 6 * nu].reshape(96, nu)
    w_head_t = w_head.T

    vectors = small_full.astype(F32).T
    g1, b1, out_b, g2, b2, down_b = (vectors[i][None] for i in range(6))
    qv_full = small_full[:, 6:8].reshape(2 * D).astype(F32)
    up_b = lax.dynamic_slice(small_full[:, 8:12].reshape(FF), (c * nu,), (nu,)).astype(F32)[None]
    head_at = (c * 8 + band) * HD
    head_bias = jnp.concatenate(
        [
            lax.dynamic_slice(qv_full, (head_at,), (HD,)),
            jnp.zeros((HD,), F32),
            lax.dynamic_slice(qv_full, (D + head_at,), (HD,)),
        ]
    )[:, None]
    marks = vectors[12].reshape(2, 8, 2, 8, 3).max(axis=(3, 4))
    pair_marks = lax.dynamic_slice(marks, (yl, z, 0), (1, 1, 2)).reshape(2)
    split = jnp.where(c == 0, pair_marks, pair_marks[::-1])
    split = (split > 0.5).astype(jnp.int32)

    w_up_c = exchange(jnp.broadcast_to(up_block[None], (8,) + up_block.shape), BAND).reshape(D, nu)
    place = np.arange(D)
    natural = place.reshape(2, 8, 2, 8, 3).transpose(3, 0, 1, 2, 4).reshape(-1)
    shuffle_np = np.zeros((D, D), np.float32)
    shuffle_np[natural, place] = 1.0
    shuffle = jnp.asarray(shuffle_np, BF)

    x2 = jnp.stack([tokens_all, swap_core(tokens_all)])
    normed2seq, qkv, att, lse = attend_fwd(split, x2, w_head_t, head_bias, g1, b1)
    att_c = exchange(att, BAND).reshape(8 * HD, 2 * ROWS)
    branch = tn(att_c, w_out_c)
    inputs = x.astype(F32)
    residual = inputs + branch[:ROWS] + swap_core(branch[ROWS:]) + out_b

    unit2, inv2 = norm_parts(residual)
    n2 = (unit2 * g2 + b2).astype(BF)
    n2p = jnp.dot(n2, shuffle, preferred_element_type=F32).astype(BF)
    n2p_pair = jnp.concatenate([n2p, swap_core(n2p)], axis=0)
    cot_pair = jnp.concatenate([cot, swap_core(cot)], axis=0)
    part_out, part_dn, grad_up, grad_down, grad_up_b = mlp(n2p_pair, cot_pair, w_up_c, w_down_c, up_b)
    got_pair = swap_core(jnp.concatenate([part_out[ROWS:], part_dn[ROWS:]], axis=0))
    output = residual + part_out[:ROWS] + got_pair[:ROWS] + down_b
    dn2p = part_dn[:ROWS] + got_pair[ROWS:]
    dn2 = lax.dot_general(dn2p, shuffle.astype(F32), (((1,), (1,)), ((), ())), precision=lax.Precision.HIGHEST)
    d_out = cot.astype(F32)
    d_res = d_out + norm_back(dn2, unit2, inv2, g2)
    d_branch = d_res.astype(BF)
    d_pair = jnp.concatenate([d_branch, swap_core(d_branch)], axis=0)
    d_att = nt(w_out_c, d_pair).astype(BF).reshape(8, HD, 2 * ROWS)
    d_att_all = exchange(d_att, BAND)
    grad_out = nn(att_c, d_pair).astype(BF)

    rows_grad = jnp.concatenate([grad_out.reshape(8, 48, D), grad_down.reshape(8, 192, D)], axis=1)
    rows_sum = lax.psum_scatter(rows_grad, "z", scatter_dimension=0, tiled=True).reshape(240, D)
    rows_send = jnp.concatenate(
        [rows_sum[:48].reshape(2, 8, 3, D), rows_sum[48:].reshape(2, 8, 12, D)], axis=2
    ).transpose(1, 0, 2, 3)
    up_parts = exchange(grad_up.reshape(8, 96, nu), BAND)
    up_line = jnp.sum(up_parts.astype(F32), axis=0).astype(BF)

    d_norm, grad_head_t, grad_head_b = attend_bwd(split, qkv, lse, d_att_all, normed2seq, w_head_t)
    d_norm_sum = (d_norm[0].astype(F32) + swap_core(d_norm[1]).astype(F32)).astype(BF)

    grad_head = grad_head_t.T.reshape(16, 48 * 3 * HD)

    d_normed = jnp.sum(exchange(d_norm_sum.reshape(8, ROWS, D), BAND).astype(F32), axis=0)
    unit1, inv1 = norm_parts(inputs)
    d_tokens = (d_res + norm_back(d_normed, unit1, inv1, g1)).astype(BF)

    def total(v):
        return jnp.sum(v, axis=0)

    qv_grad = jnp.zeros((2 * D,), F32)
    qv_grad = lax.dynamic_update_slice(qv_grad, grad_head_b[:HD, 0], (head_at,))
    qv_grad = lax.dynamic_update_slice(qv_grad, grad_head_b[2 * HD :, 0], (D + head_at,))
    up_grad_b = lax.dynamic_update_slice(jnp.zeros((FF,), F32), grad_up_b[0], (c * nu,))
    small_grad = jnp.concatenate(
        [
            jnp.stack(
                [
                    total(d_normed * unit1),
                    total(d_normed),
                    total(d_branch.astype(F32)),
                    total(dn2 * unit2),
                    total(dn2),
                    total(d_out),
                ]
            ).T,
            qv_grad.reshape(D, 2),
            up_grad_b.reshape(D, 4),
            jnp.zeros((D, 4), F32),
        ],
        axis=1,
    ).astype(BF)
    line_grad = jnp.concatenate(
        [grad_head, small_grad.reshape(16, 768), up_line.reshape(16, 6 * nu)], axis=1
    )
    line_grad = jnp.pad(line_grad, ((0, 0), (0, line_width - line_grad.shape[1])))
    line_parts = exchange(line_grad.reshape(16, line_width // 128, 128), LINE)
    line_sum = jnp.sum(line_parts.astype(F32), axis=0).reshape(line_width)
    at = 48 * 3 * HD
    head_sum = line_sum[:at].astype(BF).reshape(2, 8, 3, 3 * HD).transpose(1, 0, 2, 3).reshape(8, 18 * HD)
    small_sum = line_sum[at : at + 768].astype(BF).reshape(2, 8, 3, 16).transpose(1, 0, 2, 3).reshape(8, 96)
    at += 768
    up_sum = line_sum[at : at + 6 * nu].reshape(2, 3, nu)

    last = jnp.concatenate([rows_send.reshape(8, 30 * D), small_sum, head_sum], axis=1)
    last_width = -(-last.shape[1] // 1024) * 1024
    last = jnp.pad(last, ((0, 0), (0, last_width - last.shape[1]))).reshape(8, last_width // 128, 128)
    last_got = exchange(last, BAND).reshape(8, last_width)
    rows_sums = jnp.sum(last_got[:, : 30 * D].astype(F32), axis=0).reshape(2, 15, D)
    at = 30 * D
    small_sums = jnp.sum(last_got[:, at : at + 96].astype(F32), axis=0).reshape(2, 3, 16)
    at += 96
    head_sums = last_got[:, at : at + 18 * HD].reshape(8, 2, 3, 3 * HD).transpose(1, 2, 0, 3).reshape(2, 3, nq)

    def mine(v):
        return jnp.where(c == 0, v[0], v[1])

    def theirs(v):
        return jnp.where(c == 0, v[1], v[0])

    rows_mine, rows_theirs = mine(rows_sums).astype(BF), theirs(rows_sums).astype(BF)
    from_core, from_yl, from_both = swap_core(rows_theirs), swap_yl(rows_mine), swap_both(rows_theirs)
    rows_done = jnp.where(
        aligned, mine(rows_sums) + from_yl.astype(F32), from_core.astype(F32) + from_both.astype(F32)
    )
    cols_got2 = swap_core(
        jnp.concatenate([theirs(head_sums), theirs(up_sum).astype(BF), theirs(small_sums).astype(BF)], axis=1)
    ).astype(F32)
    qkv_done = joined(c, mine(head_sums).astype(F32), cols_got2[:, :nq], 1)
    qkv_done = qkv_done.reshape(3, HEADS, 3, HD).transpose(0, 2, 1, 3).reshape(3, 3 * D)
    up_done = joined(c, mine(up_sum), cols_got2[:, nq : nq + nu], 1)
    small_done = mine(small_sums) + cols_got2[:, nq + nu :]

    return (
        output.astype(BF)[None],
        d_tokens[None],
        small_done[:, 0],
        small_done[:, 1],
        qkv_done,
        small_done[:, 6:8].reshape(6),
        rows_done[:3],
        small_done[:, 2],
        small_done[:, 3],
        small_done[:, 4],
        up_done,
        small_done[:, 8:12].reshape(12),
        rows_done[3:],
        small_done[:, 5],
    )


def solution(mesh):
    fine = Mesh(mesh.devices.reshape(2, 8, 2, 4, 2), AXES)
    seq_band = P(SEQ, BAND, None)
    flat, flat2 = P(AXES), P(AXES, None)
    in_specs = (
        seq_band, P(SEQ, BAND), flat, flat, flat2, flat, flat2, flat,
        flat, flat, flat2, flat, flat2, flat, seq_band,
    )
    out_specs = (
        seq_band, seq_band, flat, flat, flat2, flat, flat2, flat,
        flat, flat, flat2, flat, flat2, flat,
    )
    return jax.shard_map(per_device, mesh=fine, in_specs=in_specs, out_specs=out_specs, check_vma=False)
```

```python
import math

import jax
import jax.numpy as jnp
import numpy as np
from jax import lax
from jax.experimental import pallas as pl
from jax.experimental.pallas import tpu as pltpu
from jax.sharding import Mesh, PartitionSpec as P

D = 768
HEADS = 16
HD = 48
FF = 3072
LEN = 1024
ROWS = 128
BLK = 256
HALF = FF // 2
EPS = 1e-05
SCALE = HD ** (-0.5)
BF = jnp.bfloat16
F32 = jnp.float32
HBM = pl.BlockSpec(memory_space=pltpu.HBM)


def nn(a, b):
    return lax.dot_general(a, b, (((1,), (0,)), ((), ())), preferred_element_type=F32)


def nt(a, b):
    return lax.dot_general(a, b, (((1,), (1,)), ((), ())), preferred_element_type=F32)


def tn(a, b):
    return lax.dot_general(a, b, (((0,), (0,)), ((), ())), preferred_element_type=F32)


def turned(a):
    return a.astype(F32).T.astype(BF)


def params(mebi):
    return pltpu.CompilerParams(vmem_limit_bytes=mebi << 20)


def cost(micros, size):
    return pl.CostEstimate(flops=int(micros * 1.1e9), bytes_accessed=size, transcendentals=0)


def grid_call(kernel, steps, ins, outs, out_shape, scratch, name, micros, size, mebi=8):
    return pl.pallas_call(
        kernel,
        grid=(steps,),
        in_specs=ins,
        out_specs=outs,
        out_shape=out_shape,
        scratch_shapes=scratch,
        compiler_params=params(mebi),
        cost_estimate=cost(micros, size),
        name=name,
    )


def pinned(*values):
    return tuple(pltpu.with_memory_space_constraint(v, pltpu.HBM) for v in values)


def in_hbm(*shape, dtype=BF):
    return pltpu.HBM(shape, dtype)


def full(*shape):
    return pl.BlockSpec(shape, lambda i: (0,) * len(shape))


def step_block(*shape):
    return pl.BlockSpec((None,) + shape, lambda i: (i,) + (0,) * len(shape))


def iota(shape, axis):
    return lax.broadcasted_iota(jnp.int32, shape, axis)


def like(*shape, dtype=BF):
    return jax.ShapeDtypeStruct(shape, dtype)


WIN = 192
SMALL = 3 * HD
PACK = 32


def unit_order():
    source = np.arange(D)
    target = source % 24 // 12 * (D // 2) + source // 96 * 48 + source % 96 // 24 * 12 + source % 12
    return jnp.asarray(target[:, None] == np.arange(D)[None, :], BF)


def prep_kernel(*refs):
    sources, (own_ref, other_ref), held, (buf, cbuf, sems) = refs[:14], refs[14:16], refs[16:30], refs[30:]
    copies = [pltpu.make_async_copy(a, b, sems.at[i]) for i, (a, b) in enumerate(zip(sources, held))]
    for copy in copies:
        copy.start()
    buf[...] = jnp.zeros(buf.shape, F32)
    cbuf[...] = jnp.zeros(cbuf.shape, F32)
    for copy in copies:
        copy.wait()
    wq_ref, wu_ref, wo_ref, wd_ref = held[:4]
    vectors, ids_ref, order_ref = held[4:12], held[12], held[13]

    def column(ref, stride, k):
        row = ref[...].astype(F32).reshape(1, ref.shape[0])
        shape = (3, ref.shape[0])
        keep = iota(shape, 1) == iota(shape, 0) * stride + k
        return jnp.sum(jnp.where(keep, jnp.broadcast_to(row, shape), 0.0), axis=1, keepdims=True)

    columns = [column(ref, 1, 0) for ref in vectors[:6]]
    columns += [column(vectors[6], 2, k) for k in range(2)]
    columns += [column(vectors[7], 4, k) for k in range(4)]
    mark = jnp.max(ids_ref[...].astype(F32), axis=1, keepdims=True)
    columns.append(jnp.broadcast_to(mark, (3, 1)))
    lanes = iota((3, 128), 1)
    small = jnp.zeros((3, 128), F32)
    for j, col in enumerate(columns):
        small = jnp.where(lanes == j, jnp.broadcast_to(col, (3, 128)), small)
    wq = wq_ref[...].astype(F32)
    for i in range(4):
        cbuf[8 * i : 8 * i + 3] = wu_ref[:, i * D : (i + 1) * D].astype(F32)
    chosen = nn(cbuf[...].astype(BF), order_ref[...])
    for k in range(2):
        buf[k, 0:3] = wo_ref[...].astype(F32)
        buf[k, 3:15] = wd_ref[...].astype(F32)
        for q in range(2):
            at = 8 * (2 * k + q)
            for y in range(2):
                to = slice(q * (D // 2), (q + 1) * (D // 2))
                buf[k, 15 + 3 * y : 18 + 3 * y, to] = chosen[at : at + 3, y * (D // 2) : (y + 1) * (D // 2)]
        for b in range(8):
            row, lane, at = 21 + 3 * (b // 4), (b % 4) * WIN, (k * 8 + b) * HD
            for p in range(3):
                buf[k, row : row + 3, lane + p * HD : lane + (p + 1) * HD] = wq[:, p * D + at : p * D + at + HD]
            buf[k, row : row + 3, lane + SMALL : lane + SMALL + 16] = small[:, :16]
    core0 = lax.axis_index("c") == 0
    own_ref[...] = jnp.where(core0, buf[0], buf[1]).astype(BF)
    other_ref[...] = jnp.where(core0, buf[1], buf[0]).astype(BF)


def prep(w_qkv, w_up, w_out, w_down, vectors, ids, order):
    args = (w_qkv, w_up, w_out, w_down) + vectors + (ids, order)
    return grid_call(
        prep_kernel, 1, [HBM] * len(args), [full(PACK, D)] * 2, [like(PACK, D)] * 2,
        [pltpu.VMEM(a.shape, a.dtype) for a in args]
        + [pltpu.VMEM((2, PACK, D), F32), pltpu.VMEM((32, D), F32), pltpu.SemaphoreType.DMA((len(args),))],
        "prep", 2, 100_000,
    )(*pinned(*args))


def groups_of(own, core, line, both, core0, yl0):
    def pick(a, b, c, d):
        return jnp.where(yl0, jnp.where(core0, a, b), jnp.where(core0, c, d))

    return (
        pick(own, core, line, both),
        pick(core, own, both, line),
        pick(line, both, own, core),
        pick(both, line, core, own),
    )


SENT = 48


def spread_kernel(own_ref, core_ref, line_ref, both_ref, out_ref, buf):
    core0, yl0 = lax.axis_index("c") == 0, lax.axis_index("yl") == 0
    aligned = lax.axis_index("c") == lax.axis_index("yl")
    own, core, line, both = (r[...].astype(F32) for r in (own_ref, core_ref, line_ref, both_ref))
    same, cross = jnp.where(aligned, own, line), jnp.where(aligned, core, both)
    buf[...] = jnp.zeros(buf.shape, F32)
    buf[0:15] = jnp.where(core0, same, cross)[0:15]
    buf[15:30] = jnp.where(core0, cross, same)[0:15]
    groups = groups_of(own, core, line, both, core0, yl0)
    for b in range(8):
        y, row, lane = b % 2, 21 + 3 * (b // 4), (b % 4) * WIN
        for g in range(4):
            buf[30 + 3 * g : 33 + 3 * g] = groups[g][15 + 3 * y : 18 + 3 * y]
            buf[42:45, g * WIN : (g + 1) * WIN] = groups[g][row : row + 3, lane : lane + WIN]
        out_ref[b] = buf[...].astype(BF)


def spread(packs):
    return grid_call(
        spread_kernel, 1, [full(PACK, D)] * 4, full(8, SENT, D), like(8, SENT, D),
        [pltpu.VMEM((SENT, D), F32)], "spread", 1, 1_000_000,
    )(*packs)


BLOCK = 240
LINE = 24


def collect_kernel(got_ref, blk_ref, line_ref, buf, lbuf):
    yh = lax.axis_index("yh")
    for b in range(8):
        got = got_ref[b].astype(F32)
        for c in range(2):
            k = c * 8 + b
            buf[3 * k : 3 * k + 3] = got[c * 15 : c * 15 + 3]
            for y in range(2):
                at, row = 144 + y * 48 + 3 * k, 30 + (y * 2 + c) * 3
                buf[at : at + 3] = got[row : row + 3]
        lbuf[3 * b : 3 * b + 3] = got[42:45]
    for x in range(4):
        got = got_ref[2 * x + yh].astype(F32)
        for c in range(2):
            at = 48 + (c * 4 + x) * 12
            buf[at : at + 12] = got[c * 15 + 3 : c * 15 + 15]
    line = lbuf[...].astype(BF)
    for z in range(8):
        line_ref[z] = line
    blk_ref[...] = buf[...].astype(BF)


def collect(got):
    return grid_call(
        collect_kernel, 1, [full(8, SENT, D)], [full(BLOCK, D), full(8, LINE, D)], [in_hbm(BLOCK, D), like(8, LINE, D)],
        [pltpu.VMEM((BLOCK, D), F32), pltpu.VMEM((LINE, D), F32)], "collect", 2, 2_000_000,
    )(got)


def place_of(step):
    return lax.rem(lax.axis_index("x") + step, 4)


RING = (0, 3, 1, 2)


def head_index():
    return lax.axis_index("c") * 8 + lax.axis_index("x") * 2 + lax.axis_index("yh")


def group_rows(group):
    return pl.ds(pl.multiple_of(group * 24, 8), 24)


def pair_groups():
    at = (lax.axis_index("yl") * 8 + lax.axis_index("z")) * 2
    c = lax.axis_index("c")
    return at + c, at + 1 - c


def several_images(small_ref, seq):
    own, other = pair_groups()
    block = small_ref[group_rows(jnp.where(seq == 0, own, other)), :]
    marks = jnp.where(iota(block.shape, 1) == 12, block, 0.0)
    return jnp.max(marks) > 0.5


def attend_fwd_kernel(*refs):
    pieces = refs[:10]
    (line_ref, normed_ref, unit_ref, qkv_ref, att_ref, wide_ref, lse_ref, wt_ref, vec_ref, small_ref,
     xbuf, keys_buf, wbuf, bias, sems) = refs[10:]
    seq = pl.program_id(0)

    def copies(s):
        pair, left, right, far0, far1 = pieces[5 * s : 5 * s + 5]
        targets = (
            (pair, xbuf.at[s, pl.ds(0, BLK)]),
            (left, xbuf.at[s, pl.ds(BLK, BLK)]),
            (right, xbuf.at[s, pl.ds(2 * BLK, BLK)]),
            (far0, xbuf.at[s, pl.ds(3 * BLK, ROWS)]),
            (far1, xbuf.at[s, pl.ds(3 * BLK + ROWS, ROWS)]),
        )
        return [pltpu.make_async_copy(a, b, sems.at[5 * s + i]) for i, (a, b) in enumerate(targets)]

    @pl.when(seq == 0)
    def _():
        for s in range(2):
            for copy in copies(s):
                copy.start()
        wbuf[...] = jnp.zeros(wbuf.shape, F32)
        for z in range(8):
            line = line_ref[z].astype(F32)
            for g in range(4):
                y, c = g // 2, g % 2
                at = (y * 8 + z) * 48 + c * 24
                wbuf[at : at + 24, 0:WIN] = line[:, g * WIN : (g + 1) * WIN]
        turned_w = wbuf[...].T
        wt_ref[...] = turned_w[:SMALL].astype(BF)
        vec_ref[...] = turned_w[SMALL : SMALL + 16]
        small_ref[...] = wbuf[:, SMALL : SMALL + 16]
        head = head_index()
        expand = (iota((HD, 24), 0) // 2 == iota((HD, 24), 1)).astype(F32)
        lane = iota((HD, 16), 1) == 6 + iota((HD, 16), 0) % 2
        for part, group in ((0, head), (2, 16 + head)):
            spreads = nn(expand, small_ref[group_rows(group), :])
            col = jnp.sum(jnp.where(lane, spreads, 0.0), axis=1, keepdims=True)
            bias[part * HD : (part + 1) * HD] = col
        bias[HD : 2 * HD] = jnp.zeros((HD, 1), F32)
        for copy in copies(0):
            copy.wait()

    @pl.when(seq == 1)
    def _():
        for copy in copies(1):
            copy.wait()

    gain, off = vec_ref[0:1], vec_ref[1:2]

    for k in range(4):
        rows = pl.ds(pl.multiple_of(place_of(RING[k]) * BLK, BLK), BLK)
        x = xbuf[seq, k * BLK : (k + 1) * BLK].astype(F32)
        center = jnp.mean(x, axis=-1, keepdims=True)
        xc = x - center
        unit = xc * lax.rsqrt(jnp.mean(xc * xc, axis=-1, keepdims=True) + EPS)
        normed = (unit * gain + off).astype(BF)
        unit_ref[rows, :] = unit.astype(BF)
        normed_ref[rows, :] = normed
        qkv_ref[:, rows] = (nt(wt_ref[...], normed) + bias[...]).astype(BF)

    keys_buf[...] = turned(qkv_ref[HD : 2 * HD, :])

    def block(qb, keys):
        cols = slice(qb * BLK, (qb + 1) * BLK)
        vt = qkv_ref[2 * HD : 3 * HD, keys]
        s = nn(keys_buf[keys, :], qkv_ref[0:HD, cols]) * SCALE
        peak = jnp.max(s, axis=0, keepdims=True)
        e = jnp.exp(s - peak)
        total = jnp.sum(e, axis=0, keepdims=True)
        lse_ref[:, cols] = peak + jnp.log(total)
        out = nn(vt, e.astype(BF)) * (1.0 / total)
        wide_ref[:, cols] = out
        out = out.astype(BF)
        att_ref[2 * qb, :, :] = out[:, :ROWS]
        att_ref[2 * qb + 1, :, :] = out[:, ROWS:]

    several = several_images(small_ref, seq)

    @pl.when(jnp.logical_not(several))
    def _():
        for qb in range(LEN // BLK):
            block(qb, slice(0, LEN))

    @pl.when(several)
    def _():
        for qb in range(LEN // BLK):
            block(qb, slice(qb * BLK, (qb + 1) * BLK))


def attend_fwd(pieces, line):
    return grid_call(
        attend_fwd_kernel,
        2,
        [HBM] * 10 + [full(8, LINE, D)],
        [
            step_block(LEN, D),
            step_block(LEN, D),
            step_block(SMALL, LEN),
            pl.BlockSpec((8, HD, ROWS), lambda i: (0, 0, i)),
            step_block(HD, LEN),
            step_block(1, LEN),
            full(SMALL, D),
            full(16, D),
            full(D, 16),
        ],
        [
            in_hbm(2, LEN, D),
            in_hbm(2, LEN, D),
            in_hbm(2, SMALL, LEN),
            like(8, HD, 2 * ROWS),
            in_hbm(2, HD, LEN, dtype=F32),
            in_hbm(2, 1, LEN, dtype=F32),
            in_hbm(SMALL, D),
            like(16, D, dtype=F32),
            like(D, 16, dtype=F32),
        ],
        [
            pltpu.VMEM((2, LEN, D), BF),
            pltpu.VMEM((LEN, HD), BF),
            pltpu.VMEM((D, 256), F32),
            pltpu.VMEM((SMALL, 1), F32),
            pltpu.SemaphoreType.DMA((10,)),
        ],
        "attend_fwd",
        11,
        10_000_000,
        32,
    )(*pinned(*pieces), line)


def attend_bwd_kernel(
    qkv_ref, lse_ref, wide_ref, datt_ref, normed_ref, unit_ref, w_ref, small_ref, vgrad_ref, ugrad_ref,
    down_ref, dother_ref, out_ref, keys_buf, values_buf, dqkv, acc, acc_unit, acc_bias, gbuf,
):
    seq = pl.program_id(0)
    keys_buf[...] = turned(qkv_ref[HD : 2 * HD, :])
    values_buf[...] = turned(qkv_ref[2 * HD : 3 * HD, :])

    def tile(qb, kb):
        cols = slice(qb * BLK, (qb + 1) * BLK)
        keys = slice(kb * BLK, (kb + 1) * BLK)
        qt = qkv_ref[0:HD, cols]
        dt = jnp.concatenate([datt_ref[2 * qb], datt_ref[2 * qb + 1]], axis=1)
        delta = jnp.sum(dt.astype(F32) * wide_ref[:, cols], axis=0, keepdims=True)
        probs = jnp.exp(nn(keys_buf[keys, :], qt) * SCALE - lse_ref[:, cols])
        ds = (probs * (nn(values_buf[keys, :], dt) - delta)).astype(BF)
        dq = nn(qkv_ref[HD : 2 * HD, keys], ds)
        dk = nt(qt, ds)
        dv = nt(dt, probs.astype(BF))
        if qb == kb:
            dqkv[0:HD, cols] = dq
            dqkv[HD : 2 * HD, keys] = dk
            dqkv[2 * HD : 3 * HD, keys] = dv
        else:
            dqkv[0:HD, cols] += dq
            dqkv[HD : 2 * HD, keys] += dk
            dqkv[2 * HD : 3 * HD, keys] += dv

    for qb in range(LEN // BLK):
        tile(qb, qb)

    @pl.when(jnp.logical_not(several_images(small_ref, seq)))
    def _():
        for qb in range(LEN // BLK):
            for kb in range(LEN // BLK):
                if qb != kb:
                    tile(qb, kb)

    dqkv[0 : 2 * HD, :] = dqkv[0 : 2 * HD, :] * SCALE
    d_pieces = []
    for k in range(4):
        cols = pl.ds(pl.multiple_of(place_of(RING[k]) * BLK, BLK), BLK)
        d_pieces.append(nn(turned(dqkv[:, cols]), w_ref[...]).astype(BF))
    d_b = dqkv[...].astype(BF)
    gw = nn(d_b, normed_ref[...])
    gn = nn(d_b, unit_ref[...])
    gb = jnp.sum(d_b.astype(F32), axis=1, keepdims=True)

    @pl.when(seq == 0)
    def _():
        for k in range(4):
            down_ref[k] = d_pieces[k]
        acc[...] = gw
        acc_unit[...] = gn
        acc_bias[...] = gb

    @pl.when(seq == 1)
    def _():
        for k in range(4):
            dother_ref[k] = d_pieces[k]
        w = w_ref[...].astype(F32)
        gb_all = acc_bias[...] + gb
        rows = jnp.concatenate(
            [
                acc[...] + gw,
                jnp.sum(w * (acc_unit[...] + gn), axis=0, keepdims=True),
                jnp.sum(w * gb_all, axis=0, keepdims=True),
                vgrad_ref[0:4],
                jnp.zeros((256 - SMALL - 6, D), F32),
            ],
            axis=0,
        )
        gbuf[...] = rows.T
        head = head_index()
        fold = (iota((24, HD), 0) == iota((24, HD), 1) // 2).astype(F32)
        lane = iota((HD, 256), 1) == SMALL + 6 + iota((HD, 256), 0) % 2
        for part, group in ((0, head), (2, 16 + head)):
            spreads = jnp.where(lane, jnp.broadcast_to(gb_all[part * HD : (part + 1) * HD], (HD, 256)), 0.0)
            gbuf[group_rows(group), :] += nn(fold, spreads)
        half = pl.ds(pl.multiple_of(lax.axis_index("c") * (D // 2), 8), D // 2)
        gbuf[half, SMALL + 8 : SMALL + 12] = ugrad_ref[:, 8:12]
        for z in range(8):
            for g in range(4):
                y, c = g // 2, g % 2
                at = (y * 8 + z) * 48 + c * 24
                out_ref[z, :, g * WIN : (g + 1) * WIN] = gbuf[at : at + 24, 0:WIN].astype(BF)


def attend_bwd(qkv, lse, wide, datt, normed, unit, w_t, small, vgrads, ugrads):
    return grid_call(
        attend_bwd_kernel,
        2,
        [
            step_block(SMALL, LEN),
            step_block(1, LEN),
            step_block(HD, LEN),
            pl.BlockSpec((8, HD, ROWS), lambda i: (0, 0, i)),
            step_block(LEN, D),
            step_block(LEN, D),
            full(SMALL, D),
            full(D, 16),
            full(8, D),
            full(D // 2, 16),
        ],
        [full(4, BLK, D), full(4, BLK, D), full(8, LINE, D)],
        [in_hbm(4, BLK, D), in_hbm(4, BLK, D), like(8, LINE, D)],
        [
            pltpu.VMEM((LEN, HD), BF),
            pltpu.VMEM((LEN, HD), BF),
            pltpu.VMEM((SMALL, LEN), F32),
            pltpu.VMEM((SMALL, D), F32),
            pltpu.VMEM((SMALL, D), F32),
            pltpu.VMEM((SMALL, 1), F32),
            pltpu.VMEM((D, 256), F32),
        ],
        "attend_bwd",
        11,
        12_000_000,
        32,
    )(*pinned(qkv, lse, wide), datt, *pinned(normed, unit, w_t), small, vgrads, ugrads)


def out_copies(rows_ref, wbuf, sem):
    return [
        pltpu.make_async_copy(rows_ref.at[k, pl.ds(0, 48)], wbuf.at[pl.ds(48 * k, 48)], sem.at[k]) for k in range(8)
    ]


def branch_kernel(att_ref, rows_ref, own_ref, send_ref, wbuf, sem):
    copies = out_copies(rows_ref, wbuf, sem)
    for copy in copies:
        copy.start()
    for copy in copies:
        copy.wait()
    out = tn(att_ref[...], wbuf[...])
    own_ref[...] = out[:ROWS]
    send_ref[...] = out[ROWS:]


def branch(att, rows_full):
    return grid_call(
        branch_kernel, 1, [full(8 * HD, 2 * ROWS), HBM], [full(ROWS, D)] * 2, [like(ROWS, D, dtype=F32)] * 2,
        [pltpu.VMEM((8 * HD, D), BF), pltpu.SemaphoreType.DMA((8,))], "branch", 2, 2_000_000,
    )(att, *pinned(rows_full))


def unit_rows(v):
    center = jnp.mean(v, axis=-1, keepdims=True)
    centered = v - center
    inverse = lax.rsqrt(jnp.mean(centered * centered, axis=-1, keepdims=True) + EPS)
    return centered * inverse, inverse


def norm_back(d, unit, inverse, gain):
    dg = d * gain
    return inverse * (dg - jnp.mean(dg, axis=-1, keepdims=True) - unit * jnp.mean(dg * unit, axis=-1, keepdims=True))


def middle_kernel(x_ref, own_ref, got_ref, vec_ref, res_ref, n2_ref):
    res = x_ref[...].astype(F32) + own_ref[...] + got_ref[...] + vec_ref[2:3]
    res_ref[...] = res
    n2_ref[...] = (unit_rows(res)[0] * vec_ref[3:4] + vec_ref[4:5]).astype(BF)


def middle(x, own, got, vec):
    one = full(ROWS, D)
    return grid_call(
        middle_kernel, 1, [one, one, one, full(16, D)], [one, one], [like(ROWS, D, dtype=F32), like(ROWS, D)],
        [], "middle", 1, 2_000_000,
    )(x, own, got, vec)


def after_kernel(own_ref, core_ref, got_ref, res_ref, cot_ref, vec_ref, dres_ref, dbr_ref, vg_ref):
    cot = cot_ref[...].astype(F32)
    unit, inverse = unit_rows(res_ref[...])
    dn = own_ref[...] + core_ref[0].astype(F32) + got_ref[...].astype(F32)
    dres = cot + norm_back(dn, unit, inverse, vec_ref[3:4])
    dbr = dres.astype(BF)
    dres_ref[...] = dres
    dbr_ref[...] = dbr
    sums = [dbr.astype(F32), dn * unit, dn, cot]
    for i, v in enumerate(sums):
        vg_ref[i : i + 1] = jnp.sum(v, axis=0, keepdims=True)
    vg_ref[4:8] = jnp.zeros((4, D), F32)


def after(own, core, got, res, cot, vec):
    one = full(ROWS, D)
    return grid_call(
        after_kernel, 1, [one, full(2, ROWS, D), one, one, one, full(16, D)], [one, one, full(8, D)],
        [like(ROWS, D, dtype=F32), like(ROWS, D), like(8, D, dtype=F32)], [], "after", 2, 3_000_000,
    )(own, core, got, res, cot, vec)


def branch_bwd_kernel(att_ref, own_ref, other_ref, rows_ref, grads_in, datt_ref, grads_ref, wbuf, gbuf, sem):
    copies = out_copies(rows_ref, wbuf, sem)
    for copy in copies:
        copy.start()
    d = jnp.concatenate([own_ref[...], other_ref[...]], axis=0)
    gbuf[...] = nn(att_ref[...], d).astype(BF)
    backs = [
        pltpu.make_async_copy(gbuf.at[pl.ds(48 * k, 48)], grads_ref.at[k, pl.ds(0, 48)], sem.at[8 + k]) for k in range(8)
    ]
    for back in backs:
        back.start()
    for copy in copies:
        copy.wait()
    datt_ref[...] = nt(wbuf[...], d).astype(BF)
    for back in backs:
        back.wait()


def branch_bwd(att, own, other, rows_full, grads):
    return pl.pallas_call(
        branch_bwd_kernel,
        grid=(1,),
        in_specs=[full(8 * HD, 2 * ROWS), full(ROWS, D), full(ROWS, D), HBM, HBM],
        out_specs=[full(8 * HD, 2 * ROWS), HBM],
        out_shape=[like(8 * HD, 2 * ROWS), in_hbm(8, BLOCK, D)],
        scratch_shapes=[pltpu.VMEM((8 * HD, D), BF), pltpu.VMEM((8 * HD, D), BF), pltpu.SemaphoreType.DMA((16,))],
        input_output_aliases={4: 1},
        compiler_params=params(8),
        cost_estimate=cost(3, 3_000_000),
        name="branch_bwd",
    )(att, own, other, *pinned(rows_full, grads))


TILE = 256
UNITS = FF // 4
STEPS = UNITS // TILE
FOUR = 4 * ROWS


def mlp_kernel(*refs):
    rows, cots = refs[:4], refs[4:8]
    (small_ref, w_ref, oself, ocore, oline, dself, dcore, dline, g_ref, gb_ref,
     nbuf, cbuf, ubuf, dbuf, gdbuf, gubuf, out, sems) = refs[8:]
    j = pl.program_id(0)

    @pl.when(j == 0)
    def _():
        copies = []
        for z in range(8):
            for y in range(2):
                source, target = w_ref.at[z, pl.ds(144 + y * 48, 48)], ubuf.at[pl.ds(y * 384 + z * 48, 48)]
                copies.append(pltpu.make_async_copy(source, target, sems.at[3 * z + y]))
            source, target = w_ref.at[z, pl.ds(48, 96)], dbuf.at[pl.ds(z * 96, 96)]
            copies.append(pltpu.make_async_copy(source, target, sems.at[3 * z + 2]))
        for copy in copies:
            copy.start()
        for i in range(4):
            nbuf[i * ROWS : (i + 1) * ROWS] = rows[i][...]
            cbuf[i * ROWS : (i + 1) * ROWS] = cots[i][...]
        for copy in copies:
            copy.wait()

    spot = pl.ds(pl.multiple_of(j * TILE, TILE), TILE)
    wu, wd = ubuf[:, spot], dbuf[spot, :]
    half = pl.ds(pl.multiple_of(lax.axis_index("c") * (D // 2), 8), D // 2)
    row = iota((D // 2, 1), 0)
    first = row // 24 * 48 + lax.rem(row, 24) // 6 * 12 + lax.rem(row, 3) * 4
    mine = lax.rem(row, 6) // 3 == lax.axis_index("yh")
    at = jnp.where(mine, first, -4) // 4
    keep = at == iota((D // 2, TILE), 1) // 4 + j * (TILE // 4)
    pick = (iota((16, TILE), 0) == 8 + iota((16, TILE), 1) % 4).astype(F32)
    bias = jnp.sum(jnp.where(keep, nn(small_ref[half, :], pick), 0.0), axis=0, keepdims=True)
    up = nn(nbuf[...], wu) + bias
    cdf = 0.5 * (1.0 + lax.erf(up * 2.0 ** (-0.5)))
    hidden = (up * cdf).astype(BF)
    dh = nt(cbuf[...], wd).astype(BF).astype(F32)
    slope = cdf + up * jnp.exp(-0.5 * up * up) * (2.0 * math.pi) ** (-0.5)
    d_up = (dh * slope).astype(BF)
    total = jnp.sum(d_up.astype(F32), axis=0, keepdims=True)
    gb = nt(jnp.where(keep, jnp.broadcast_to(total, keep.shape), 0.0), pick)
    gdbuf[spot, :] = tn(hidden, cbuf[...]).astype(BF)
    gu = tn(nbuf[...], d_up).astype(BF)
    for z in range(8):
        for y in range(2):
            gubuf[z, y * 48 : y * 48 + 48, spot] = gu[y * 384 + z * 48 : y * 384 + z * 48 + 48]
    out_part = nn(hidden, wd)
    dn_part = nt(d_up, wu)

    @pl.when(j == 0)
    def _():
        out[0] = out_part
        out[1] = dn_part
        gb_ref[...] = gb

    @pl.when(j > 0)
    def _():
        out[0] += out_part
        out[1] += dn_part
        gb_ref[...] += gb

    @pl.when(j == STEPS - 1)
    def _():
        backs = [
            pltpu.make_async_copy(gdbuf.at[pl.ds(96 * z, 96)], g_ref.at[z, pl.ds(48, 96)], sems.at[z]) for z in range(8)
        ]
        backs.append(pltpu.make_async_copy(gubuf, g_ref.at[:, pl.ds(144, 96)], sems.at[8]))
        for back in backs:
            back.start()
        for i, (own, core, line) in enumerate(((oself, ocore, oline), (dself, dcore, dline))):
            own[...] = out[i, :ROWS]
            core[0] = out[i, ROWS : 2 * ROWS].astype(BF)
            line[...] = out[i, 2 * ROWS : 3 * ROWS]
            core[1] = out[i, 3 * ROWS :].astype(BF)
        for back in backs:
            back.wait()


def mlp(rows, cots, small, rows_full):
    one, two = full(ROWS, D), full(2, ROWS, D)
    parts = [in_hbm(ROWS, D, dtype=F32), like(2, ROWS, D), like(ROWS, D, dtype=F32)]
    return grid_call(
        mlp_kernel,
        STEPS,
        [one] * 8 + [full(D, 16), HBM],
        [one, two, one] * 2 + [HBM, full(D // 2, 16)],
        parts * 2 + [in_hbm(8, BLOCK, D), in_hbm(D // 2, 16, dtype=F32)],
        [
            pltpu.VMEM((FOUR, D), BF),
            pltpu.VMEM((FOUR, D), BF),
            pltpu.VMEM((D, UNITS), BF),
            pltpu.VMEM((UNITS, D), BF),
            pltpu.VMEM((UNITS, D), BF),
            pltpu.VMEM((8, 96, UNITS), BF),
            pltpu.VMEM((2, FOUR, D), F32),
            pltpu.SemaphoreType.DMA((24,)),
        ],
        "mlp",
        10,
        8_000_000,
        32,
    )(*rows, *cots, small, *pinned(rows_full))


def join_kernel(own_ref, got_ref, pair, left, right, far0, far1):
    for k, ref in enumerate((pair, left, right)):
        ref[...] = (own_ref[k].astype(F32) + got_ref[k].astype(F32)).astype(BF)
    far = (own_ref[3].astype(F32) + got_ref[3].astype(F32)).astype(BF)
    far0[...] = far[:ROWS]
    far1[...] = far[ROWS:]


def join(own, got):
    pieces = [(BLK, D)] * 3 + [(ROWS, D)] * 2
    return grid_call(
        join_kernel, 1, [full(4, BLK, D)] * 2, [full(*p) for p in pieces], [like(*p) for p in pieces],
        [], "join", 1, 5_000_000, 16,
    )(*pinned(own, got))


def deal_kernel(got_ref, sum_ref, out_ref, buf, line):
    total = got_ref[0].astype(F32)
    for z in range(1, 8):
        total = total + got_ref[z].astype(F32)
    line[...] = total
    buf[...] = jnp.zeros(buf.shape, F32)
    for b in range(8):
        for c in range(2):
            k = c * 8 + b
            buf[c * 15 : c * 15 + 3] = sum_ref[3 * k : 3 * k + 3].astype(F32)
            at = 48 + (c * 4 + b // 2) * 12
            down = sum_ref[at : at + 12].astype(F32)
            buf[c * 15 + 3 : c * 15 + 15] = jnp.where(lax.axis_index("yh") == b % 2, down, 0.0)
            for y in range(2):
                at, row = 144 + y * 48 + 3 * k, 30 + (y * 2 + c) * 3
                buf[row : row + 3] = sum_ref[at : at + 3].astype(F32)
        buf[42:45] = line[3 * b : 3 * b + 3]
        out_ref[b] = buf[...].astype(BF)


def deal(got, sums):
    return grid_call(
        deal_kernel, 1, [full(8, LINE, D), full(BLOCK, D)], full(8, SENT, D), like(8, SENT, D),
        [pltpu.VMEM((SENT, D), F32), pltpu.VMEM((LINE, D), F32)], "deal", 2, 2_000_000,
    )(got, *pinned(sums))


def share_kernel(got_ref, own_ref, core_ref, line_ref, both_ref, buf, tot):
    core0, yl0 = lax.axis_index("c") == 0, lax.axis_index("yl") == 0
    parts = [got_ref[b].astype(F32) for b in range(8)]
    for y in range(2):
        total = parts[y]
        for b in range(2 + y, 8, 2):
            total = total + parts[b]
        tot[y] = total
    both_units = tot[0] + tot[1]
    buf[...] = jnp.zeros(buf.shape, F32)
    for g in range(4):
        c = g % 2
        buf[g, 0:15] = both_units[c * 15 : c * 15 + 15]
        for y in range(2):
            buf[g, 15 + 3 * y : 18 + 3 * y] = tot[y, 30 + 3 * g : 33 + 3 * g]
        for b in range(8):
            row, lane = 21 + 3 * (b // 4), (b % 4) * WIN
            buf[g, row : row + 3, lane : lane + WIN] = parts[b][42:45, g * WIN : (g + 1) * WIN]
        buf[g, 21:24, SMALL : SMALL + 16] = both_units[42:45, g * WIN + SMALL : g * WIN + SMALL + 16]
    groups = groups_of(*(buf[g] for g in range(4)), core0, yl0)
    own_ref[...] = groups[0]
    core_ref[...] = groups[1].astype(BF)
    line_ref[...] = groups[2].astype(BF)
    both_ref[...] = groups[3].astype(BF)


def share(got):
    one = full(PACK, D)
    return grid_call(
        share_kernel, 1, [full(8, SENT, D)], [one] * 4, [like(PACK, D, dtype=F32)] + [like(PACK, D)] * 3,
        [pltpu.VMEM((4, PACK, D), F32), pltpu.VMEM((2, SENT, D), F32)], "share", 2, 2_000_000,
    )(got)


def finish_kernel(own_ref, core_ref, line_ref, both_ref, order_ref, wq_ref, wu_ref, wo_ref, wd_ref, *refs):
    vectors, (buf, qbuf, cbuf) = refs[:8], refs[8:]
    core0 = lax.axis_index("c") == 0
    aligned = lax.axis_index("c") == lax.axis_index("yl")
    own, core, line, both = (r[...].astype(F32) for r in (own_ref, core_ref, line_ref, both_ref))
    cbuf[...] = jnp.zeros(cbuf.shape, F32)
    buf[0] = jnp.where(aligned, own + line, core + both)
    wo_ref[...] = buf[0, 0:3]
    wd_ref[...] = buf[0, 3:15]
    mine, theirs = own + line, core + both
    buf[0] = jnp.where(core0, mine, theirs)
    buf[1] = jnp.where(core0, theirs, mine)
    for k in range(2):
        for q in range(2):
            to = slice(q * (D // 2), (q + 1) * (D // 2))
            at = 8 * (2 * k + q)
            for y in range(2):
                cbuf[at : at + 3, y * (D // 2) : (y + 1) * (D // 2)] = buf[k, 15 + 3 * y : 18 + 3 * y, to]
        for b in range(8):
            row, lane, at = 21 + 3 * (b // 4), (b % 4) * WIN, (k * 8 + b) * HD
            for p in range(3):
                qbuf[0:3, p * D + at : p * D + at + HD] = buf[k, row : row + 3, lane + p * HD : lane + (p + 1) * HD]
    wq_ref[...] = qbuf[0:3]
    rest = cbuf[...]
    parts = []
    for _ in range(3):
        parts.append(rest.astype(BF))
        rest = rest - parts[-1].astype(F32)
    sums = nt(jnp.concatenate(parts, axis=0), order_ref[...])
    total = sums[0:32] + sums[32:64] + sums[64:96]
    for i in range(4):
        wu_ref[:, i * D : (i + 1) * D] = total[8 * i : 8 * i + 3]
    small = (buf[0] + buf[1])[21:24, SMALL : SMALL + 16]

    def row_of(first, stride, count):
        shape = (3, count)
        keep = iota(shape, 1) // stride == iota(shape, 0)
        total = jnp.zeros((1, count), F32)
        for k in range(stride):
            values = jnp.broadcast_to(small[:, first + k : first + k + 1], shape)
            total += jnp.sum(jnp.where(keep & (iota(shape, 1) % stride == k), values, 0.0), axis=0, keepdims=True)
        return total.reshape(count)

    for i in range(6):
        vectors[i][...] = row_of(i, 1, 3)
    vectors[6][...] = row_of(6, 2, 6)
    vectors[7][...] = row_of(8, 4, 12)


def finish(parts, order):
    shapes = [(3, 3 * D), (3, FF), (3, D), (12, D)] + [(3,)] * 6 + [(6,), (12,)]
    return grid_call(
        finish_kernel, 1, [full(PACK, D)] * 4 + [full(D, D)], [full(*s) for s in shapes], [like(*s, dtype=F32) for s in shapes],
        [pltpu.VMEM((2, PACK, D), F32), pltpu.VMEM((8, 3 * D), F32), pltpu.VMEM((32, D), F32)], "finish", 2, 1_000_000,
    )(*parts, *pinned(order))


AXES = ("yl", "z", "c", "x", "yh")
SEQ = ("yl", "z", "c")
BAND = ("x", "yh")
SWAP = [(0, 1), (1, 0)]
RIGHT = [(i, (i + 1) % 4) for i in range(4)]
LEFT = [(i, (i + 3) % 4) for i in range(4)]


def swap_core(v):
    return lax.ppermute(v, "c", SWAP)


def swap_yl(v):
    return lax.ppermute(v, "yl", SWAP)


def swap_yh(v):
    return lax.ppermute(v, "yh", SWAP)


def swap_both(v):
    return lax.ppermute(v, ("yl", "c"), [(0, 3), (1, 2), (2, 1), (3, 0)])


def four_rows(v):
    line = swap_yh(v)
    return v, swap_core(v), line, swap_core(line)


def exchange(v, axes):
    return lax.all_to_all(v, axes, 0, 0, tiled=True)


def ring_far(far0, far1):
    return lax.ppermute(far0, "x", RIGHT), lax.ppermute(far1, "x", LEFT)


def ring_near(left, right, from_left, from_right):
    from_left, from_right = from_left.astype(F32), from_right.astype(F32)
    n = from_left.shape[0]
    right = jnp.concatenate([(right[:n].astype(F32) + from_left).astype(BF), right[n:]], axis=0)
    left = jnp.concatenate([left[:n], (left[n:].astype(F32) + from_right).astype(BF)], axis=0)
    return lax.ppermute(right, "x", RIGHT), lax.ppermute(left, "x", LEFT)


def per_device(
    tokens, image_ids, ln1_gain, ln1_bias, w_qkv, qv_bias, w_out, out_bias,
    ln2_gain, ln2_bias, w_up, up_bias, w_down, down_bias, cotangent,
):
    first = lax.axis_index("yh") == 0
    x = tokens[0]
    cot = cotangent[0]

    order = unit_order()
    pack_own, pack_other = prep(
        w_qkv, w_up, w_out, w_down, (ln1_gain, ln1_bias, out_bias, ln2_gain, ln2_bias, down_bias, qv_bias, up_bias),
        image_ids, order,
    )
    got_yh = swap_yh(x)
    pair = jnp.stack([jnp.where(first, x, got_yh), jnp.where(first, got_yh, x)])
    sent = spread((pack_own, swap_core(pack_other), swap_yl(pack_own), swap_both(pack_other)))
    sent, pair = lax.optimization_barrier((sent, pair))
    got, pair = lax.optimization_barrier((exchange(sent, BAND), pair))
    left = lax.ppermute(pair, "x", RIGHT)
    right = lax.ppermute(pair, "x", LEFT)
    block, line = collect(got)
    rows_full = lax.all_gather(block, "z", axis=0)
    far0 = lax.ppermute(left[0], "x", RIGHT)
    far1 = lax.ppermute(right[1], "x", LEFT)
    line_got = exchange(line, "z")
    token_pieces = (pair.reshape(BLK, D), left.reshape(BLK, D), right.reshape(BLK, D), far0, far1)
    other_pieces = tuple(swap_core(v) for v in token_pieces)
    cots = four_rows(cot)

    normed, unit, qkv, att, wide, lse, w_t, vec, small = attend_fwd(token_pieces + other_pieces, line_got)
    att, *cots = lax.optimization_barrier((att, *cots))
    att_c = exchange(att, BAND).reshape(8 * HD, 2 * ROWS)
    branch_own, branch_send = branch(att_c, rows_full)
    residual, n2 = middle(x, branch_own, swap_core(branch_send), vec)

    rows = four_rows(n2)
    o_self, o_core, o_line, d_self, d_core, d_line, grads, ugrads = mlp(rows, cots, small, rows_full)
    d_core = swap_core(d_core)
    d_line = swap_yh((d_line + d_core[1].astype(F32)).astype(BF))
    d_res, d_branch, vgrads = after(d_self, d_core, d_line, residual, cot, vec)
    d_att, grads = branch_bwd(att_c, d_branch, swap_core(d_branch), rows_full, grads)
    grad_sum = lax.psum_scatter(grads, "z", scatter_dimension=0, tiled=True).reshape(BLOCK, D)
    d_att_all = exchange(d_att.reshape(8, HD, 2 * ROWS), BAND)
    o_core = swap_core(o_core)
    o_line = swap_yh((o_line + o_core[1].astype(F32)).astype(BF))
    output = residual + o_self + o_core[0].astype(F32) + o_line.astype(F32) + vec[5:6]

    d_own, d_other, line_grad = attend_bwd(qkv, lse, wide, d_att_all, normed, unit, w_t, small, vgrads, ugrads)
    line_sum = exchange(line_grad, "z")
    d_pair, d_left, d_right, d_far0, d_far1 = join(d_own, swap_core(d_other))
    line_sum, d_far0, d_far1 = lax.optimization_barrier((line_sum, *ring_far(d_far0, d_far1)))
    from_left, from_right = ring_near(d_left, d_right, d_far0, d_far1)
    last, from_left, from_right = lax.optimization_barrier((exchange(deal(line_sum, grad_sum), BAND), from_left, from_right))
    total = d_pair.astype(F32) + from_left.astype(F32) + from_right.astype(F32)
    keep = jnp.where(first, total[:ROWS], total[ROWS:])
    give = jnp.where(first, total[ROWS:], total[:ROWS])
    d_normed = keep + swap_yh(give.astype(BF)).astype(F32)
    unit1, inv1 = unit_rows(x.astype(F32))
    d_tokens = (d_res + norm_back(d_normed, unit1, inv1, vec[0:1])).astype(BF)

    own, to_core, to_yl, to_both = share(last)
    done = finish((own, swap_core(to_core), swap_yl(to_yl), swap_both(to_both)), order)
    g_qkv, g_up, g_out, g_down, l1g, l1b, ob, l2g, l2b, db, qvb, upb = done
    return (
        output.astype(BF)[None], d_tokens[None], l1g, l1b, g_qkv, qvb, g_out, ob, l2g, l2b, g_up, upb, g_down, db,
    )


def solution(mesh):
    fine = Mesh(mesh.devices.reshape(2, 8, 2, 4, 2), AXES)
    seq_band = P(SEQ, BAND, None)
    flat, flat2 = P(AXES), P(AXES, None)
    in_specs = (
        seq_band, P(SEQ, BAND), flat, flat, flat2, flat, flat2, flat,
        flat, flat, flat2, flat, flat2, flat, seq_band,
    )
    out_specs = (
        seq_band, seq_band, flat, flat, flat2, flat, flat2, flat,
        flat, flat, flat2, flat, flat2, flat,
    )
    return jax.shard_map(per_device, mesh=fine, in_specs=in_specs, out_specs=out_specs, check_vma=False)
```

```python
import math

import jax
import jax.numpy as jnp
from jax import lax
from jax.experimental import pallas as pl
from jax.experimental.pallas import tpu as pltpu
from jax.sharding import Mesh, PartitionSpec as P

D = 768
HEADS = 16
HD = 48
FF = 3072
LEN = 1024
ROWS = 128
BLK = 256
HALF = FF // 2
EPS = 1e-05
SCALE = HD ** (-0.5)
BF = jnp.bfloat16
F32 = jnp.float32
HBM = pl.BlockSpec(memory_space=pltpu.HBM)


def nn(a, b):
    return lax.dot_general(a, b, (((1,), (0,)), ((), ())), preferred_element_type=F32)


def nt(a, b):
    return lax.dot_general(a, b, (((1,), (1,)), ((), ())), preferred_element_type=F32)


def tn(a, b):
    return lax.dot_general(a, b, (((0,), (0,)), ((), ())), preferred_element_type=F32)


def turned(a):
    return a.astype(F32).T.astype(BF)


def params(mebi):
    return pltpu.CompilerParams(vmem_limit_bytes=mebi << 20)


def cost(micros, size):
    return pl.CostEstimate(flops=1000, bytes_accessed=1000, transcendentals=0)


def grid_call(kernel, steps, ins, outs, out_shape, scratch, name, micros, size, mebi=8):
    return pl.pallas_call(
        kernel,
        grid=(steps,),
        in_specs=ins,
        out_specs=outs,
        out_shape=out_shape,
        scratch_shapes=scratch,
        compiler_params=params(mebi),
        cost_estimate=cost(micros, size),
        name=name,
    )


def pinned(*values):
    return tuple(pltpu.with_memory_space_constraint(v, pltpu.HBM) for v in values)


def in_hbm(*shape, dtype=BF):
    return pltpu.HBM(shape, dtype)


def full(*shape):
    return pl.BlockSpec(shape, lambda i: (0,) * len(shape))


def step_block(*shape):
    return pl.BlockSpec((None,) + shape, lambda i: (i,) + (0,) * len(shape))


def iota(shape, axis):
    return lax.broadcasted_iota(jnp.int32, shape, axis)


def like(*shape, dtype=BF):
    return jax.ShapeDtypeStruct(shape, dtype)


WIN = 192
SMALL = 3 * HD
PACK = 32


def unit_order():
    source = iota((D, 1), 0)
    part = lax.rem(source, 24)
    target = part // 12 * (D // 2) + source // 96 * 48 + lax.rem(source, 96) // 24 * 12 + lax.rem(part, 12)
    return (target == iota((D, D), 1)).astype(F32).astype(BF)


def prep_kernel(*refs):
    sources, (own_ref, other_ref, unit_ref, wide_ref, inv_ref), held, (buf, cbuf, sems) = refs[:14], refs[14:19], refs[19:33], refs[33:]
    copies = [pltpu.make_async_copy(a, b, sems.at[i]) for i, (a, b) in enumerate(zip(sources, held))]
    for copy in copies:
        copy.start()
    buf[...] = jnp.zeros(buf.shape, F32)
    cbuf[...] = jnp.zeros(cbuf.shape, F32)
    order = unit_order()
    copies[13].wait()
    unit, inverse = unit_rows(held[13][...].astype(F32))
    unit_ref[...] = unit.astype(BF)
    wide_ref[...] = unit
    inv_ref[...] = inverse
    for copy in copies[:13]:
        copy.wait()
    wq_ref, wu_ref, wo_ref, wd_ref = held[:4]
    vectors, ids_ref = held[4:12], held[12]

    def column(ref, stride, k):
        row = ref[...].astype(F32).reshape(1, ref.shape[0])
        shape = (3, ref.shape[0])
        keep = iota(shape, 1) == iota(shape, 0) * stride + k
        return jnp.sum(jnp.where(keep, jnp.broadcast_to(row, shape), 0.0), axis=1, keepdims=True)

    columns = [column(ref, 1, 0) for ref in vectors[:6]]
    columns += [column(vectors[6], 2, k) for k in range(2)]
    columns += [column(vectors[7], 4, k) for k in range(4)]
    mark = jnp.max(ids_ref[...].astype(F32), axis=1, keepdims=True)
    columns.append(jnp.broadcast_to(mark, (3, 1)))
    lanes = iota((3, 128), 1)
    small = jnp.zeros((3, 128), F32)
    for j, col in enumerate(columns):
        small = jnp.where(lanes == j, jnp.broadcast_to(col, (3, 128)), small)
    wq = wq_ref[...].astype(F32)
    for i in range(4):
        cbuf[8 * i : 8 * i + 3] = wu_ref[:, i * D : (i + 1) * D].astype(F32)
    chosen = nn(cbuf[...].astype(BF), order)
    for k in range(2):
        buf[k, 0:3] = wo_ref[...].astype(F32)
        buf[k, 3:15] = wd_ref[...].astype(F32)
        for q in range(2):
            at = 8 * (2 * k + q)
            for y in range(2):
                to = slice(q * (D // 2), (q + 1) * (D // 2))
                buf[k, 15 + 3 * y : 18 + 3 * y, to] = chosen[at : at + 3, y * (D // 2) : (y + 1) * (D // 2)]
        for b in range(8):
            row, lane, at = 21 + 3 * (b // 4), (b % 4) * WIN, (k * 8 + b) * HD
            for p in range(3):
                buf[k, row : row + 3, lane + p * HD : lane + (p + 1) * HD] = wq[:, p * D + at : p * D + at + HD]
            buf[k, row : row + 3, lane + SMALL : lane + SMALL + 16] = small[:, :16]
    core0 = lax.axis_index("c") == 0
    own_ref[...] = jnp.where(core0, buf[0], buf[1]).astype(BF)
    other_ref[...] = jnp.where(core0, buf[1], buf[0]).astype(BF)


def prep(w_qkv, w_up, w_out, w_down, vectors, ids, x):
    args = (w_qkv, w_up, w_out, w_down) + vectors + (ids, x)
    return grid_call(
        prep_kernel, 1, [HBM] * len(args), [full(PACK, D)] * 2 + [full(ROWS, D)] * 2 + [full(ROWS, 1)],
        [like(PACK, D)] * 2 + [like(ROWS, D), in_hbm(ROWS, D, dtype=F32), in_hbm(ROWS, 1, dtype=F32)],
        [pltpu.VMEM(a.shape, a.dtype) for a in args]
        + [pltpu.VMEM((2, PACK, D), F32), pltpu.VMEM((32, D), F32), pltpu.SemaphoreType.DMA((len(args),))],
        "prep", 2, 100_000,
    )(*pinned(*args))


def groups_of(own, core, line, both, core0, yl0):
    def pick(a, b, c, d):
        return jnp.where(yl0, jnp.where(core0, a, b), jnp.where(core0, c, d))

    return (
        pick(own, core, line, both),
        pick(core, own, both, line),
        pick(line, both, own, core),
        pick(both, line, core, own),
    )


SENT = 48


def spread_kernel(own_ref, core_ref, line_ref, both_ref, out_ref, buf):
    core0, yl0 = lax.axis_index("c") == 0, lax.axis_index("yl") == 0
    aligned = lax.axis_index("c") == lax.axis_index("yl")
    own, core, line, both = (r[...].astype(F32) for r in (own_ref, core_ref, line_ref, both_ref))
    same, cross = jnp.where(aligned, own, line), jnp.where(aligned, core, both)
    buf[...] = jnp.zeros(buf.shape, F32)
    buf[0:15] = jnp.where(core0, same, cross)[0:15]
    buf[15:30] = jnp.where(core0, cross, same)[0:15]
    groups = groups_of(own, core, line, both, core0, yl0)
    for b in range(8):
        y, row, lane = b % 2, 21 + 3 * (b // 4), (b % 4) * WIN
        for g in range(4):
            buf[30 + 3 * g : 33 + 3 * g] = groups[g][15 + 3 * y : 18 + 3 * y]
            buf[42:45, g * WIN : (g + 1) * WIN] = groups[g][row : row + 3, lane : lane + WIN]
        out_ref[b] = buf[...].astype(BF)


def spread(packs):
    return grid_call(
        spread_kernel, 1, [full(PACK, D)] * 4, full(8, SENT, D), like(8, SENT, D),
        [pltpu.VMEM((SENT, D), F32)], "spread", 1, 1_000_000,
    )(*packs)


BLOCK = 240
LINE = 24


def collect_kernel(got_ref, blk_ref, line_ref, buf, lbuf):
    yh = lax.axis_index("yh")
    for b in range(8):
        got = got_ref[b].astype(F32)
        for c in range(2):
            k = c * 8 + b
            buf[3 * k : 3 * k + 3] = got[c * 15 : c * 15 + 3]
            for y in range(2):
                at, row = 144 + y * 48 + 3 * k, 30 + (y * 2 + c) * 3
                buf[at : at + 3] = got[row : row + 3]
        lbuf[3 * b : 3 * b + 3] = got[42:45]
    for x in range(4):
        got = got_ref[2 * x + yh].astype(F32)
        for c in range(2):
            at = 48 + (c * 4 + x) * 12
            buf[at : at + 12] = got[c * 15 + 3 : c * 15 + 15]
    line = lbuf[...].astype(BF)
    for z in range(8):
        line_ref[z] = line
    blk_ref[...] = buf[...].astype(BF)


def collect(got):
    return grid_call(
        collect_kernel, 1, [full(8, SENT, D)], [full(BLOCK, D), full(8, LINE, D)], [in_hbm(BLOCK, D), like(8, LINE, D)],
        [pltpu.VMEM((BLOCK, D), F32), pltpu.VMEM((LINE, D), F32)], "collect", 2, 2_000_000,
    )(got)


def place_of(step):
    return lax.rem(lax.axis_index("x") + step, 4)


RING = (0, 3, 1, 2)


def head_index():
    return lax.axis_index("c") * 8 + lax.axis_index("x") * 2 + lax.axis_index("yh")


def group_rows(group):
    return pl.ds(pl.multiple_of(group * 24, 8), 24)


def pair_groups():
    at = (lax.axis_index("yl") * 8 + lax.axis_index("z")) * 2
    c = lax.axis_index("c")
    return at + c, at + 1 - c


def several_images(small_ref, seq):
    own, other = pair_groups()
    block = small_ref[group_rows(jnp.where(seq == 0, own, other)), :]
    marks = jnp.where(iota(block.shape, 1) == 12, block, 0.0)
    return jnp.max(marks) > 0.5


def piece_cols(k):
    return pl.ds(pl.multiple_of(place_of(RING[k]) * BLK, BLK), BLK)


def piece_copies(pieces, target, sems, s):
    at, copies = 0, []
    for i, piece in enumerate(pieces[5 * s : 5 * s + 5]):
        rows = piece.shape[0]
        copies.append(pltpu.make_async_copy(piece, target.at[s, pl.ds(at, rows)], sems.at[5 * s + i]))
        at += rows
    return copies


def attend_fwd_kernel(*refs):
    pieces = refs[:10]
    (line_ref, qkv_hbm, att_ref, wide_hbm, lse_hbm, wt_hbm, vec_ref, small_ref,
     xbuf, qkv_ref, wide_ref, lse_ref, wt_ref, keys_buf, wbuf, bias, sems) = refs[10:]
    seq = pl.program_id(0)

    def outgoing(s):
        return (
            pltpu.make_async_copy(qkv_ref.at[s], qkv_hbm.at[s], sems.at[10 + 3 * s]),
            pltpu.make_async_copy(wide_ref.at[s], wide_hbm.at[s], sems.at[11 + 3 * s]),
            pltpu.make_async_copy(lse_ref.at[s], lse_hbm.at[s], sems.at[12 + 3 * s]),
        )

    @pl.when(seq == 0)
    def _():
        for s in range(2):
            for copy in piece_copies(pieces, xbuf, sems, s):
                copy.start()
        wbuf[...] = jnp.zeros(wbuf.shape, F32)
        for z in range(8):
            line = line_ref[z].astype(F32)
            for g in range(4):
                y, c = g // 2, g % 2
                at = (y * 8 + z) * 48 + c * 24
                wbuf[at : at + 24, 0:WIN] = line[:, g * WIN : (g + 1) * WIN]
        turned_w = wbuf[...].T
        wt_ref[...] = turned_w[:SMALL].astype(BF)
        pltpu.make_async_copy(wt_ref, wt_hbm, sems.at[16]).start()
        vec_ref[...] = turned_w[SMALL : SMALL + 16]
        small_ref[...] = wbuf[:, SMALL : SMALL + 16]
        head = head_index()
        expand = (iota((HD, 24), 0) // 2 == iota((HD, 24), 1)).astype(F32)
        lane = iota((HD, 16), 1) == 6 + iota((HD, 16), 0) % 2
        for part, group in ((0, head), (2, 16 + head)):
            spreads = nn(expand, small_ref[group_rows(group), :])
            col = jnp.sum(jnp.where(lane, spreads, 0.0), axis=1, keepdims=True)
            bias[part * HD : (part + 1) * HD] = col
        bias[HD : 2 * HD] = jnp.zeros((HD, 1), F32)

    gain, off = vec_ref[0:1], vec_ref[1:2]
    for s in range(2):

        @pl.when(seq == s)
        def _(s=s):
            for copy in piece_copies(pieces, xbuf, sems, s):
                copy.wait()

    for k in range(4):
        rows = xbuf[seq, k * BLK : (k + 1) * BLK]
        normed = (rows.astype(F32) * gain + off).astype(BF)
        qkv_ref[seq, :, piece_cols(k)] = (nt(wt_ref[...], normed) + bias[...]).astype(BF)
    for s in range(2):

        @pl.when(seq == s)
        def _(s=s):
            outgoing(s)[0].start()

    keys_buf[...] = turned(qkv_ref[seq, HD : 2 * HD, :])

    def block(qb, keys):
        cols = slice(qb * BLK, (qb + 1) * BLK)
        vt = qkv_ref[seq, 2 * HD : 3 * HD, keys]
        s = nn(keys_buf[keys, :], qkv_ref[seq, 0:HD, cols]) * SCALE
        peak = jnp.max(s, axis=0, keepdims=True)
        e = jnp.exp(s - peak)
        total = jnp.sum(e, axis=0, keepdims=True)
        lse_ref[seq, :, cols] = peak + jnp.log(total)
        out = nn(vt, e.astype(BF)) * (1.0 / total)
        wide_ref[seq, :, cols] = out
        out = out.astype(BF)
        att_ref[2 * qb, :, :] = out[:, :ROWS]
        att_ref[2 * qb + 1, :, :] = out[:, ROWS:]

    several = several_images(small_ref, seq)

    @pl.when(jnp.logical_not(several))
    def _():
        for qb in range(LEN // BLK):
            block(qb, slice(0, LEN))

    @pl.when(several)
    def _():
        for qb in range(LEN // BLK):
            block(qb, slice(qb * BLK, (qb + 1) * BLK))

    for s in range(2):

        @pl.when(seq == s)
        def _(s=s):
            for copy in outgoing(s)[1:]:
                copy.start()

    @pl.when(seq == 1)
    def _():
        pltpu.make_async_copy(wt_ref, wt_hbm, sems.at[16]).wait()
        for s in range(2):
            for copy in outgoing(s):
                copy.wait()


def attend_fwd(pieces, line):
    return grid_call(
        attend_fwd_kernel,
        2,
        [HBM] * 10 + [full(8, LINE, D)],
        [HBM, pl.BlockSpec((8, HD, ROWS), lambda i: (0, 0, i)), HBM, HBM, HBM, full(16, D), full(D, 16)],
        [
            in_hbm(2, SMALL, LEN),
            like(8, HD, 2 * ROWS),
            in_hbm(2, HD, LEN, dtype=F32),
            in_hbm(2, 1, LEN, dtype=F32),
            in_hbm(SMALL, D),
            like(16, D, dtype=F32),
            like(D, 16, dtype=F32),
        ],
        [
            pltpu.VMEM((2, LEN, D), BF),
            pltpu.VMEM((2, SMALL, LEN), BF),
            pltpu.VMEM((2, HD, LEN), F32),
            pltpu.VMEM((2, 1, LEN), F32),
            pltpu.VMEM((SMALL, D), BF),
            pltpu.VMEM((LEN, HD), BF),
            pltpu.VMEM((D, 256), F32),
            pltpu.VMEM((SMALL, 1), F32),
            pltpu.SemaphoreType.DMA((17,)),
        ],
        "attend_fwd",
        9,
        10_000_000,
        24,
    )(*pinned(*pieces), line)


def attend_bwd_kernel(*refs):
    pieces = refs[:10]
    (qkv_hbm, lse_hbm, wide_hbm, datt_ref, w_hbm, small_ref, vec_ref, vgrad_ref, ugrad_ref,
     down_hbm, dother_hbm, out_ref,
     ubuf, qkv_ref, lse_ref, wide_ref, w_ref, dbuf,
     rows_buf, values_buf, dq_buf, dkv_buf, fbuf, acc, acc_bias, gbuf, sems) = refs[10:]
    seq = pl.program_id(0)

    def first_in():
        pairs = ((qkv_hbm, qkv_ref), (lse_hbm, lse_ref), (wide_hbm, wide_ref))
        return [pltpu.make_async_copy(a, b, sems.at[10 + i]) for i, (a, b) in enumerate(pairs)]

    def w_in():
        return pltpu.make_async_copy(w_hbm, w_ref, sems.at[13])

    def out(s):
        return pltpu.make_async_copy(dbuf.at[s], (down_hbm, dother_hbm)[s], sems.at[14 + s])

    @pl.when(seq == 0)
    def _():
        for copy in first_in() + [w_in()]:
            copy.start()
        for s in range(2):
            for copy in piece_copies(pieces, ubuf, sems, s):
                copy.start()
        for copy in first_in():
            copy.wait()

    rows_buf[:, 0 : 3 * HD] = turned(qkv_ref[seq])
    d_out = jnp.concatenate([datt_ref[b] for b in range(8)], axis=1)
    values_buf[:, 0:HD] = turned(d_out)
    delta_all = jnp.sum(d_out.astype(F32) * wide_ref[seq], axis=0, keepdims=True)
    QS, KS = 256, 256

    def scores(qb, kb):
        cols = slice(qb * QS, (qb + 1) * QS)
        keys = slice(kb * KS, (kb + 1) * KS)
        qt = qkv_ref[seq, 0:HD, cols]
        dt = d_out[:, cols]
        probs = jnp.exp(nn(rows_buf[keys, HD : 2 * HD], qt) * SCALE - lse_ref[seq, :, cols])
        ds = (probs * (nn(rows_buf[keys, 2 * HD : 3 * HD], dt) - delta_all[:, cols])).astype(BF)
        return probs.astype(BF), ds

    def products(qb, kb, probs, ds, first_q, first_k):
        cols = slice(qb * QS, (qb + 1) * QS)
        keys = slice(kb * KS, (kb + 1) * KS)
        dq = nn(qkv_ref[seq, HD : 2 * HD, keys], ds)
        dk = nn(ds, rows_buf[cols, 0:HD])
        dv = nn(probs, values_buf[cols, 0:HD])
        if first_q:
            dq_buf[:, cols] = dq
        else:
            dq_buf[:, cols] += dq
        if first_k:
            dkv_buf[keys, 0:HD] = dk
            dkv_buf[keys, HD : 2 * HD] = dv
        else:
            dkv_buf[keys, 0:HD] += dk
            dkv_buf[keys, HD : 2 * HD] += dv

    def sweep(tiles):
        seen_q, seen_k, held = set(), set(), None
        for tile in tiles + [None]:
            now = (tile, scores(*tile)) if tile else None
            if held is not None:
                (qb, kb), (probs, ds) = held
                products(qb, kb, probs, ds, qb not in seen_q, kb not in seen_k)
                seen_q.add(qb)
                seen_k.add(kb)
            held = now

    several = several_images(small_ref, seq)

    @pl.when(jnp.logical_not(several))
    def _():
        sweep([(qb, kb) for qb in range(LEN // QS) for kb in range(LEN // KS)])

    @pl.when(several)
    def _():
        for b in range(4):
            cols = slice(b * BLK, (b + 1) * BLK)
            qt = qkv_ref[seq, 0:HD, cols]
            dt = d_out[:, cols]
            probs = jnp.exp(nn(rows_buf[cols, HD : 2 * HD], qt) * SCALE - lse_ref[seq, :, cols])
            ds = (probs * (nn(rows_buf[cols, 2 * HD : 3 * HD], dt) - delta_all[:, cols])).astype(BF)
            dq_buf[:, cols] = nn(qkv_ref[seq, HD : 2 * HD, cols], ds)
            dkv_buf[cols, 0:HD] = nn(ds, rows_buf[cols, 0:HD])
            dkv_buf[cols, HD : 2 * HD] = nn(probs.astype(BF), values_buf[cols, 0:HD])

    dkv = dkv_buf[...]
    by_row = jnp.concatenate(
        [dq_buf[...].T * SCALE, dkv[:, 0:HD] * SCALE, dkv[:, HD : 2 * HD]], axis=1
    ).astype(BF)
    by_feature = turned(by_row)

    rows_buf[:, 0 : 3 * HD] = by_row
    fbuf[...] = by_feature

    @pl.when(seq == 0)
    def _():
        w_in().wait()

    for k in range(4):
        dbuf[seq, k] = nn(rows_buf[piece_cols(k), 0 : 3 * HD], w_ref[...]).astype(BF)
    for s in range(2):

        @pl.when(seq == s)
        def _(s=s):
            out(s).start()
            for copy in piece_copies(pieces, ubuf, sems, s):
                copy.wait()

    gn = jnp.zeros((SMALL, D), F32)
    for k in range(4):
        gn = gn + nn(fbuf[:, piece_cols(k)], ubuf[seq, k * BLK : (k + 1) * BLK])
    gb = jnp.sum(by_feature.astype(F32), axis=1, keepdims=True)

    @pl.when(seq == 0)
    def _():
        acc[...] = gn
        acc_bias[...] = gb

    @pl.when(seq == 1)
    def _():
        w = w_ref[...].astype(F32)
        gb_all = acc_bias[...] + gb
        gn_all = acc[...] + gn
        rows = jnp.concatenate(
            [
                gn_all * vec_ref[0:1] + gb_all * vec_ref[1:2],
                jnp.sum(w * gn_all, axis=0, keepdims=True),
                jnp.sum(w * gb_all, axis=0, keepdims=True),
                vgrad_ref[0:4],
                jnp.zeros((256 - SMALL - 6, D), F32),
            ],
            axis=0,
        )
        gbuf[...] = rows.T
        head = head_index()
        fold = (iota((24, HD), 0) == iota((24, HD), 1) // 2).astype(F32)
        lane = iota((HD, 256), 1) == SMALL + 6 + iota((HD, 256), 0) % 2
        for part, group in ((0, head), (2, 16 + head)):
            spreads = jnp.where(lane, jnp.broadcast_to(gb_all[part * HD : (part + 1) * HD], (HD, 256)), 0.0)
            gbuf[group_rows(group), :] += nn(fold, spreads)
        half = pl.ds(pl.multiple_of(lax.axis_index("c") * (D // 2), 8), D // 2)
        gbuf[half, SMALL + 8 : SMALL + 12] = ugrad_ref[:, 8:12]
        for z in range(8):
            for g in range(4):
                y, c = g // 2, g % 2
                at = (y * 8 + z) * 48 + c * 24
                out_ref[z, :, g * WIN : (g + 1) * WIN] = gbuf[at : at + 24, 0:WIN].astype(BF)
        for s in range(2):
            out(s).wait()


def attend_bwd(pieces, qkv, lse, wide, datt, w_t, small, vec, vgrads, ugrads):
    return grid_call(
        attend_bwd_kernel,
        2,
        [HBM] * 13
        + [pl.BlockSpec((8, HD, ROWS), lambda i: (0, 0, i)), HBM, full(D, 16), full(16, D), full(8, D), full(D // 2, 16)],
        [HBM, HBM, full(8, LINE, D)],
        [in_hbm(4, BLK, D), in_hbm(4, BLK, D), like(8, LINE, D)],
        [
            pltpu.VMEM((2, LEN, D), BF),
            pltpu.VMEM((2, SMALL, LEN), BF),
            pltpu.VMEM((2, 1, LEN), F32),
            pltpu.VMEM((2, HD, LEN), F32),
            pltpu.VMEM((SMALL, D), BF),
            pltpu.VMEM((2, 4, BLK, D), BF),
            pltpu.VMEM((LEN, SMALL), BF),
            pltpu.VMEM((LEN, HD), BF),
            pltpu.VMEM((HD, LEN), F32),
            pltpu.VMEM((LEN, 2 * HD), F32),
            pltpu.VMEM((SMALL, LEN), BF),
            pltpu.VMEM((SMALL, D), F32),
            pltpu.VMEM((SMALL, 1), F32),
            pltpu.VMEM((D, 256), F32),
            pltpu.SemaphoreType.DMA((16,)),
        ],
        "attend_bwd",
        10,
        12_000_000,
        28,
    )(*pinned(*pieces, qkv, lse, wide), datt, *pinned(w_t), small, vec, vgrads, ugrads)


def out_copies(rows_ref, wbuf, sem):
    return [
        pltpu.make_async_copy(rows_ref.at[k, pl.ds(0, 48)], wbuf.at[pl.ds(48 * k, 48)], sem.at[k]) for k in range(8)
    ]


def branch_kernel(att_ref, rows_ref, own_ref, send_ref, wbuf, sem):
    copies = out_copies(rows_ref, wbuf, sem)
    for copy in copies:
        copy.start()
    for copy in copies:
        copy.wait()
    out = tn(att_ref[...], wbuf[...])
    own_ref[...] = out[:ROWS]
    send_ref[...] = out[ROWS:]


def branch(att, rows_full):
    return grid_call(
        branch_kernel, 1, [full(8 * HD, 2 * ROWS), HBM], [full(ROWS, D)] * 2, [like(ROWS, D, dtype=F32)] * 2,
        [pltpu.VMEM((8 * HD, D), BF), pltpu.SemaphoreType.DMA((8,))], "branch", 2, 2_000_000,
    )(att, *pinned(rows_full))


def unit_rows(v):
    center = jnp.mean(v, axis=-1, keepdims=True)
    centered = v - center
    inverse = lax.rsqrt(jnp.mean(centered * centered, axis=-1, keepdims=True) + EPS)
    return centered * inverse, inverse


def norm_back(d, unit, inverse, gain):
    dg = d * gain
    return inverse * (dg - jnp.mean(dg, axis=-1, keepdims=True) - unit * jnp.mean(dg * unit, axis=-1, keepdims=True))


def middle_kernel(x_ref, own_ref, got_ref, vec_ref, res_ref, n2_ref):
    res = x_ref[...].astype(F32) + own_ref[...] + got_ref[...] + vec_ref[2:3]
    res_ref[...] = res
    n2_ref[...] = (unit_rows(res)[0] * vec_ref[3:4] + vec_ref[4:5]).astype(BF)


def middle(x, own, got, vec):
    one = full(ROWS, D)
    return grid_call(
        middle_kernel, 1, [one, one, one, full(16, D)], [one, one], [in_hbm(ROWS, D, dtype=F32), like(ROWS, D)],
        [], "middle", 1, 2_000_000,
    )(x, own, got, vec)


def after_kernel(own_ref, core_ref, got_ref, res_ref, cot_ref, vec_ref, dres_ref, dbr_ref, vg_ref):
    cot = cot_ref[...].astype(F32)
    unit, inverse = unit_rows(res_ref[...])
    dn = own_ref[...] + core_ref[0].astype(F32) + got_ref[...].astype(F32)
    dres = cot + norm_back(dn, unit, inverse, vec_ref[3:4])
    dbr = dres.astype(BF)
    dres_ref[...] = dres
    dbr_ref[...] = dbr
    sums = [dbr.astype(F32), dn * unit, dn, cot]
    for i, v in enumerate(sums):
        vg_ref[i : i + 1] = jnp.sum(v, axis=0, keepdims=True)
    vg_ref[4:8] = jnp.zeros((4, D), F32)


def after(own, core, got, res, cot, vec):
    one = full(ROWS, D)
    return grid_call(
        after_kernel, 1, [one, full(2, ROWS, D), one, one, one, full(16, D)], [one, one, full(8, D)],
        [like(ROWS, D, dtype=F32), like(ROWS, D), like(8, D, dtype=F32)], [], "after", 2, 3_000_000,
    )(own, core, got, *pinned(res), cot, vec)


def branch_bwd_kernel(att_ref, own_ref, other_ref, rows_ref, grads_in, datt_ref, grads_ref, wbuf, gbuf, sem):
    copies = out_copies(rows_ref, wbuf, sem)
    for copy in copies:
        copy.start()
    d = jnp.concatenate([own_ref[...], other_ref[...]], axis=0)
    gbuf[...] = nn(att_ref[...], d).astype(BF)
    backs = [
        pltpu.make_async_copy(gbuf.at[pl.ds(48 * k, 48)], grads_ref.at[k, pl.ds(0, 48)], sem.at[8 + k]) for k in range(8)
    ]
    for back in backs:
        back.start()
    for copy in copies:
        copy.wait()
    datt_ref[...] = nt(wbuf[...], d).astype(BF)
    for back in backs:
        back.wait()


def branch_bwd(att, own, other, rows_full, grads):
    return pl.pallas_call(
        branch_bwd_kernel,
        grid=(1,),
        in_specs=[full(8 * HD, 2 * ROWS), full(ROWS, D), full(ROWS, D), HBM, HBM],
        out_specs=[full(8 * HD, 2 * ROWS), HBM],
        out_shape=[like(8 * HD, 2 * ROWS), in_hbm(8, BLOCK, D)],
        scratch_shapes=[pltpu.VMEM((8 * HD, D), BF), pltpu.VMEM((8 * HD, D), BF), pltpu.SemaphoreType.DMA((16,))],
        input_output_aliases={4: 1},
        compiler_params=params(8),
        cost_estimate=cost(3, 3_000_000),
        name="branch_bwd",
    )(att, own, other, *pinned(rows_full, grads))


TILE = 256
UNITS = FF // 4
STEPS = UNITS // TILE
FOUR = 4 * ROWS


def unit_rule():
    row = iota((D // 2, 1), 0)
    first = row // 24 * 48 + lax.rem(row, 24) // 6 * 12 + lax.rem(row, 3) * 4
    mine = lax.rem(row, 6) // 3 == lax.axis_index("yh")
    keep = jnp.where(mine, first // 4, -1) == iota((D // 2, UNITS), 1) // 4
    pick = (iota((16, UNITS), 0) == 8 + iota((16, UNITS), 1) % 4).astype(F32)
    return keep, pick


def unit_bias_kernel(small_ref, out_ref):
    keep, pick = unit_rule()
    half = pl.ds(pl.multiple_of(lax.axis_index("c") * (D // 2), 8), D // 2)
    out_ref[...] = jnp.sum(jnp.where(keep, nn(small_ref[half, :], pick), 0.0), axis=0, keepdims=True)


def unit_bias(small):
    return grid_call(
        unit_bias_kernel, 1, [full(D, 16)], full(1, UNITS), like(1, UNITS, dtype=F32), [], "unit_bias", 1, 500_000
    )(small)


def unit_bias_grad_kernel(total_ref, out_ref):
    keep, pick = unit_rule()
    out_ref[...] = nt(jnp.where(keep, jnp.broadcast_to(total_ref[...], keep.shape), 0.0), pick)


def unit_bias_grad(total):
    return grid_call(
        unit_bias_grad_kernel, 1, [full(1, UNITS)], full(D // 2, 16), like(D // 2, 16, dtype=F32), [],
        "unit_bias_grad", 1, 500_000,
    )(total)


def mlp_kernel(*refs):
    rows, cots = refs[:4], refs[4:8]
    (bias_ref, w_ref, oself, ocore, oline, dself, dcore, dline, g_ref, total_ref,
     nbuf, cbuf, up_ref, down_ref, gdbuf, gubuf, out, sems, in_sems) = refs[8:]
    j = pl.program_id(0)

    def weights(step):
        lanes, copies = pl.ds(step * TILE, TILE), []
        for z in range(8):
            for y in range(2):
                source = w_ref.at[z, pl.ds(144 + y * 48, 48), lanes]
                copies.append((source, up_ref.at[pl.ds(y * 384 + z * 48, 48), lanes]))
        for p in range(step * 8, step * 8 + 8):
            copies.append((w_ref.at[p // 3, pl.ds(48 + p % 3 * 32, 32)], down_ref.at[pl.ds(32 * p, 32)]))
        return [pltpu.make_async_copy(a, b, in_sems.at[24 * step + i]) for i, (a, b) in enumerate(copies)]

    @pl.when(j == 0)
    def _():
        for step in range(STEPS):
            for copy in weights(step):
                copy.start()
        for i in range(4):
            nbuf[i * ROWS : (i + 1) * ROWS] = rows[i][...]
            cbuf[i * ROWS : (i + 1) * ROWS] = cots[i][...]

    for step in range(STEPS):

        @pl.when(j == step)
        def _(step=step):
            for copy in weights(step):
                copy.wait()

    spot = pl.ds(pl.multiple_of(j * TILE, TILE), TILE)
    wu, wd = up_ref[:, spot], down_ref[spot, :]
    up = nn(nbuf[...], wu) + bias_ref[...]
    cdf = 0.5 * (1.0 + lax.erf(up * 2.0 ** (-0.5)))
    hidden = (up * cdf).astype(BF)
    dh = nt(cbuf[...], wd).astype(BF).astype(F32)
    slope = cdf + up * jnp.exp(-0.5 * up * up) * (2.0 * math.pi) ** (-0.5)
    d_up = (dh * slope).astype(BF)
    total_ref[...] = jnp.sum(d_up.astype(F32), axis=0, keepdims=True)
    gdbuf[spot, :] = tn(hidden, cbuf[...]).astype(BF)
    gu = tn(nbuf[...], d_up).astype(BF)
    for z in range(8):
        for y in range(2):
            gubuf[z, y * 48 : y * 48 + 48, spot] = gu[y * 384 + z * 48 : y * 384 + z * 48 + 48]

    def backs(step):
        copies = [
            pltpu.make_async_copy(
                gdbuf.at[pl.ds(32 * p, 32)], g_ref.at[p // 3, pl.ds(48 + p % 3 * 32, 32)], sems.at[p]
            )
            for p in range(step * 8, step * 8 + 8)
        ]
        lanes = pl.ds(step * TILE, TILE)
        target = g_ref.at[:, pl.ds(144, 96), lanes]
        return copies + [pltpu.make_async_copy(gubuf.at[:, :, lanes], target, sems.at[24 + step])]

    for step in range(STEPS):

        @pl.when(j == step)
        def _(step=step):
            for back in backs(step):
                back.start()

    out_part = nn(hidden, wd)
    dn_part = nt(d_up, wu)

    @pl.when(j == 0)
    def _():
        out[0] = out_part
        out[1] = dn_part

    @pl.when((j > 0) & (j < STEPS - 1))
    def _():
        out[0] += out_part
        out[1] += dn_part

    @pl.when(j == STEPS - 1)
    def _():
        for i, (own, core, line, part) in enumerate(
            ((oself, ocore, oline, out_part), (dself, dcore, dline, dn_part))
        ):
            whole = out[i] + part
            own[...] = whole[:ROWS]
            core[0] = whole[ROWS : 2 * ROWS].astype(BF)
            line[...] = whole[2 * ROWS : 3 * ROWS]
            core[1] = whole[3 * ROWS :].astype(BF)
        for step in range(STEPS):
            for back in backs(step):
                back.wait()


def mlp(rows, cots, bias, rows_full):
    one, two = full(ROWS, D), full(2, ROWS, D)
    parts = [like(ROWS, D, dtype=F32), like(2, ROWS, D), like(ROWS, D, dtype=F32)]
    cut = pl.BlockSpec((1, TILE), lambda j: (0, j))
    return grid_call(
        mlp_kernel,
        STEPS,
        [one] * 8 + [cut, HBM],
        [one, two, one] * 2 + [HBM, cut],
        parts * 2 + [in_hbm(8, BLOCK, D), like(1, UNITS, dtype=F32)],
        [
            pltpu.VMEM((FOUR, D), BF),
            pltpu.VMEM((FOUR, D), BF),
            pltpu.VMEM((D, UNITS), BF),
            pltpu.VMEM((UNITS, D), BF),
            pltpu.VMEM((UNITS, D), BF),
            pltpu.VMEM((8, 96, UNITS), BF),
            pltpu.VMEM((2, FOUR, D), F32),
            pltpu.SemaphoreType.DMA((24 + STEPS,)),
            pltpu.SemaphoreType.DMA((24 * STEPS,)),
        ],
        "mlp",
        8,
        8_000_000,
        28,
    )(*rows, *cots, bias, *pinned(rows_full))


def join_kernel(own_ref, got_ref, pair, left, right, far0, far1):
    for k, ref in enumerate((pair, left, right)):
        ref[...] = (own_ref[k].astype(F32) + got_ref[k].astype(F32)).astype(BF)
    far = (own_ref[3].astype(F32) + got_ref[3].astype(F32)).astype(BF)
    far0[...] = far[:ROWS]
    far1[...] = far[ROWS:]


def join(own, got):
    pieces = [(BLK, D)] * 3 + [(ROWS, D)] * 2
    return grid_call(
        join_kernel, 1, [full(4, BLK, D)] * 2, [full(*p) for p in pieces], [in_hbm(*p) for p in pieces],
        [], "join", 1, 5_000_000, 16,
    )(*pinned(own, got))


def deal_kernel(got_ref, sum_ref, out_ref, buf, line):
    total = got_ref[0].astype(F32)
    for z in range(1, 8):
        total = total + got_ref[z].astype(F32)
    line[...] = total
    buf[...] = jnp.zeros(buf.shape, F32)
    for b in range(8):
        for c in range(2):
            k = c * 8 + b
            buf[c * 15 : c * 15 + 3] = sum_ref[3 * k : 3 * k + 3].astype(F32)
            at = 48 + (c * 4 + b // 2) * 12
            down = sum_ref[at : at + 12].astype(F32)
            buf[c * 15 + 3 : c * 15 + 15] = jnp.where(lax.axis_index("yh") == b % 2, down, 0.0)
            for y in range(2):
                at, row = 144 + y * 48 + 3 * k, 30 + (y * 2 + c) * 3
                buf[row : row + 3] = sum_ref[at : at + 3].astype(F32)
        buf[42:45] = line[3 * b : 3 * b + 3]
        out_ref[b] = buf[...].astype(BF)


def deal(got, sums):
    return grid_call(
        deal_kernel, 1, [full(8, LINE, D), full(BLOCK, D)], full(8, SENT, D), like(8, SENT, D),
        [pltpu.VMEM((SENT, D), F32), pltpu.VMEM((LINE, D), F32)], "deal", 2, 2_000_000,
    )(got, *pinned(sums))


def share_kernel(got_ref, own_ref, core_ref, line_ref, both_ref, buf, tot):
    core0, yl0 = lax.axis_index("c") == 0, lax.axis_index("yl") == 0
    parts = [got_ref[b].astype(F32) for b in range(8)]
    for y in range(2):
        total = parts[y]
        for b in range(2 + y, 8, 2):
            total = total + parts[b]
        tot[y] = total
    both_units = tot[0] + tot[1]
    buf[...] = jnp.zeros(buf.shape, F32)
    for g in range(4):
        c = g % 2
        buf[g, 0:15] = both_units[c * 15 : c * 15 + 15]
        for y in range(2):
            buf[g, 15 + 3 * y : 18 + 3 * y] = tot[y, 30 + 3 * g : 33 + 3 * g]
        for b in range(8):
            row, lane = 21 + 3 * (b // 4), (b % 4) * WIN
            buf[g, row : row + 3, lane : lane + WIN] = parts[b][42:45, g * WIN : (g + 1) * WIN]
        buf[g, 21:24, SMALL : SMALL + 16] = both_units[42:45, g * WIN + SMALL : g * WIN + SMALL + 16]
    groups = groups_of(*(buf[g] for g in range(4)), core0, yl0)
    own_ref[...] = groups[0]
    core_ref[...] = groups[1].astype(BF)
    line_ref[...] = groups[2].astype(BF)
    both_ref[...] = groups[3].astype(BF)


def share(got):
    one = full(PACK, D)
    return grid_call(
        share_kernel, 1, [full(8, SENT, D)], [one] * 4, [like(PACK, D, dtype=F32)] + [like(PACK, D)] * 3,
        [pltpu.VMEM((4, PACK, D), F32), pltpu.VMEM((2, SENT, D), F32)], "share", 2, 2_000_000,
    )(got)


def finish_kernel(own_ref, core_ref, line_ref, both_ref, wq_ref, wu_ref, wo_ref, wd_ref, *refs):
    vectors, (buf, qbuf, cbuf) = refs[:8], refs[8:]
    core0 = lax.axis_index("c") == 0
    aligned = lax.axis_index("c") == lax.axis_index("yl")
    own, core, line, both = (r[...].astype(F32) for r in (own_ref, core_ref, line_ref, both_ref))
    cbuf[...] = jnp.zeros(cbuf.shape, F32)
    buf[0] = jnp.where(aligned, own + line, core + both)
    wo_ref[...] = buf[0, 0:3]
    wd_ref[...] = buf[0, 3:15]
    mine, theirs = own + line, core + both
    buf[0] = jnp.where(core0, mine, theirs)
    buf[1] = jnp.where(core0, theirs, mine)
    for k in range(2):
        for q in range(2):
            to = slice(q * (D // 2), (q + 1) * (D // 2))
            at = 8 * (2 * k + q)
            for y in range(2):
                cbuf[at : at + 3, y * (D // 2) : (y + 1) * (D // 2)] = buf[k, 15 + 3 * y : 18 + 3 * y, to]
        for b in range(8):
            row, lane, at = 21 + 3 * (b // 4), (b % 4) * WIN, (k * 8 + b) * HD
            for p in range(3):
                qbuf[0:3, p * D + at : p * D + at + HD] = buf[k, row : row + 3, lane + p * HD : lane + (p + 1) * HD]
    wq_ref[...] = qbuf[0:3]
    rest = cbuf[...]
    parts = []
    for _ in range(3):
        parts.append(rest.astype(BF))
        rest = rest - parts[-1].astype(F32)
    sums = nt(jnp.concatenate(parts, axis=0), unit_order())
    total = sums[0:32] + sums[32:64] + sums[64:96]
    for i in range(4):
        wu_ref[:, i * D : (i + 1) * D] = total[8 * i : 8 * i + 3]
    small = (buf[0] + buf[1])[21:24, SMALL : SMALL + 16]

    def row_of(first, stride, count):
        shape = (3, count)
        keep = iota(shape, 1) // stride == iota(shape, 0)
        total = jnp.zeros((1, count), F32)
        for k in range(stride):
            values = jnp.broadcast_to(small[:, first + k : first + k + 1], shape)
            total += jnp.sum(jnp.where(keep & (iota(shape, 1) % stride == k), values, 0.0), axis=0, keepdims=True)
        return total.reshape(count)

    for i in range(6):
        vectors[i][...] = row_of(i, 1, 3)
    vectors[6][...] = row_of(6, 2, 6)
    vectors[7][...] = row_of(8, 4, 12)


def finish(parts):
    shapes = [(3, 3 * D), (3, FF), (3, D), (12, D)] + [(3,)] * 6 + [(6,), (12,)]
    return grid_call(
        finish_kernel, 1, [full(PACK, D)] * 4, [full(*s) for s in shapes], [like(*s, dtype=F32) for s in shapes],
        [pltpu.VMEM((2, PACK, D), F32), pltpu.VMEM((8, 3 * D), F32), pltpu.VMEM((32, D), F32)], "finish", 2, 1_000_000,
    )(*parts)


AXES = ("yl", "z", "c", "x", "yh")
SEQ = ("yl", "z", "c")
BAND = ("x", "yh")
SWAP = [(0, 1), (1, 0)]
RIGHT = [(i, (i + 1) % 4) for i in range(4)]
LEFT = [(i, (i + 3) % 4) for i in range(4)]


def swap_core(v):
    return lax.ppermute(v, "c", SWAP)


def swap_yl(v):
    return lax.ppermute(v, "yl", SWAP)


def swap_yh(v):
    return lax.ppermute(v, "yh", SWAP)


def swap_both(v):
    return lax.ppermute(v, ("yl", "c"), [(0, 3), (1, 2), (2, 1), (3, 0)])


def four_rows(v):
    line = swap_yh(v)
    return v, swap_core(v), line, swap_core(line)


def exchange(v, axes):
    return lax.all_to_all(v, axes, 0, 0, tiled=True)


def ring_far(far0, far1):
    return lax.ppermute(far0, "x", RIGHT), lax.ppermute(far1, "x", LEFT)


def ring_add_kernel(left_ref, right_ref, from_left, from_right, left_out, right_out):
    left_out[0:ROWS] = left_ref[0:ROWS]
    left_out[ROWS:] = (left_ref[ROWS:].astype(F32) + from_right[...].astype(F32)).astype(BF)
    right_out[0:ROWS] = (right_ref[0:ROWS].astype(F32) + from_left[...].astype(F32)).astype(BF)
    right_out[ROWS:] = right_ref[ROWS:]


def ring_add(left, right, from_left, from_right):
    two, one = full(BLK, D), full(ROWS, D)
    return grid_call(
        ring_add_kernel, 1, [two, two, one, one], [two, two], [in_hbm(BLK, D)] * 2, [], "ring_add", 1, 2_000_000
    )(*pinned(left, right), from_left, from_right)


def settle_kernel(pair_ref, left_ref, right_ref, keep_ref, give_ref):
    first = lax.axis_index("yh") == 0
    total = pair_ref[...].astype(F32) + left_ref[...].astype(F32) + right_ref[...].astype(F32)
    keep_ref[...] = jnp.where(first, total[:ROWS], total[ROWS:])
    give_ref[...] = jnp.where(first, total[ROWS:], total[:ROWS]).astype(BF)


def settle(pair, left, right):
    two, one = full(BLK, D), full(ROWS, D)
    return grid_call(
        settle_kernel, 1, [two, two, two], [one, one], [like(ROWS, D, dtype=F32), like(ROWS, D)], [],
        "settle", 1, 2_000_000,
    )(*pinned(pair), left, right)


def tokens_kernel(keep_ref, got_ref, res_ref, unit_ref, inv_ref, vec_ref, out_ref):
    d = keep_ref[...] + got_ref[...].astype(F32)
    out_ref[...] = (res_ref[...] + norm_back(d, unit_ref[...], inv_ref[...], vec_ref[0:1])).astype(BF)


def tokens_grad(keep, got, res, unit, inverse, vec):
    one = full(ROWS, D)
    return grid_call(
        tokens_kernel, 1, [one, one, one, one, full(ROWS, 1), full(16, D)], one, like(ROWS, D), [],
        "tokens_grad", 1, 2_000_000,
    )(keep, got, res, unit, inverse, vec)


def per_device(
    tokens, image_ids, ln1_gain, ln1_bias, w_qkv, qv_bias, w_out, out_bias,
    ln2_gain, ln2_bias, w_up, up_bias, w_down, down_bias, cotangent,
):
    first = lax.axis_index("yh") == 0
    x = tokens[0]
    cot = cotangent[0]

    pack_own, pack_other, unit, unit1, inv1 = prep(
        w_qkv, w_up, w_out, w_down, (ln1_gain, ln1_bias, out_bias, ln2_gain, ln2_bias, down_bias, qv_bias, up_bias),
        image_ids, x,
    )
    sent = spread((pack_own, swap_core(pack_other), swap_yl(pack_own), swap_both(pack_other)))
    got_yh = swap_yh(unit)
    pair = jnp.stack([jnp.where(first, unit, got_yh), jnp.where(first, got_yh, unit)])
    got, pair = lax.optimization_barrier((exchange(sent, BAND), pair))
    left = lax.ppermute(pair, "x", RIGHT)
    right = lax.ppermute(pair, "x", LEFT)
    block, line = collect(got)
    rows_full = lax.all_gather(block, "z", axis=0)
    far0 = lax.ppermute(left[0], "x", RIGHT)
    far1 = lax.ppermute(right[1], "x", LEFT)
    line_got = exchange(line, "z")
    token_pieces = (pair.reshape(BLK, D), left.reshape(BLK, D), right.reshape(BLK, D), far0, far1)
    other_pieces = tuple(swap_core(v) for v in token_pieces)
    cot_after, _ = lax.optimization_barrier((cot, far0))
    cots = four_rows(cot_after)

    qkv, att, wide, lse, w_t, vec, small = attend_fwd(token_pieces + other_pieces, line_got)
    att, *cots = lax.optimization_barrier((att, *cots))
    att_c = exchange(att, BAND).reshape(8 * HD, 2 * ROWS)
    branch_own, branch_send = branch(att_c, rows_full)
    residual, n2 = middle(x, branch_own, swap_core(branch_send), vec)

    rows = four_rows(n2)
    o_self, o_core, o_line, d_self, d_core, d_line, grads, utotal = mlp(rows, cots, unit_bias(small), rows_full)
    d_core = swap_core(d_core)
    d_line = swap_yh((d_line + d_core[1].astype(F32)).astype(BF))
    d_res, d_branch, vgrads = after(d_self, d_core, d_line, residual, cot, vec)
    d_att, grads = branch_bwd(att_c, d_branch, swap_core(d_branch), rows_full, grads)
    grad_sum = lax.psum_scatter(grads, "z", scatter_dimension=0, tiled=True).reshape(BLOCK, D)
    d_att_all = exchange(d_att.reshape(8, HD, 2 * ROWS), BAND)
    o_core = swap_core(o_core)
    o_line = (o_line + o_core[1].astype(F32)).astype(BF)
    d_att_all, o_line, utotal = lax.optimization_barrier((d_att_all, o_line, utotal))

    d_own, d_other, line_grad = attend_bwd(
        token_pieces + other_pieces, qkv, lse, wide, d_att_all, w_t, small, vec, vgrads, unit_bias_grad(utotal)
    )
    line_sum = exchange(line_grad, "z")
    d_pair, d_left, d_right, d_far0, d_far1 = join(d_own, swap_core(d_other))
    d_left, d_right = ring_add(d_left, d_right, *ring_far(d_far0, d_far1))
    line_sum, d_left, d_right, o_line = lax.optimization_barrier((line_sum, d_left, d_right, swap_yh(o_line)))
    from_left, from_right = lax.ppermute(d_right, "x", RIGHT), lax.ppermute(d_left, "x", LEFT)
    keep, give = settle(d_pair, from_left, from_right)
    last, give = lax.optimization_barrier((exchange(deal(line_sum, grad_sum), BAND), swap_yh(give)))
    d_tokens = tokens_grad(keep, give, d_res, unit1, inv1, vec)

    own, to_core, to_yl, to_both = share(last)
    done = finish((own, swap_core(to_core), swap_yl(to_yl), swap_both(to_both)))
    g_qkv, g_up, g_out, g_down, l1g, l1b, ob, l2g, l2b, db, qvb, upb = done
    output = residual + o_self + o_core[0].astype(F32) + o_line.astype(F32) + vec[5:6]
    return (
        output.astype(BF)[None], d_tokens[None], l1g, l1b, g_qkv, qvb, g_out, ob, l2g, l2b, g_up, upb, g_down, db,
    )


def solution(mesh):
    fine = Mesh(mesh.devices.reshape(2, 8, 2, 4, 2), AXES)
    seq_band = P(SEQ, BAND, None)
    flat, flat2 = P(AXES), P(AXES, None)
    in_specs = (
        seq_band, P(SEQ, BAND), flat, flat, flat2, flat, flat2, flat,
        flat, flat, flat2, flat, flat2, flat, seq_band,
    )
    out_specs = (
        seq_band, seq_band, flat, flat, flat2, flat, flat2, flat,
        flat, flat, flat2, flat, flat2, flat,
    )
    return jax.shard_map(per_device, mesh=fine, in_specs=in_specs, out_specs=out_specs, check_vma=False)
```

```python
import math

import jax
import jax.numpy as jnp
from jax import lax
from jax.experimental import pallas as pl
from jax.experimental.pallas import tpu as pltpu
from jax.sharding import Mesh, PartitionSpec as P

D = 768
HEADS = 16
HD = 48
FF = 3072
LEN = 1024
ROWS = 128
BLK = 256
HALF = FF // 2
EPS = 1e-05
SCALE = HD ** (-0.5)
BF = jnp.bfloat16
F32 = jnp.float32
HBM = pl.BlockSpec(memory_space=pltpu.HBM)


def nn(a, b):
    return lax.dot_general(a, b, (((1,), (0,)), ((), ())), preferred_element_type=F32)


def nt(a, b):
    return lax.dot_general(a, b, (((1,), (1,)), ((), ())), preferred_element_type=F32)


def tn(a, b):
    return lax.dot_general(a, b, (((0,), (0,)), ((), ())), preferred_element_type=F32)


def turned(a):
    return a.astype(F32).T.astype(BF)


def params(mebi):
    return pltpu.CompilerParams(vmem_limit_bytes=mebi << 20)


def cost(micros, size):
    return pl.CostEstimate(flops=1000, bytes_accessed=1000, transcendentals=0)


def grid_call(kernel, steps, ins, outs, out_shape, scratch, name, micros, size, mebi=8):
    return pl.pallas_call(
        kernel,
        grid=(steps,),
        in_specs=ins,
        out_specs=outs,
        out_shape=out_shape,
        scratch_shapes=scratch,
        compiler_params=params(mebi),
        cost_estimate=cost(micros, size),
        name=name,
    )


def pinned(*values):
    return tuple(pltpu.with_memory_space_constraint(v, pltpu.HBM) for v in values)


def in_hbm(*shape, dtype=BF):
    return pltpu.HBM(shape, dtype)


def full(*shape):
    return pl.BlockSpec(shape, lambda i: (0,) * len(shape))


def step_block(*shape):
    return pl.BlockSpec((None,) + shape, lambda i: (i,) + (0,) * len(shape))


def iota(shape, axis):
    return lax.broadcasted_iota(jnp.int32, shape, axis)


def like(*shape, dtype=BF):
    return jax.ShapeDtypeStruct(shape, dtype)


WIN = 192
SMALL = 3 * HD
PACK = 32


def unit_order():
    source = iota((D, 1), 0)
    part = lax.rem(source, 24)
    target = part // 12 * (D // 2) + source // 96 * 48 + lax.rem(source, 96) // 24 * 12 + lax.rem(part, 12)
    return (target == iota((D, D), 1)).astype(F32).astype(BF)


def prep_kernel(*refs):
    sources, (own_ref, other_ref, unit_ref, wide_ref, inv_ref), held, (buf, cbuf, sems) = refs[:14], refs[14:19], refs[19:33], refs[33:]
    copies = [pltpu.make_async_copy(a, b, sems.at[i]) for i, (a, b) in enumerate(zip(sources, held))]
    for copy in copies:
        copy.start()
    buf[...] = jnp.zeros(buf.shape, F32)
    cbuf[...] = jnp.zeros(cbuf.shape, F32)
    order = unit_order()
    copies[13].wait()
    unit, inverse = unit_rows(held[13][...].astype(F32))
    unit_ref[...] = unit.astype(BF)
    wide_ref[...] = unit
    inv_ref[...] = inverse
    for copy in copies[:13]:
        copy.wait()
    wq_ref, wu_ref, wo_ref, wd_ref = held[:4]
    vectors, ids_ref = held[4:12], held[12]

    def column(ref, stride, k):
        row = ref[...].astype(F32).reshape(1, ref.shape[0])
        shape = (3, ref.shape[0])
        keep = iota(shape, 1) == iota(shape, 0) * stride + k
        return jnp.sum(jnp.where(keep, jnp.broadcast_to(row, shape), 0.0), axis=1, keepdims=True)

    columns = [column(ref, 1, 0) for ref in vectors[:6]]
    columns += [column(vectors[6], 2, k) for k in range(2)]
    columns += [column(vectors[7], 4, k) for k in range(4)]
    mark = jnp.max(ids_ref[...].astype(F32), axis=1, keepdims=True)
    columns.append(jnp.broadcast_to(mark, (3, 1)))
    lanes = iota((3, 128), 1)
    small = jnp.zeros((3, 128), F32)
    for j, col in enumerate(columns):
        small = jnp.where(lanes == j, jnp.broadcast_to(col, (3, 128)), small)
    wq = wq_ref[...].astype(F32)
    for i in range(4):
        cbuf[8 * i : 8 * i + 3] = wu_ref[:, i * D : (i + 1) * D].astype(F32)
    chosen = nn(cbuf[...].astype(BF), order)
    for k in range(2):
        buf[k, 0:3] = wo_ref[...].astype(F32)
        buf[k, 3:15] = wd_ref[...].astype(F32)
        for q in range(2):
            at = 8 * (2 * k + q)
            for y in range(2):
                to = slice(q * (D // 2), (q + 1) * (D // 2))
                buf[k, 15 + 3 * y : 18 + 3 * y, to] = chosen[at : at + 3, y * (D // 2) : (y + 1) * (D // 2)]
        for b in range(8):
            row, lane, at = 21 + 3 * (b // 4), (b % 4) * WIN, (k * 8 + b) * HD
            for p in range(3):
                buf[k, row : row + 3, lane + p * HD : lane + (p + 1) * HD] = wq[:, p * D + at : p * D + at + HD]
            buf[k, row : row + 3, lane + SMALL : lane + SMALL + 16] = small[:, :16]
    core0 = lax.axis_index("c") == 0
    own_ref[...] = jnp.where(core0, buf[0], buf[1]).astype(BF)
    other_ref[...] = jnp.where(core0, buf[1], buf[0]).astype(BF)


def prep(w_qkv, w_up, w_out, w_down, vectors, ids, x):
    args = (w_qkv, w_up, w_out, w_down) + vectors + (ids, x)
    return grid_call(
        prep_kernel, 1, [HBM] * len(args), [full(PACK, D)] * 2 + [full(ROWS, D)] * 2 + [full(ROWS, 1)],
        [like(PACK, D)] * 2 + [like(ROWS, D), in_hbm(ROWS, D, dtype=F32), in_hbm(ROWS, 1, dtype=F32)],
        [pltpu.VMEM(a.shape, a.dtype) for a in args]
        + [pltpu.VMEM((2, PACK, D), F32), pltpu.VMEM((32, D), F32), pltpu.SemaphoreType.DMA((len(args),))],
        "prep", 2, 100_000,
    )(*pinned(*args))


def groups_of(own, core, line, both, core0, yl0):
    def pick(a, b, c, d):
        return jnp.where(yl0, jnp.where(core0, a, b), jnp.where(core0, c, d))

    return (
        pick(own, core, line, both),
        pick(core, own, both, line),
        pick(line, both, own, core),
        pick(both, line, core, own),
    )


SENT = 48


def spread_kernel(own_ref, core_ref, line_ref, both_ref, out_ref, buf):
    core0, yl0 = lax.axis_index("c") == 0, lax.axis_index("yl") == 0
    aligned = lax.axis_index("c") == lax.axis_index("yl")
    own, core, line, both = (r[...].astype(F32) for r in (own_ref, core_ref, line_ref, both_ref))
    same, cross = jnp.where(aligned, own, line), jnp.where(aligned, core, both)
    buf[...] = jnp.zeros(buf.shape, F32)
    buf[0:15] = jnp.where(core0, same, cross)[0:15]
    buf[15:30] = jnp.where(core0, cross, same)[0:15]
    groups = groups_of(own, core, line, both, core0, yl0)
    for b in range(8):
        y, row, lane = b % 2, 21 + 3 * (b // 4), (b % 4) * WIN
        for g in range(4):
            buf[30 + 3 * g : 33 + 3 * g] = groups[g][15 + 3 * y : 18 + 3 * y]
            buf[42:45, g * WIN : (g + 1) * WIN] = groups[g][row : row + 3, lane : lane + WIN]
        out_ref[b] = buf[...].astype(BF)


def spread(packs):
    return grid_call(
        spread_kernel, 1, [full(PACK, D)] * 4, full(8, SENT, D), like(8, SENT, D),
        [pltpu.VMEM((SENT, D), F32)], "spread", 1, 1_000_000,
    )(*packs)


BLOCK = 240
LINE = 24


def collect_kernel(got_ref, blk_ref, line_ref, buf, lbuf):
    yh = lax.axis_index("yh")
    for b in range(8):
        got = got_ref[b].astype(F32)
        for c in range(2):
            k = c * 8 + b
            buf[3 * k : 3 * k + 3] = got[c * 15 : c * 15 + 3]
            for y in range(2):
                at, row = 144 + y * 48 + 3 * k, 30 + (y * 2 + c) * 3
                buf[at : at + 3] = got[row : row + 3]
        lbuf[3 * b : 3 * b + 3] = got[42:45]
    for x in range(4):
        got = got_ref[2 * x + yh].astype(F32)
        for c in range(2):
            at = 48 + (c * 4 + x) * 12
            buf[at : at + 12] = got[c * 15 + 3 : c * 15 + 15]
    line = lbuf[...].astype(BF)
    for z in range(8):
        line_ref[z] = line
    blk_ref[...] = buf[...].astype(BF)


def collect(got):
    return grid_call(
        collect_kernel, 1, [full(8, SENT, D)], [full(BLOCK, D), full(8, LINE, D)], [in_hbm(BLOCK, D), like(8, LINE, D)],
        [pltpu.VMEM((BLOCK, D), F32), pltpu.VMEM((LINE, D), F32)], "collect", 2, 2_000_000,
    )(got)


def place_of(step):
    return lax.rem(lax.axis_index("x") + step, 4)


RING = (0, 3, 1, 2)


def head_index():
    return lax.axis_index("c") * 8 + lax.axis_index("x") * 2 + lax.axis_index("yh")


def group_rows(group):
    return pl.ds(pl.multiple_of(group * 24, 8), 24)


def pair_groups():
    at = (lax.axis_index("yl") * 8 + lax.axis_index("z")) * 2
    c = lax.axis_index("c")
    return at + c, at + 1 - c


def several_images(small_ref, seq):
    own, other = pair_groups()
    block = small_ref[group_rows(jnp.where(seq == 0, own, other)), :]
    marks = jnp.where(iota(block.shape, 1) == 12, block, 0.0)
    return jnp.max(marks) > 0.5


def piece_cols(k):
    return pl.ds(pl.multiple_of(place_of(RING[k]) * BLK, BLK), BLK)


def piece_copies(pieces, target, sems, s):
    at, copies = 0, []
    for i, piece in enumerate(pieces[5 * s : 5 * s + 5]):
        rows = piece.shape[0]
        copies.append(pltpu.make_async_copy(piece, target.at[s, pl.ds(at, rows)], sems.at[5 * s + i]))
        at += rows
    return copies


def attend_fwd_kernel(*refs):
    pieces = refs[:10]
    (line_ref, qkv_hbm, att_ref, wide_hbm, lse_hbm, wt_hbm, vec_ref, small_ref,
     xbuf, qkv_ref, wide_ref, lse_ref, wt_ref, keys_buf, wbuf, bias, sems) = refs[10:]
    seq = pl.program_id(0)

    def outgoing(s):
        return (
            pltpu.make_async_copy(qkv_ref.at[s], qkv_hbm.at[s], sems.at[10 + 3 * s]),
            pltpu.make_async_copy(wide_ref.at[s], wide_hbm.at[s], sems.at[11 + 3 * s]),
            pltpu.make_async_copy(lse_ref.at[s], lse_hbm.at[s], sems.at[12 + 3 * s]),
        )

    @pl.when(seq == 0)
    def _():
        for s in range(2):
            for copy in piece_copies(pieces, xbuf, sems, s):
                copy.start()
        wbuf[...] = jnp.zeros(wbuf.shape, F32)
        for z in range(8):
            line = line_ref[z].astype(F32)
            for g in range(4):
                y, c = g // 2, g % 2
                at = (y * 8 + z) * 48 + c * 24
                wbuf[at : at + 24, 0:WIN] = line[:, g * WIN : (g + 1) * WIN]
        turned_w = wbuf[...].T
        wt_ref[...] = turned_w[:SMALL].astype(BF)
        pltpu.make_async_copy(wt_ref, wt_hbm, sems.at[16]).start()
        vec_ref[...] = turned_w[SMALL : SMALL + 16]
        small_ref[...] = wbuf[:, SMALL : SMALL + 16]
        head = head_index()
        expand = (iota((HD, 24), 0) // 2 == iota((HD, 24), 1)).astype(F32)
        lane = iota((HD, 16), 1) == 6 + iota((HD, 16), 0) % 2
        for part, group in ((0, head), (2, 16 + head)):
            spreads = nn(expand, small_ref[group_rows(group), :])
            col = jnp.sum(jnp.where(lane, spreads, 0.0), axis=1, keepdims=True)
            bias[part * HD : (part + 1) * HD] = col
        bias[HD : 2 * HD] = jnp.zeros((HD, 1), F32)

    gain, off = vec_ref[0:1], vec_ref[1:2]
    for s in range(2):

        @pl.when(seq == s)
        def _(s=s):
            for copy in piece_copies(pieces, xbuf, sems, s):
                copy.wait()

    for k in range(4):
        rows = xbuf[seq, k * BLK : (k + 1) * BLK]
        normed = (rows.astype(F32) * gain + off).astype(BF)
        qkv_ref[seq, :, piece_cols(k)] = (nt(wt_ref[...], normed) + bias[...]).astype(BF)
    for s in range(2):

        @pl.when(seq == s)
        def _(s=s):
            outgoing(s)[0].start()

    keys_buf[...] = turned(qkv_ref[seq, HD : 2 * HD, :])

    def block(qb, keys):
        cols = slice(qb * BLK, (qb + 1) * BLK)
        vt = qkv_ref[seq, 2 * HD : 3 * HD, keys]
        s = nn(keys_buf[keys, :], qkv_ref[seq, 0:HD, cols]) * SCALE
        peak = jnp.max(s, axis=0, keepdims=True)
        e = jnp.exp(s - peak)
        total = jnp.sum(e, axis=0, keepdims=True)
        lse_ref[seq, :, cols] = peak + jnp.log(total)
        out = nn(vt, e.astype(BF)) * (1.0 / total)
        wide_ref[seq, :, cols] = out
        out = out.astype(BF)
        low, high = out[:, :ROWS], out[:, ROWS:]
        att_ref[2 * qb, 0] = low
        att_ref[2 * qb, 1] = high
        att_ref[2 * qb + 1, 0] = high
        att_ref[2 * qb + 1, 1] = low

    several = several_images(small_ref, seq)

    @pl.when(jnp.logical_not(several))
    def _():
        for qb in range(LEN // BLK):
            block(qb, slice(0, LEN))

    @pl.when(several)
    def _():
        for qb in range(LEN // BLK):
            block(qb, slice(qb * BLK, (qb + 1) * BLK))

    for s in range(2):

        @pl.when(seq == s)
        def _(s=s):
            for copy in outgoing(s)[1:]:
                copy.start()

    @pl.when(seq == 1)
    def _():
        pltpu.make_async_copy(wt_ref, wt_hbm, sems.at[16]).wait()
        for s in range(2):
            for copy in outgoing(s):
                copy.wait()


def attend_fwd(pieces, line):
    return grid_call(
        attend_fwd_kernel,
        2,
        [HBM] * 10 + [full(8, LINE, D)],
        [HBM, pl.BlockSpec((8, 2, HD, ROWS), lambda i: (0, 0, 0, i)), HBM, HBM, HBM, full(16, D), full(D, 16)],
        [
            in_hbm(2, SMALL, LEN),
            like(8, 2, HD, 2 * ROWS),
            in_hbm(2, HD, LEN, dtype=F32),
            in_hbm(2, 1, LEN, dtype=F32),
            in_hbm(SMALL, D),
            like(16, D, dtype=F32),
            like(D, 16, dtype=F32),
        ],
        [
            pltpu.VMEM((2, LEN, D), BF),
            pltpu.VMEM((2, SMALL, LEN), BF),
            pltpu.VMEM((2, HD, LEN), F32),
            pltpu.VMEM((2, 1, LEN), F32),
            pltpu.VMEM((SMALL, D), BF),
            pltpu.VMEM((LEN, HD), BF),
            pltpu.VMEM((D, 256), F32),
            pltpu.VMEM((SMALL, 1), F32),
            pltpu.SemaphoreType.DMA((17,)),
        ],
        "attend_fwd",
        9,
        10_000_000,
        24,
    )(*pinned(*pieces), line)


def attend_bwd_kernel(*refs):
    pieces = refs[:10]
    (qkv_hbm, lse_hbm, wide_hbm, datt_ref, w_hbm, small_ref, vec_ref, vgrad_ref, ugrad_ref,
     down_hbm, dother_hbm, out_ref,
     ubuf, qkv_ref, lse_ref, wide_ref, w_ref, dbuf,
     rows_buf, values_buf, dq_buf, dkv_buf, fbuf, acc, acc_bias, gbuf, sems) = refs[10:]
    seq = pl.program_id(0)

    def first_in():
        pairs = ((qkv_hbm, qkv_ref), (lse_hbm, lse_ref), (wide_hbm, wide_ref))
        return [pltpu.make_async_copy(a, b, sems.at[10 + i]) for i, (a, b) in enumerate(pairs)]

    def w_in():
        return pltpu.make_async_copy(w_hbm, w_ref, sems.at[13])

    def out(s):
        return pltpu.make_async_copy(dbuf.at[s], (down_hbm, dother_hbm)[s], sems.at[14 + s])

    @pl.when(seq == 0)
    def _():
        for copy in first_in() + [w_in()]:
            copy.start()
        for s in range(2):
            for copy in piece_copies(pieces, ubuf, sems, s):
                copy.start()
        for copy in first_in():
            copy.wait()

    rows_buf[:, 0 : 3 * HD] = turned(qkv_ref[seq])
    d_out = jnp.concatenate([datt_ref[b] for b in range(8)], axis=1)
    values_buf[:, 0:HD] = turned(d_out)
    delta_all = jnp.sum(d_out.astype(F32) * wide_ref[seq], axis=0, keepdims=True)
    QS, KS = 256, 256

    def scores(qb, kb):
        cols = slice(qb * QS, (qb + 1) * QS)
        keys = slice(kb * KS, (kb + 1) * KS)
        qt = qkv_ref[seq, 0:HD, cols]
        dt = d_out[:, cols]
        probs = jnp.exp(nn(rows_buf[keys, HD : 2 * HD], qt) * SCALE - lse_ref[seq, :, cols])
        ds = (probs * (nn(rows_buf[keys, 2 * HD : 3 * HD], dt) - delta_all[:, cols])).astype(BF)
        return probs.astype(BF), ds

    def products(qb, kb, probs, ds, first_q, first_k):
        cols = slice(qb * QS, (qb + 1) * QS)
        keys = slice(kb * KS, (kb + 1) * KS)
        dq = nn(qkv_ref[seq, HD : 2 * HD, keys], ds)
        dk = nn(ds, rows_buf[cols, 0:HD])
        dv = nn(probs, values_buf[cols, 0:HD])
        if first_q:
            dq_buf[:, cols] = dq
        else:
            dq_buf[:, cols] += dq
        if first_k:
            dkv_buf[keys, 0:HD] = dk
            dkv_buf[keys, HD : 2 * HD] = dv
        else:
            dkv_buf[keys, 0:HD] += dk
            dkv_buf[keys, HD : 2 * HD] += dv

    def sweep(tiles):
        seen_q, seen_k, held = set(), set(), None
        for tile in tiles + [None]:
            now = (tile, scores(*tile)) if tile else None
            if held is not None:
                (qb, kb), (probs, ds) = held
                products(qb, kb, probs, ds, qb not in seen_q, kb not in seen_k)
                seen_q.add(qb)
                seen_k.add(kb)
            held = now

    several = several_images(small_ref, seq)

    @pl.when(jnp.logical_not(several))
    def _():
        sweep([(qb, kb) for qb in range(LEN // QS) for kb in range(LEN // KS)])

    @pl.when(several)
    def _():
        for b in range(4):
            cols = slice(b * BLK, (b + 1) * BLK)
            qt = qkv_ref[seq, 0:HD, cols]
            dt = d_out[:, cols]
            probs = jnp.exp(nn(rows_buf[cols, HD : 2 * HD], qt) * SCALE - lse_ref[seq, :, cols])
            ds = (probs * (nn(rows_buf[cols, 2 * HD : 3 * HD], dt) - delta_all[:, cols])).astype(BF)
            dq_buf[:, cols] = nn(qkv_ref[seq, HD : 2 * HD, cols], ds)
            dkv_buf[cols, 0:HD] = nn(ds, rows_buf[cols, 0:HD])
            dkv_buf[cols, HD : 2 * HD] = nn(probs.astype(BF), values_buf[cols, 0:HD])

    dkv = dkv_buf[...]
    by_row = jnp.concatenate(
        [dq_buf[...].T * SCALE, dkv[:, 0:HD] * SCALE, dkv[:, HD : 2 * HD]], axis=1
    ).astype(BF)
    by_feature = turned(by_row)

    rows_buf[:, 0 : 3 * HD] = by_row
    fbuf[...] = by_feature

    @pl.when(seq == 0)
    def _():
        w_in().wait()

    for k in range(4):
        dbuf[seq, k] = nn(rows_buf[piece_cols(k), 0 : 3 * HD], w_ref[...]).astype(BF)
    for s in range(2):

        @pl.when(seq == s)
        def _(s=s):
            out(s).start()
            for copy in piece_copies(pieces, ubuf, sems, s):
                copy.wait()

    gn = jnp.zeros((SMALL, D), F32)
    for k in range(4):
        gn = gn + nn(fbuf[:, piece_cols(k)], ubuf[seq, k * BLK : (k + 1) * BLK])
    gb = jnp.sum(by_feature.astype(F32), axis=1, keepdims=True)

    @pl.when(seq == 0)
    def _():
        acc[...] = gn
        acc_bias[...] = gb

    @pl.when(seq == 1)
    def _():
        w = w_ref[...].astype(F32)
        gb_all = acc_bias[...] + gb
        gn_all = acc[...] + gn
        rows = jnp.concatenate(
            [
                gn_all * vec_ref[0:1] + gb_all * vec_ref[1:2],
                jnp.sum(w * gn_all, axis=0, keepdims=True),
                jnp.sum(w * gb_all, axis=0, keepdims=True),
                vgrad_ref[0:4],
                jnp.zeros((256 - SMALL - 6, D), F32),
            ],
            axis=0,
        )
        gbuf[...] = rows.T
        head = head_index()
        fold = (iota((24, HD), 0) == iota((24, HD), 1) // 2).astype(F32)
        lane = iota((HD, 256), 1) == SMALL + 6 + iota((HD, 256), 0) % 2
        for part, group in ((0, head), (2, 16 + head)):
            spreads = jnp.where(lane, jnp.broadcast_to(gb_all[part * HD : (part + 1) * HD], (HD, 256)), 0.0)
            gbuf[group_rows(group), :] += nn(fold, spreads)
        half = pl.ds(pl.multiple_of(lax.axis_index("c") * (D // 2), 8), D // 2)
        gbuf[half, SMALL + 8 : SMALL + 12] = ugrad_ref[:, 8:12]
        for z in range(8):
            for g in range(4):
                y, c = g // 2, g % 2
                at = (y * 8 + z) * 48 + c * 24
                out_ref[z, :, g * WIN : (g + 1) * WIN] = gbuf[at : at + 24, 0:WIN].astype(BF)
        for s in range(2):
            out(s).wait()


def attend_bwd(pieces, qkv, lse, wide, datt, w_t, small, vec, vgrads, ugrads):
    return grid_call(
        attend_bwd_kernel,
        2,
        [HBM] * 13
        + [pl.BlockSpec((8, HD, ROWS), lambda i: (0, 0, i)), HBM, full(D, 16), full(16, D), full(8, D), full(D // 2, 16)],
        [HBM, HBM, full(8, LINE, D)],
        [in_hbm(4, BLK, D), in_hbm(4, BLK, D), like(8, LINE, D)],
        [
            pltpu.VMEM((2, LEN, D), BF),
            pltpu.VMEM((2, SMALL, LEN), BF),
            pltpu.VMEM((2, 1, LEN), F32),
            pltpu.VMEM((2, HD, LEN), F32),
            pltpu.VMEM((SMALL, D), BF),
            pltpu.VMEM((2, 4, BLK, D), BF),
            pltpu.VMEM((LEN, SMALL), BF),
            pltpu.VMEM((LEN, HD), BF),
            pltpu.VMEM((HD, LEN), F32),
            pltpu.VMEM((LEN, 2 * HD), F32),
            pltpu.VMEM((SMALL, LEN), BF),
            pltpu.VMEM((SMALL, D), F32),
            pltpu.VMEM((SMALL, 1), F32),
            pltpu.VMEM((D, 256), F32),
            pltpu.SemaphoreType.DMA((16,)),
        ],
        "attend_bwd",
        10,
        12_000_000,
        28,
    )(*pinned(*pieces, qkv, lse, wide), datt, *pinned(w_t), small, vec, vgrads, ugrads)


def out_copies(rows_ref, wbuf, sem):
    return [
        pltpu.make_async_copy(rows_ref.at[k, pl.ds(0, 48)], wbuf.at[pl.ds(48 * k, 48)], sem.at[k]) for k in range(8)
    ]


def branch_kernel(att_ref, rows_ref, own_ref, send_ref, keep_ref, wbuf, sem):
    copies = out_copies(rows_ref, wbuf, sem)
    for copy in copies:
        copy.start()
    parts = [att_ref[:, y].reshape(8 * HD, 2 * ROWS) for y in range(2)]
    keep_ref[...] = parts[0]
    for copy in copies:
        copy.wait()
    for y in range(2):
        out = tn(parts[y], wbuf[...])
        own_ref[y] = out[:ROWS]
        send_ref[y] = out[ROWS:]


def branch(att, rows_full):
    two = full(2, ROWS, D)
    return grid_call(
        branch_kernel, 1, [full(8, 2, HD, 2 * ROWS), HBM], [two, two, full(8 * HD, 2 * ROWS)],
        [like(2, ROWS, D, dtype=F32)] * 2 + [like(8 * HD, 2 * ROWS)],
        [pltpu.VMEM((8 * HD, D), BF), pltpu.SemaphoreType.DMA((8,))], "branch", 2, 2_000_000, 16,
    )(att, *pinned(rows_full))


def unit_rows(v):
    center = jnp.mean(v, axis=-1, keepdims=True)
    centered = v - center
    inverse = lax.rsqrt(jnp.mean(centered * centered, axis=-1, keepdims=True) + EPS)
    return centered * inverse, inverse


def norm_back(d, unit, inverse, gain):
    dg = d * gain
    return inverse * (dg - jnp.mean(dg, axis=-1, keepdims=True) - unit * jnp.mean(dg * unit, axis=-1, keepdims=True))


def middle_kernel(x_ref, line_ref, own_ref, got_ref, vec_ref, res_ref, n2_ref):
    for y, rows in enumerate((x_ref, line_ref)):
        res = rows[...].astype(F32) + own_ref[y] + got_ref[y] + vec_ref[2:3]
        if y == 0:
            res_ref[...] = res
        n2_ref[y] = (unit_rows(res)[0] * vec_ref[3:4] + vec_ref[4:5]).astype(BF)


def middle(x, line, own, got, vec):
    one, two = full(ROWS, D), full(2, ROWS, D)
    return grid_call(
        middle_kernel, 1, [one, one, two, two, full(16, D)], [one, two],
        [in_hbm(ROWS, D, dtype=F32), like(2, ROWS, D)], [], "middle", 1, 2_000_000,
    )(x, line, own, got, vec)


def after_kernel(own_ref, core_ref, got_ref, res_ref, cot_ref, vec_ref, dres_ref, dbr_ref, vg_ref):
    cot = cot_ref[...].astype(F32)
    unit, inverse = unit_rows(res_ref[...])
    dn = own_ref[...] + core_ref[0].astype(F32) + got_ref[...].astype(F32)
    dres = cot + norm_back(dn, unit, inverse, vec_ref[3:4])
    dbr = dres.astype(BF)
    dres_ref[...] = dres
    dbr_ref[...] = dbr
    sums = [dbr.astype(F32), dn * unit, dn, cot]
    for i, v in enumerate(sums):
        vg_ref[i : i + 1] = jnp.sum(v, axis=0, keepdims=True)
    vg_ref[4:8] = jnp.zeros((4, D), F32)


def after(own, core, got, res, cot, vec):
    one = full(ROWS, D)
    return grid_call(
        after_kernel, 1, [one, full(2, ROWS, D), one, one, one, full(16, D)], [one, one, full(8, D)],
        [like(ROWS, D, dtype=F32), like(ROWS, D), like(8, D, dtype=F32)], [], "after", 2, 3_000_000,
    )(own, core, got, *pinned(res), cot, vec)


def branch_bwd_kernel(att_ref, own_ref, other_ref, rows_ref, grads_in, datt_ref, grads_ref, wbuf, gbuf, sem):
    copies = out_copies(rows_ref, wbuf, sem)
    for copy in copies:
        copy.start()
    d = jnp.concatenate([own_ref[...], other_ref[...]], axis=0)
    gbuf[...] = nn(att_ref[...], d).astype(BF)
    backs = [
        pltpu.make_async_copy(gbuf.at[pl.ds(48 * k, 48)], grads_ref.at[k, pl.ds(0, 48)], sem.at[8 + k]) for k in range(8)
    ]
    for back in backs:
        back.start()
    for copy in copies:
        copy.wait()
    datt_ref[...] = nt(wbuf[...], d).astype(BF)
    for back in backs:
        back.wait()


def branch_bwd(att, own, other, rows_full, grads):
    return pl.pallas_call(
        branch_bwd_kernel,
        grid=(1,),
        in_specs=[full(8 * HD, 2 * ROWS), full(ROWS, D), full(ROWS, D), HBM, HBM],
        out_specs=[full(8 * HD, 2 * ROWS), HBM],
        out_shape=[like(8 * HD, 2 * ROWS), in_hbm(8, BLOCK, D)],
        scratch_shapes=[pltpu.VMEM((8 * HD, D), BF), pltpu.VMEM((8 * HD, D), BF), pltpu.SemaphoreType.DMA((16,))],
        input_output_aliases={4: 1},
        compiler_params=params(8),
        cost_estimate=cost(3, 3_000_000),
        name="branch_bwd",
    )(att, own, other, *pinned(rows_full, grads))


TILE = 256
UNITS = FF // 4
STEPS = UNITS // TILE
FOUR = 4 * ROWS


def unit_rule():
    row = iota((D // 2, 1), 0)
    first = row // 24 * 48 + lax.rem(row, 24) // 6 * 12 + lax.rem(row, 3) * 4
    mine = lax.rem(row, 6) // 3 == lax.axis_index("yh")
    keep = jnp.where(mine, first // 4, -1) == iota((D // 2, UNITS), 1) // 4
    pick = (iota((16, UNITS), 0) == 8 + iota((16, UNITS), 1) % 4).astype(F32)
    return keep, pick


def unit_bias_kernel(small_ref, out_ref):
    keep, pick = unit_rule()
    half = pl.ds(pl.multiple_of(lax.axis_index("c") * (D // 2), 8), D // 2)
    out_ref[...] = jnp.sum(jnp.where(keep, nn(small_ref[half, :], pick), 0.0), axis=0, keepdims=True)


def unit_bias(small):
    return grid_call(
        unit_bias_kernel, 1, [full(D, 16)], full(1, UNITS), like(1, UNITS, dtype=F32), [], "unit_bias", 1, 500_000
    )(small)


def unit_bias_grad_kernel(total_ref, out_ref):
    keep, pick = unit_rule()
    out_ref[...] = nt(jnp.where(keep, jnp.broadcast_to(total_ref[...], keep.shape), 0.0), pick)


def unit_bias_grad(total):
    return grid_call(
        unit_bias_grad_kernel, 1, [full(1, UNITS)], full(D // 2, 16), like(D // 2, 16, dtype=F32), [],
        "unit_bias_grad", 1, 500_000,
    )(total)


def mlp_kernel(*refs):
    rows, cots = refs[:2], refs[2:6]
    (bias_ref, w_ref, oself, ocore, oline, dself, dcore, dline, g_ref, total_ref,
     nbuf, cbuf, up_ref, down_ref, gdbuf, gubuf, out, sems, in_sems) = refs[6:]
    j = pl.program_id(0)

    def weights(step):
        lanes, copies = pl.ds(step * TILE, TILE), []
        for z in range(8):
            for y in range(2):
                source = w_ref.at[z, pl.ds(144 + y * 48, 48), lanes]
                copies.append((source, up_ref.at[pl.ds(y * 384 + z * 48, 48), lanes]))
        for p in range(step * 8, step * 8 + 8):
            copies.append((w_ref.at[p // 3, pl.ds(48 + p % 3 * 32, 32)], down_ref.at[pl.ds(32 * p, 32)]))
        return [pltpu.make_async_copy(a, b, in_sems.at[24 * step + i]) for i, (a, b) in enumerate(copies)]

    @pl.when(j == 0)
    def _():
        for step in range(STEPS):
            for copy in weights(step):
                copy.start()
        for i in range(4):
            nbuf[i * ROWS : (i + 1) * ROWS] = rows[i % 2][i // 2]
            cbuf[i * ROWS : (i + 1) * ROWS] = cots[i][...]

    for step in range(STEPS):

        @pl.when(j == step)
        def _(step=step):
            for copy in weights(step):
                copy.wait()

    spot = pl.ds(pl.multiple_of(j * TILE, TILE), TILE)
    wu, wd = up_ref[:, spot], down_ref[spot, :]
    up = nn(nbuf[...], wu) + bias_ref[...]
    cdf = 0.5 * (1.0 + lax.erf(up * 2.0 ** (-0.5)))
    hidden = (up * cdf).astype(BF)
    dh = nt(cbuf[...], wd).astype(BF).astype(F32)
    slope = cdf + up * jnp.exp(-0.5 * up * up) * (2.0 * math.pi) ** (-0.5)
    d_up = (dh * slope).astype(BF)
    total_ref[...] = jnp.sum(d_up.astype(F32), axis=0, keepdims=True)
    gdbuf[spot, :] = tn(hidden, cbuf[...]).astype(BF)
    gu = tn(nbuf[...], d_up).astype(BF)
    for z in range(8):
        for y in range(2):
            gubuf[z, y * 48 : y * 48 + 48, spot] = gu[y * 384 + z * 48 : y * 384 + z * 48 + 48]

    def backs(step):
        copies = [
            pltpu.make_async_copy(
                gdbuf.at[pl.ds(32 * p, 32)], g_ref.at[p // 3, pl.ds(48 + p % 3 * 32, 32)], sems.at[p]
            )
            for p in range(step * 8, step * 8 + 8)
        ]
        lanes = pl.ds(step * TILE, TILE)
        target = g_ref.at[:, pl.ds(144, 96), lanes]
        return copies + [pltpu.make_async_copy(gubuf.at[:, :, lanes], target, sems.at[24 + step])]

    for step in range(STEPS):

        @pl.when(j == step)
        def _(step=step):
            for back in backs(step):
                back.start()

    out_part = nn(hidden, wd)
    dn_part = nt(d_up, wu)

    @pl.when(j == 0)
    def _():
        out[0] = out_part
        out[1] = dn_part

    @pl.when((j > 0) & (j < STEPS - 1))
    def _():
        out[0] += out_part
        out[1] += dn_part

    @pl.when(j == STEPS - 1)
    def _():
        for i, (own, core, line, part) in enumerate(
            ((oself, ocore, oline, out_part), (dself, dcore, dline, dn_part))
        ):
            whole = out[i] + part
            own[...] = whole[:ROWS]
            core[0] = whole[ROWS : 2 * ROWS].astype(BF)
            line[...] = whole[2 * ROWS : 3 * ROWS]
            core[1] = whole[3 * ROWS :].astype(BF)
        for step in range(STEPS):
            for back in backs(step):
                back.wait()


def mlp(rows, cots, bias, rows_full):
    one, two = full(ROWS, D), full(2, ROWS, D)
    parts = [like(ROWS, D, dtype=F32), like(2, ROWS, D), like(ROWS, D, dtype=F32)]
    cut = pl.BlockSpec((1, TILE), lambda j: (0, j))
    return grid_call(
        mlp_kernel,
        STEPS,
        [two] * 2 + [one] * 4 + [cut, HBM],
        [one, two, one] * 2 + [HBM, cut],
        parts * 2 + [in_hbm(8, BLOCK, D), like(1, UNITS, dtype=F32)],
        [
            pltpu.VMEM((FOUR, D), BF),
            pltpu.VMEM((FOUR, D), BF),
            pltpu.VMEM((D, UNITS), BF),
            pltpu.VMEM((UNITS, D), BF),
            pltpu.VMEM((UNITS, D), BF),
            pltpu.VMEM((8, 96, UNITS), BF),
            pltpu.VMEM((2, FOUR, D), F32),
            pltpu.SemaphoreType.DMA((24 + STEPS,)),
            pltpu.SemaphoreType.DMA((24 * STEPS,)),
        ],
        "mlp",
        8,
        8_000_000,
        28,
    )(*rows, *cots, bias, *pinned(rows_full))


def join_kernel(own_ref, got_ref, pair, left, right, far0, far1):
    for k, ref in enumerate((pair, left, right)):
        ref[...] = (own_ref[k].astype(F32) + got_ref[k].astype(F32)).astype(BF)
    far = (own_ref[3].astype(F32) + got_ref[3].astype(F32)).astype(BF)
    far0[...] = far[:ROWS]
    far1[...] = far[ROWS:]


def join(own, got):
    pieces = [(BLK, D)] * 3 + [(ROWS, D)] * 2
    return grid_call(
        join_kernel, 1, [full(4, BLK, D)] * 2, [full(*p) for p in pieces], [in_hbm(*p) for p in pieces],
        [], "join", 1, 5_000_000, 16,
    )(*pinned(own, got))


def deal_kernel(got_ref, sum_ref, out_ref, buf, line):
    total = got_ref[0].astype(F32)
    for z in range(1, 8):
        total = total + got_ref[z].astype(F32)
    line[...] = total
    buf[...] = jnp.zeros(buf.shape, F32)
    for b in range(8):
        for c in range(2):
            k = c * 8 + b
            buf[c * 15 : c * 15 + 3] = sum_ref[3 * k : 3 * k + 3].astype(F32)
            at = 48 + (c * 4 + b // 2) * 12
            down = sum_ref[at : at + 12].astype(F32)
            buf[c * 15 + 3 : c * 15 + 15] = jnp.where(lax.axis_index("yh") == b % 2, down, 0.0)
            for y in range(2):
                at, row = 144 + y * 48 + 3 * k, 30 + (y * 2 + c) * 3
                buf[row : row + 3] = sum_ref[at : at + 3].astype(F32)
        buf[42:45] = line[3 * b : 3 * b + 3]
        out_ref[b] = buf[...].astype(BF)


def deal(got, sums):
    return grid_call(
        deal_kernel, 1, [full(8, LINE, D), full(BLOCK, D)], full(8, SENT, D), like(8, SENT, D),
        [pltpu.VMEM((SENT, D), F32), pltpu.VMEM((LINE, D), F32)], "deal", 2, 2_000_000,
    )(got, *pinned(sums))


def share_kernel(got_ref, own_ref, core_ref, line_ref, both_ref, buf, tot):
    core0, yl0 = lax.axis_index("c") == 0, lax.axis_index("yl") == 0
    parts = [got_ref[b].astype(F32) for b in range(8)]
    for y in range(2):
        total = parts[y]
        for b in range(2 + y, 8, 2):
            total = total + parts[b]
        tot[y] = total
    both_units = tot[0] + tot[1]
    buf[...] = jnp.zeros(buf.shape, F32)
    for g in range(4):
        c = g % 2
        buf[g, 0:15] = both_units[c * 15 : c * 15 + 15]
        for y in range(2):
            buf[g, 15 + 3 * y : 18 + 3 * y] = tot[y, 30 + 3 * g : 33 + 3 * g]
        for b in range(8):
            row, lane = 21 + 3 * (b // 4), (b % 4) * WIN
            buf[g, row : row + 3, lane : lane + WIN] = parts[b][42:45, g * WIN : (g + 1) * WIN]
        buf[g, 21:24, SMALL : SMALL + 16] = both_units[42:45, g * WIN + SMALL : g * WIN + SMALL + 16]
    groups = groups_of(*(buf[g] for g in range(4)), core0, yl0)
    own_ref[...] = groups[0]
    core_ref[...] = groups[1].astype(BF)
    line_ref[...] = groups[2].astype(BF)
    both_ref[...] = groups[3].astype(BF)


def share(got):
    one = full(PACK, D)
    return grid_call(
        share_kernel, 1, [full(8, SENT, D)], [one] * 4, [like(PACK, D, dtype=F32)] + [like(PACK, D)] * 3,
        [pltpu.VMEM((4, PACK, D), F32), pltpu.VMEM((2, SENT, D), F32)], "share", 2, 2_000_000,
    )(got)


def finish_kernel(own_ref, core_ref, line_ref, both_ref, wq_ref, wu_ref, wo_ref, wd_ref, *refs):
    vectors, (buf, qbuf, cbuf) = refs[:8], refs[8:]
    core0 = lax.axis_index("c") == 0
    aligned = lax.axis_index("c") == lax.axis_index("yl")
    own, core, line, both = (r[...].astype(F32) for r in (own_ref, core_ref, line_ref, both_ref))
    cbuf[...] = jnp.zeros(cbuf.shape, F32)
    buf[0] = jnp.where(aligned, own + line, core + both)
    wo_ref[...] = buf[0, 0:3]
    wd_ref[...] = buf[0, 3:15]
    mine, theirs = own + line, core + both
    buf[0] = jnp.where(core0, mine, theirs)
    buf[1] = jnp.where(core0, theirs, mine)
    for k in range(2):
        for q in range(2):
            to = slice(q * (D // 2), (q + 1) * (D // 2))
            at = 8 * (2 * k + q)
            for y in range(2):
                cbuf[at : at + 3, y * (D // 2) : (y + 1) * (D // 2)] = buf[k, 15 + 3 * y : 18 + 3 * y, to]
        for b in range(8):
            row, lane, at = 21 + 3 * (b // 4), (b % 4) * WIN, (k * 8 + b) * HD
            for p in range(3):
                qbuf[0:3, p * D + at : p * D + at + HD] = buf[k, row : row + 3, lane + p * HD : lane + (p + 1) * HD]
    wq_ref[...] = qbuf[0:3]
    rest = cbuf[...]
    parts = []
    for _ in range(3):
        parts.append(rest.astype(BF))
        rest = rest - parts[-1].astype(F32)
    sums = nt(jnp.concatenate(parts, axis=0), unit_order())
    total = sums[0:32] + sums[32:64] + sums[64:96]
    for i in range(4):
        wu_ref[:, i * D : (i + 1) * D] = total[8 * i : 8 * i + 3]
    small = (buf[0] + buf[1])[21:24, SMALL : SMALL + 16]

    def row_of(first, stride, count):
        shape = (3, count)
        keep = iota(shape, 1) // stride == iota(shape, 0)
        total = jnp.zeros((1, count), F32)
        for k in range(stride):
            values = jnp.broadcast_to(small[:, first + k : first + k + 1], shape)
            total += jnp.sum(jnp.where(keep & (iota(shape, 1) % stride == k), values, 0.0), axis=0, keepdims=True)
        return total.reshape(count)

    for i in range(6):
        vectors[i][...] = row_of(i, 1, 3)
    vectors[6][...] = row_of(6, 2, 6)
    vectors[7][...] = row_of(8, 4, 12)


def finish(parts):
    shapes = [(3, 3 * D), (3, FF), (3, D), (12, D)] + [(3,)] * 6 + [(6,), (12,)]
    return grid_call(
        finish_kernel, 1, [full(PACK, D)] * 4, [full(*s) for s in shapes], [like(*s, dtype=F32) for s in shapes],
        [pltpu.VMEM((2, PACK, D), F32), pltpu.VMEM((8, 3 * D), F32), pltpu.VMEM((32, D), F32)], "finish", 2, 1_000_000,
    )(*parts)


AXES = ("yl", "z", "c", "x", "yh")
SEQ = ("yl", "z", "c")
BAND = ("x", "yh")
SWAP = [(0, 1), (1, 0)]
RIGHT = [(i, (i + 1) % 4) for i in range(4)]
LEFT = [(i, (i + 3) % 4) for i in range(4)]


def swap_core(v):
    return lax.ppermute(v, "c", SWAP)


def swap_yl(v):
    return lax.ppermute(v, "yl", SWAP)


def swap_yh(v):
    return lax.ppermute(v, "yh", SWAP)


def swap_both(v):
    return lax.ppermute(v, ("yl", "c"), [(0, 3), (1, 2), (2, 1), (3, 0)])


def exchange(v, axes):
    return lax.all_to_all(v, axes, 0, 0, tiled=True)


def ring_far(far0, far1):
    return lax.ppermute(far0, "x", RIGHT), lax.ppermute(far1, "x", LEFT)


def ring_add_kernel(left_ref, right_ref, from_left, from_right, left_out, right_out):
    left_out[0:ROWS] = left_ref[0:ROWS]
    left_out[ROWS:] = (left_ref[ROWS:].astype(F32) + from_right[...].astype(F32)).astype(BF)
    right_out[0:ROWS] = (right_ref[0:ROWS].astype(F32) + from_left[...].astype(F32)).astype(BF)
    right_out[ROWS:] = right_ref[ROWS:]


def ring_add(left, right, from_left, from_right):
    two, one = full(BLK, D), full(ROWS, D)
    return grid_call(
        ring_add_kernel, 1, [two, two, one, one], [two, two], [in_hbm(BLK, D)] * 2, [], "ring_add", 1, 2_000_000
    )(*pinned(left, right), from_left, from_right)


def settle_kernel(pair_ref, left_ref, right_ref, keep_ref, give_ref):
    first = lax.axis_index("yh") == 0
    total = pair_ref[...].astype(F32) + left_ref[...].astype(F32) + right_ref[...].astype(F32)
    keep_ref[...] = jnp.where(first, total[:ROWS], total[ROWS:])
    give_ref[...] = jnp.where(first, total[ROWS:], total[:ROWS]).astype(BF)


def settle(pair, left, right):
    two, one = full(BLK, D), full(ROWS, D)
    return grid_call(
        settle_kernel, 1, [two, two, two], [one, one], [like(ROWS, D, dtype=F32), like(ROWS, D)], [],
        "settle", 1, 2_000_000,
    )(*pinned(pair), left, right)


def tokens_kernel(keep_ref, got_ref, res_ref, unit_ref, inv_ref, vec_ref, out_ref):
    d = keep_ref[...] + got_ref[...].astype(F32)
    out_ref[...] = (res_ref[...] + norm_back(d, unit_ref[...], inv_ref[...], vec_ref[0:1])).astype(BF)


def tokens_grad(keep, got, res, unit, inverse, vec):
    one = full(ROWS, D)
    return grid_call(
        tokens_kernel, 1, [one, one, one, one, full(ROWS, 1), full(16, D)], one, like(ROWS, D), [],
        "tokens_grad", 1, 2_000_000,
    )(keep, got, res, unit, inverse, vec)


def per_device(
    tokens, image_ids, ln1_gain, ln1_bias, w_qkv, qv_bias, w_out, out_bias,
    ln2_gain, ln2_bias, w_up, up_bias, w_down, down_bias, cotangent,
):
    first = lax.axis_index("yh") == 0
    x = tokens[0]
    cot = cotangent[0]

    pack_own, pack_other, unit, unit1, inv1 = prep(
        w_qkv, w_up, w_out, w_down, (ln1_gain, ln1_bias, out_bias, ln2_gain, ln2_bias, down_bias, qv_bias, up_bias),
        image_ids, x,
    )
    sent = spread((pack_own, swap_core(pack_other), swap_yl(pack_own), swap_both(pack_other)))
    got_yh = swap_yh(unit)
    pair = jnp.stack([jnp.where(first, unit, got_yh), jnp.where(first, got_yh, unit)])
    got, pair = lax.optimization_barrier((exchange(sent, BAND), pair))
    left = lax.ppermute(pair, "x", RIGHT)
    right = lax.ppermute(pair, "x", LEFT)
    block, line = collect(got)
    rows_full = lax.all_gather(block, "z", axis=0)
    far0 = lax.ppermute(left[0], "x", RIGHT)
    far1 = lax.ppermute(right[1], "x", LEFT)
    line_got = exchange(line, "z")
    token_pieces = (pair.reshape(BLK, D), left.reshape(BLK, D), right.reshape(BLK, D), far0, far1)
    other_pieces = tuple(swap_core(v) for v in token_pieces)
    line_got, cot_line, x_line = lax.optimization_barrier((line_got, swap_yh(cot), swap_yh(x)))
    cots = (cot, swap_core(cot), cot_line, swap_core(cot_line))

    qkv, att, wide, lse, w_t, vec, small = attend_fwd(token_pieces + other_pieces, line_got)
    att, *cots = lax.optimization_barrier((att, *cots))
    branch_own, branch_send, att_c = branch(exchange(att, BAND), rows_full)
    residual, n2 = middle(x, x_line, branch_own, swap_core(branch_send), vec)

    rows = (n2, swap_core(n2))
    o_self, o_core, o_line, d_self, d_core, d_line, grads, utotal = mlp(rows, cots, unit_bias(small), rows_full)
    d_core = swap_core(d_core)
    d_line = swap_yh((d_line + d_core[1].astype(F32)).astype(BF))
    d_res, d_branch, vgrads = after(d_self, d_core, d_line, residual, cot, vec)
    d_att, grads = branch_bwd(att_c, d_branch, swap_core(d_branch), rows_full, grads)
    grad_sum = lax.psum_scatter(grads, "z", scatter_dimension=0, tiled=True).reshape(BLOCK, D)
    d_att_all = exchange(d_att.reshape(8, HD, 2 * ROWS), BAND)
    o_core = swap_core(o_core)
    o_line = (o_line + o_core[1].astype(F32)).astype(BF)
    d_att_all, o_line, utotal = lax.optimization_barrier((d_att_all, o_line, utotal))

    d_own, d_other, line_grad = attend_bwd(
        token_pieces + other_pieces, qkv, lse, wide, d_att_all, w_t, small, vec, vgrads, unit_bias_grad(utotal)
    )
    line_sum = exchange(line_grad, "z")
    d_pair, d_left, d_right, d_far0, d_far1 = join(d_own, swap_core(d_other))
    d_left, d_right = ring_add(d_left, d_right, *ring_far(d_far0, d_far1))
    line_sum, d_left, d_right, o_line = lax.optimization_barrier((line_sum, d_left, d_right, swap_yh(o_line)))
    from_left, from_right = lax.ppermute(d_right, "x", RIGHT), lax.ppermute(d_left, "x", LEFT)
    keep, give = settle(d_pair, from_left, from_right)
    last, give = lax.optimization_barrier((exchange(deal(line_sum, grad_sum), BAND), swap_yh(give)))
    d_tokens = tokens_grad(keep, give, d_res, unit1, inv1, vec)

    own, to_core, to_yl, to_both = share(last)
    done = finish((own, swap_core(to_core), swap_yl(to_yl), swap_both(to_both)))
    g_qkv, g_up, g_out, g_down, l1g, l1b, ob, l2g, l2b, db, qvb, upb = done
    output = residual + o_self + o_core[0].astype(F32) + o_line.astype(F32) + vec[5:6]
    return (
        output.astype(BF)[None], d_tokens[None], l1g, l1b, g_qkv, qvb, g_out, ob, l2g, l2b, g_up, upb, g_down, db,
    )


def solution(mesh):
    fine = Mesh(mesh.devices.reshape(2, 8, 2, 4, 2), AXES)
    seq_band = P(SEQ, BAND, None)
    flat, flat2 = P(AXES), P(AXES, None)
    in_specs = (
        seq_band, P(SEQ, BAND), flat, flat, flat2, flat, flat2, flat,
        flat, flat, flat2, flat, flat2, flat, seq_band,
    )
    out_specs = (
        seq_band, seq_band, flat, flat, flat2, flat, flat2, flat,
        flat, flat, flat2, flat, flat2, flat,
    )
    return jax.shard_map(per_device, mesh=fine, in_specs=in_specs, out_specs=out_specs, check_vma=False)
```

```python
import math

import jax
import jax.numpy as jnp
from jax import lax
from jax.experimental import pallas as pl
from jax.experimental.pallas import tpu as pltpu
from jax.sharding import Mesh, PartitionSpec as P

D = 768
HEADS = 16
HD = 48
FF = 3072
LEN = 1024
ROWS = 128
BLK = 256
HALF = FF // 2
EPS = 1e-05
SCALE = HD ** (-0.5)
BF = jnp.bfloat16
F32 = jnp.float32
HBM = pl.BlockSpec(memory_space=pltpu.HBM)


def nn(a, b):
    return lax.dot_general(a, b, (((1,), (0,)), ((), ())), preferred_element_type=F32)


def nt(a, b):
    return lax.dot_general(a, b, (((1,), (1,)), ((), ())), preferred_element_type=F32)


def tn(a, b):
    return lax.dot_general(a, b, (((0,), (0,)), ((), ())), preferred_element_type=F32)


def turned(a):
    return a.astype(F32).T.astype(BF)


def params(mebi):
    return pltpu.CompilerParams(vmem_limit_bytes=mebi << 20)


def cost(micros, size):
    return pl.CostEstimate(flops=1000, bytes_accessed=1000, transcendentals=0)


def grid_call(kernel, steps, ins, outs, out_shape, scratch, name, micros, size, mebi=8):
    return pl.pallas_call(
        kernel,
        grid=(steps,),
        in_specs=ins,
        out_specs=outs,
        out_shape=out_shape,
        scratch_shapes=scratch,
        compiler_params=params(mebi),
        cost_estimate=cost(micros, size),
        name=name,
    )


def pinned(*values):
    return tuple(pltpu.with_memory_space_constraint(v, pltpu.HBM) for v in values)


def in_hbm(*shape, dtype=BF):
    return pltpu.HBM(shape, dtype)


def full(*shape):
    return pl.BlockSpec(shape, lambda i: (0,) * len(shape))


def step_block(*shape):
    return pl.BlockSpec((None,) + shape, lambda i: (i,) + (0,) * len(shape))


def iota(shape, axis):
    return lax.broadcasted_iota(jnp.int32, shape, axis)


def like(*shape, dtype=BF):
    return jax.ShapeDtypeStruct(shape, dtype)


WIN = 192
SMALL = 3 * HD
PACK = 32


def unit_order():
    source = iota((D, 1), 0)
    part = lax.rem(source, 24)
    target = part // 12 * (D // 2) + source // 96 * 48 + lax.rem(source, 96) // 24 * 12 + lax.rem(part, 12)
    return (target == iota((D, D), 1)).astype(F32).astype(BF)


def prep_kernel(*refs):
    sources, (own_ref, other_ref, unit_ref, wide_ref, inv_ref), held, (buf, cbuf, sems) = refs[:14], refs[14:19], refs[19:33], refs[33:]
    copies = [pltpu.make_async_copy(a, b, sems.at[i]) for i, (a, b) in enumerate(zip(sources, held))]
    for copy in copies:
        copy.start()
    buf[...] = jnp.zeros(buf.shape, F32)
    cbuf[...] = jnp.zeros(cbuf.shape, F32)
    order = unit_order()
    copies[13].wait()
    unit, inverse = unit_rows(held[13][...].astype(F32))
    unit_ref[...] = unit.astype(BF)
    wide_ref[...] = unit
    inv_ref[...] = inverse
    for copy in copies[:13]:
        copy.wait()
    wq_ref, wu_ref, wo_ref, wd_ref = held[:4]
    vectors, ids_ref = held[4:12], held[12]

    def column(ref, stride, k):
        row = ref[...].astype(F32).reshape(1, ref.shape[0])
        shape = (3, ref.shape[0])
        keep = iota(shape, 1) == iota(shape, 0) * stride + k
        return jnp.sum(jnp.where(keep, jnp.broadcast_to(row, shape), 0.0), axis=1, keepdims=True)

    columns = [column(ref, 1, 0) for ref in vectors[:6]]
    columns += [column(vectors[6], 2, k) for k in range(2)]
    columns += [column(vectors[7], 4, k) for k in range(4)]
    mark = jnp.max(ids_ref[...].astype(F32), axis=1, keepdims=True)
    columns.append(jnp.broadcast_to(mark, (3, 1)))
    lanes = iota((3, 128), 1)
    small = jnp.zeros((3, 128), F32)
    for j, col in enumerate(columns):
        small = jnp.where(lanes == j, jnp.broadcast_to(col, (3, 128)), small)
    wq = wq_ref[...].astype(F32)
    for i in range(4):
        cbuf[8 * i : 8 * i + 3] = wu_ref[:, i * D : (i + 1) * D].astype(F32)
    chosen = nn(cbuf[...].astype(BF), order)
    for k in range(2):
        buf[k, 0:3] = wo_ref[...].astype(F32)
        buf[k, 3:15] = wd_ref[...].astype(F32)
        for q in range(2):
            at = 8 * (2 * k + q)
            for y in range(2):
                to = slice(q * (D // 2), (q + 1) * (D // 2))
                buf[k, 15 + 3 * y : 18 + 3 * y, to] = chosen[at : at + 3, y * (D // 2) : (y + 1) * (D // 2)]
        for b in range(8):
            row, lane, at = 21 + 3 * (b // 4), (b % 4) * WIN, (k * 8 + b) * HD
            for p in range(3):
                buf[k, row : row + 3, lane + p * HD : lane + (p + 1) * HD] = wq[:, p * D + at : p * D + at + HD]
            buf[k, row : row + 3, lane + SMALL : lane + SMALL + 16] = small[:, :16]
    core0 = lax.axis_index("c") == 0
    own_ref[...] = jnp.where(core0, buf[0], buf[1]).astype(BF)
    other_ref[...] = jnp.where(core0, buf[1], buf[0]).astype(BF)


def prep(w_qkv, w_up, w_out, w_down, vectors, ids, x):
    args = (w_qkv, w_up, w_out, w_down) + vectors + (ids, x)
    return grid_call(
        prep_kernel, 1, [HBM] * len(args), [full(PACK, D)] * 2 + [full(ROWS, D)] * 2 + [full(ROWS, 1)],
        [like(PACK, D)] * 2 + [like(ROWS, D), in_hbm(ROWS, D, dtype=F32), in_hbm(ROWS, 1, dtype=F32)],
        [pltpu.VMEM(a.shape, a.dtype) for a in args]
        + [pltpu.VMEM((2, PACK, D), F32), pltpu.VMEM((32, D), F32), pltpu.SemaphoreType.DMA((len(args),))],
        "prep", 2, 100_000,
    )(*pinned(*args))


def groups_of(own, core, line, both, core0, yl0):
    def pick(a, b, c, d):
        return jnp.where(yl0, jnp.where(core0, a, b), jnp.where(core0, c, d))

    return (
        pick(own, core, line, both),
        pick(core, own, both, line),
        pick(line, both, own, core),
        pick(both, line, core, own),
    )


SENT = 48


def spread_kernel(own_ref, core_ref, line_ref, both_ref, out_ref, buf):
    core0, yl0 = lax.axis_index("c") == 0, lax.axis_index("yl") == 0
    aligned = lax.axis_index("c") == lax.axis_index("yl")
    own, core, line, both = (r[...].astype(F32) for r in (own_ref, core_ref, line_ref, both_ref))
    same, cross = jnp.where(aligned, own, line), jnp.where(aligned, core, both)
    buf[...] = jnp.zeros(buf.shape, F32)
    buf[0:15] = jnp.where(core0, same, cross)[0:15]
    buf[15:30] = jnp.where(core0, cross, same)[0:15]
    groups = groups_of(own, core, line, both, core0, yl0)
    for b in range(8):
        y, row, lane = b % 2, 21 + 3 * (b // 4), (b % 4) * WIN
        for g in range(4):
            buf[30 + 3 * g : 33 + 3 * g] = groups[g][15 + 3 * y : 18 + 3 * y]
            buf[42:45, g * WIN : (g + 1) * WIN] = groups[g][row : row + 3, lane : lane + WIN]
        out_ref[b] = buf[...].astype(BF)


def spread(packs):
    return grid_call(
        spread_kernel, 1, [full(PACK, D)] * 4, full(8, SENT, D), like(8, SENT, D),
        [pltpu.VMEM((SENT, D), F32)], "spread", 1, 1_000_000,
    )(*packs)


BLOCK = 240
LINE = 24


def collect_kernel(got_ref, blk_ref, line_ref, buf, lbuf):
    yh = lax.axis_index("yh")
    for b in range(8):
        got = got_ref[b].astype(F32)
        for c in range(2):
            k = c * 8 + b
            buf[3 * k : 3 * k + 3] = got[c * 15 : c * 15 + 3]
            for y in range(2):
                at, row = 144 + y * 48 + 3 * k, 30 + (y * 2 + c) * 3
                buf[at : at + 3] = got[row : row + 3]
        lbuf[3 * b : 3 * b + 3] = got[42:45]
    for x in range(4):
        got = got_ref[2 * x + yh].astype(F32)
        for c in range(2):
            at = 48 + (c * 4 + x) * 12
            buf[at : at + 12] = got[c * 15 + 3 : c * 15 + 15]
    line = lbuf[...].astype(BF)
    for z in range(8):
        line_ref[z] = line
    blk_ref[...] = buf[...].astype(BF)


def collect(got):
    return grid_call(
        collect_kernel, 1, [full(8, SENT, D)], [full(BLOCK, D), full(8, LINE, D)], [in_hbm(BLOCK, D), like(8, LINE, D)],
        [pltpu.VMEM((BLOCK, D), F32), pltpu.VMEM((LINE, D), F32)], "collect", 2, 2_000_000,
    )(got)


def place_of(step):
    return lax.rem(lax.axis_index("x") + step, 4)


RING = (0, 3, 1, 2)


def head_index():
    return lax.axis_index("c") * 8 + lax.axis_index("x") * 2 + lax.axis_index("yh")


def group_rows(group):
    return pl.ds(pl.multiple_of(group * 24, 8), 24)


def pair_groups():
    at = (lax.axis_index("yl") * 8 + lax.axis_index("z")) * 2
    c = lax.axis_index("c")
    return at + c, at + 1 - c


def several_images(small_ref, seq):
    own, other = pair_groups()
    block = small_ref[group_rows(jnp.where(seq == 0, own, other)), :]
    marks = jnp.where(iota(block.shape, 1) == 12, block, 0.0)
    return jnp.max(marks) > 0.5


def piece_cols(k):
    return pl.ds(pl.multiple_of(place_of(RING[k]) * BLK, BLK), BLK)


def piece_copies(pieces, target, sems, s):
    at, copies = 0, []
    for i, piece in enumerate(pieces[5 * s : 5 * s + 5]):
        rows = piece.shape[0]
        copies.append(pltpu.make_async_copy(piece, target.at[s, pl.ds(at, rows)], sems.at[5 * s + i]))
        at += rows
    return copies


def attend_fwd_kernel(*refs):
    pieces = refs[:10]
    (line_ref, qkv_hbm, att_ref, wide_hbm, lse_hbm, wt_hbm, vec_ref, small_ref,
     xbuf, qkv_ref, wide_ref, lse_ref, wt_ref, keys_buf, wbuf, bias, sems) = refs[10:]
    seq = pl.program_id(0)

    def outgoing(s, kinds):
        pairs = ((qkv_ref, qkv_hbm), (wide_ref, wide_hbm), (lse_ref, lse_hbm))
        return [pltpu.make_async_copy(pairs[i][0].at[s], pairs[i][1].at[s], sems.at[10 + 3 * s + i]) for i in kinds]

    @pl.when(seq == 0)
    def _():
        for s in range(2):
            for copy in piece_copies(pieces, xbuf, sems, s):
                copy.start()
        wbuf[...] = jnp.zeros(wbuf.shape, F32)
        for z in range(8):
            line = line_ref[z].astype(F32)
            for g in range(4):
                y, c = g // 2, g % 2
                at = (y * 8 + z) * 48 + c * 24
                wbuf[at : at + 24, 0:WIN] = line[:, g * WIN : (g + 1) * WIN]
        turned_w = wbuf[...].T
        wt_ref[...] = turned_w[:SMALL].astype(BF)
        pltpu.make_async_copy(wt_ref, wt_hbm, sems.at[16]).start()
        vec_ref[...] = turned_w[SMALL : SMALL + 16]
        small_ref[...] = wbuf[:, SMALL : SMALL + 16]
        head = head_index()
        expand = (iota((HD, 24), 0) // 2 == iota((HD, 24), 1)).astype(F32)
        lane = iota((HD, 16), 1) == 6 + iota((HD, 16), 0) % 2
        for part, group in ((0, head), (2, 16 + head)):
            spreads = nn(expand, small_ref[group_rows(group), :])
            col = jnp.sum(jnp.where(lane, spreads, 0.0), axis=1, keepdims=True)
            bias[part * HD : (part + 1) * HD] = col
        bias[HD : 2 * HD] = jnp.zeros((HD, 1), F32)

    gain, off = vec_ref[0:1], vec_ref[1:2]
    for s in range(2):

        @pl.when(seq == s)
        def _(s=s):
            for copy in piece_copies(pieces, xbuf, sems, s):
                copy.wait()

    for k in range(4):
        rows = xbuf[seq, k * BLK : (k + 1) * BLK]
        normed = (rows.astype(F32) * gain + off).astype(BF)
        qkv_ref[seq, :, piece_cols(k)] = (nt(wt_ref[...], normed) + bias[...]).astype(BF)
    for s in range(2):

        @pl.when(seq == s)
        def _(s=s):
            for copy in outgoing(s, (0,)):
                copy.start()

    keys_buf[...] = turned(qkv_ref[seq, HD : 2 * HD, :])

    def block(qb, keys):
        cols = slice(qb * BLK, (qb + 1) * BLK)
        vt = qkv_ref[seq, 2 * HD : 3 * HD, keys]
        s = nn(keys_buf[keys, :], qkv_ref[seq, 0:HD, cols]) * SCALE
        peak = jnp.max(s, axis=0, keepdims=True)
        e = jnp.exp(s - peak)
        total = jnp.sum(e, axis=0, keepdims=True)
        lse_ref[seq, :, cols] = peak + jnp.log(total)
        out = nn(vt, e.astype(BF)) * (1.0 / total)
        wide_ref[seq, :, cols] = out
        out = out.astype(BF)
        low, high = out[:, :ROWS], out[:, ROWS:]
        att_ref[2 * qb, 0] = low
        att_ref[2 * qb, 1] = high
        att_ref[2 * qb + 1, 0] = high
        att_ref[2 * qb + 1, 1] = low

    several = several_images(small_ref, seq)

    @pl.when(jnp.logical_not(several))
    def _():
        for qb in range(LEN // BLK):
            block(qb, slice(0, LEN))

    @pl.when(several)
    def _():
        for qb in range(LEN // BLK):
            block(qb, slice(qb * BLK, (qb + 1) * BLK))

    for s in range(2):

        @pl.when(seq == s)
        def _(s=s):
            for copy in outgoing(s, (1, 2)):
                copy.start()

    @pl.when(seq == 1)
    def _():
        pltpu.make_async_copy(wt_ref, wt_hbm, sems.at[16]).wait()
        for s in range(2):
            for copy in outgoing(s, (0, 1, 2)):
                copy.wait()


def attend_fwd(pieces, line):
    return grid_call(
        attend_fwd_kernel,
        2,
        [HBM] * 10 + [full(8, LINE, D)],
        [HBM, pl.BlockSpec((8, 2, HD, ROWS), lambda i: (0, 0, 0, i)), HBM, HBM, HBM, full(16, D), full(D, 16)],
        [
            in_hbm(2, SMALL, LEN),
            like(8, 2, HD, 2 * ROWS),
            in_hbm(2, HD, LEN, dtype=F32),
            in_hbm(2, 1, LEN, dtype=F32),
            in_hbm(SMALL, D),
            like(16, D, dtype=F32),
            like(D, 16, dtype=F32),
        ],
        [
            pltpu.VMEM((2, LEN, D), BF),
            pltpu.VMEM((2, SMALL, LEN), BF),
            pltpu.VMEM((2, HD, LEN), F32),
            pltpu.VMEM((2, 1, LEN), F32),
            pltpu.VMEM((SMALL, D), BF),
            pltpu.VMEM((LEN, HD), BF),
            pltpu.VMEM((D, 256), F32),
            pltpu.VMEM((SMALL, 1), F32),
            pltpu.SemaphoreType.DMA((17,)),
        ],
        "attend_fwd",
        9,
        10_000_000,
        24,
    )(*pinned(*pieces), line)


def attend_bwd_kernel(*refs):
    pieces = refs[:10]
    (qkv_hbm, lse_hbm, wide_hbm, datt_ref, w_hbm, small_ref, vec_ref, vgrad_ref, ugrad_ref,
     down_far, down_near, dother_far, dother_near, out_ref,
     ubuf, qkv_ref, lse_ref, wide_ref, w_ref, dbuf,
     rows_buf, values_buf, dq_buf, dkv_buf, fbuf, acc, acc_bias, gbuf, sems) = refs[10:]
    seq = pl.program_id(0)

    def first_in():
        pairs = ((qkv_hbm, qkv_ref), (lse_hbm, lse_ref), (wide_hbm, wide_ref))
        return [pltpu.make_async_copy(a, b, sems.at[10 + i]) for i, (a, b) in enumerate(pairs)]

    def w_in():
        return pltpu.make_async_copy(w_hbm, w_ref, sems.at[13])

    def out(s):
        far, near = ((down_far, down_near), (dother_far, dother_near))[s]
        return [
            pltpu.make_async_copy(dbuf.at[s, 3], far, sems.at[14 + 2 * s]),
            pltpu.make_async_copy(dbuf.at[s, pl.ds(0, 3)], near, sems.at[15 + 2 * s]),
        ]

    @pl.when(seq == 0)
    def _():
        for copy in first_in() + [w_in()]:
            copy.start()
        for s in range(2):
            for copy in piece_copies(pieces, ubuf, sems, s):
                copy.start()
        for copy in first_in():
            copy.wait()

    rows_buf[:, 0 : 3 * HD] = turned(qkv_ref[seq])
    d_out = jnp.concatenate([datt_ref[b] for b in range(8)], axis=1)
    values_buf[:, 0:HD] = turned(d_out)
    delta_all = jnp.sum(d_out.astype(F32) * wide_ref[seq], axis=0, keepdims=True)
    QS, KS = 256, 256

    def scores(qb, kb):
        cols = slice(qb * QS, (qb + 1) * QS)
        keys = slice(kb * KS, (kb + 1) * KS)
        qt = qkv_ref[seq, 0:HD, cols]
        dt = d_out[:, cols]
        probs = jnp.exp(nn(rows_buf[keys, HD : 2 * HD], qt) * SCALE - lse_ref[seq, :, cols])
        ds = (probs * (nn(rows_buf[keys, 2 * HD : 3 * HD], dt) - delta_all[:, cols])).astype(BF)
        return probs.astype(BF), ds

    def products(qb, kb, probs, ds, first_q, first_k):
        cols = slice(qb * QS, (qb + 1) * QS)
        keys = slice(kb * KS, (kb + 1) * KS)
        dq = nn(qkv_ref[seq, HD : 2 * HD, keys], ds)
        dk = nn(ds, rows_buf[cols, 0:HD])
        dv = nn(probs, values_buf[cols, 0:HD])
        if first_q:
            dq_buf[:, cols] = dq
        else:
            dq_buf[:, cols] += dq
        if first_k:
            dkv_buf[keys, 0:HD] = dk
            dkv_buf[keys, HD : 2 * HD] = dv
        else:
            dkv_buf[keys, 0:HD] += dk
            dkv_buf[keys, HD : 2 * HD] += dv

    def sweep(tiles):
        seen_q, seen_k, held = set(), set(), None
        for tile in tiles + [None]:
            now = (tile, scores(*tile)) if tile else None
            if held is not None:
                (qb, kb), (probs, ds) = held
                products(qb, kb, probs, ds, qb not in seen_q, kb not in seen_k)
                seen_q.add(qb)
                seen_k.add(kb)
            held = now

    several = several_images(small_ref, seq)

    @pl.when(jnp.logical_not(several))
    def _():
        sweep([(qb, kb) for qb in range(LEN // QS) for kb in range(LEN // KS)])

    @pl.when(several)
    def _():
        for b in range(4):
            cols = slice(b * BLK, (b + 1) * BLK)
            qt = qkv_ref[seq, 0:HD, cols]
            dt = d_out[:, cols]
            probs = jnp.exp(nn(rows_buf[cols, HD : 2 * HD], qt) * SCALE - lse_ref[seq, :, cols])
            ds = (probs * (nn(rows_buf[cols, 2 * HD : 3 * HD], dt) - delta_all[:, cols])).astype(BF)
            dq_buf[:, cols] = nn(qkv_ref[seq, HD : 2 * HD, cols], ds)
            dkv_buf[cols, 0:HD] = nn(ds, rows_buf[cols, 0:HD])
            dkv_buf[cols, HD : 2 * HD] = nn(probs.astype(BF), values_buf[cols, 0:HD])

    dkv = dkv_buf[...]
    by_row = jnp.concatenate(
        [dq_buf[...].T * SCALE, dkv[:, 0:HD] * SCALE, dkv[:, HD : 2 * HD]], axis=1
    ).astype(BF)
    by_feature = turned(by_row)

    rows_buf[:, 0 : 3 * HD] = by_row
    fbuf[...] = by_feature

    @pl.when(seq == 0)
    def _():
        w_in().wait()

    for k in range(4):
        dbuf[seq, k] = nn(rows_buf[piece_cols(k), 0 : 3 * HD], w_ref[...]).astype(BF)
    for s in range(2):

        @pl.when(seq == s)
        def _(s=s):
            for copy in out(s):
                copy.start()
            for copy in piece_copies(pieces, ubuf, sems, s):
                copy.wait()

    gn = jnp.zeros((SMALL, D), F32)
    for k in range(4):
        gn = gn + nn(fbuf[:, piece_cols(k)], ubuf[seq, k * BLK : (k + 1) * BLK])
    gb = jnp.sum(by_feature.astype(F32), axis=1, keepdims=True)

    @pl.when(seq == 0)
    def _():
        acc[...] = gn
        acc_bias[...] = gb

    @pl.when(seq == 1)
    def _():
        w = w_ref[...].astype(F32)
        gb_all = acc_bias[...] + gb
        gn_all = acc[...] + gn
        rows = jnp.concatenate(
            [
                gn_all * vec_ref[0:1] + gb_all * vec_ref[1:2],
                jnp.sum(w * gn_all, axis=0, keepdims=True),
                jnp.sum(w * gb_all, axis=0, keepdims=True),
                vgrad_ref[0:4],
                jnp.zeros((256 - SMALL - 6, D), F32),
            ],
            axis=0,
        )
        gbuf[...] = rows.T
        head = head_index()
        fold = (iota((24, HD), 0) == iota((24, HD), 1) // 2).astype(F32)
        lane = iota((HD, 256), 1) == SMALL + 6 + iota((HD, 256), 0) % 2
        for part, group in ((0, head), (2, 16 + head)):
            spreads = jnp.where(lane, jnp.broadcast_to(gb_all[part * HD : (part + 1) * HD], (HD, 256)), 0.0)
            gbuf[group_rows(group), :] += nn(fold, spreads)
        half = pl.ds(pl.multiple_of(lax.axis_index("c") * (D // 2), 8), D // 2)
        gbuf[half, SMALL + 8 : SMALL + 12] = ugrad_ref[:, 8:12]
        for z in range(8):
            for g in range(4):
                y, c = g // 2, g % 2
                at = (y * 8 + z) * 48 + c * 24
                out_ref[z, :, g * WIN : (g + 1) * WIN] = gbuf[at : at + 24, 0:WIN].astype(BF)
        for s in range(2):
            for copy in out(s):
                copy.wait()


def attend_bwd(pieces, qkv, lse, wide, datt, w_t, small, vec, vgrads, ugrads):
    return grid_call(
        attend_bwd_kernel,
        2,
        [HBM] * 13
        + [pl.BlockSpec((8, HD, ROWS), lambda i: (0, 0, i)), HBM, full(D, 16), full(16, D), full(8, D), full(D // 2, 16)],
        [HBM] * 4 + [full(8, LINE, D)],
        [in_hbm(BLK, D), in_hbm(3, BLK, D)] * 2 + [like(8, LINE, D)],
        [
            pltpu.VMEM((2, LEN, D), BF),
            pltpu.VMEM((2, SMALL, LEN), BF),
            pltpu.VMEM((2, 1, LEN), F32),
            pltpu.VMEM((2, HD, LEN), F32),
            pltpu.VMEM((SMALL, D), BF),
            pltpu.VMEM((2, 4, BLK, D), BF),
            pltpu.VMEM((LEN, SMALL), BF),
            pltpu.VMEM((LEN, HD), BF),
            pltpu.VMEM((HD, LEN), F32),
            pltpu.VMEM((LEN, 2 * HD), F32),
            pltpu.VMEM((SMALL, LEN), BF),
            pltpu.VMEM((SMALL, D), F32),
            pltpu.VMEM((SMALL, 1), F32),
            pltpu.VMEM((D, 256), F32),
            pltpu.SemaphoreType.DMA((18,)),
        ],
        "attend_bwd",
        10,
        12_000_000,
        28,
    )(*pinned(*pieces, qkv, lse, wide), datt, *pinned(w_t), small, vec, vgrads, ugrads)


def out_copies(rows_ref, wbuf, sem):
    return [
        pltpu.make_async_copy(rows_ref.at[k, pl.ds(0, 48)], wbuf.at[pl.ds(48 * k, 48)], sem.at[k]) for k in range(8)
    ]


def branch_kernel(att_ref, rows_ref, own_ref, send_ref, keep_ref, wbuf, sem):
    copies = out_copies(rows_ref, wbuf, sem)
    for copy in copies:
        copy.start()
    parts = [att_ref[:, y].reshape(8 * HD, 2 * ROWS) for y in range(2)]
    keep_ref[...] = parts[0]
    for copy in copies:
        copy.wait()
    for y in range(2):
        out = tn(parts[y], wbuf[...])
        own_ref[y] = out[:ROWS]
        send_ref[y] = out[ROWS:].astype(BF)


def branch(att, rows_full):
    two = full(2, ROWS, D)
    return grid_call(
        branch_kernel, 1, [full(8, 2, HD, 2 * ROWS), HBM], [two, two, full(8 * HD, 2 * ROWS)],
        [like(2, ROWS, D, dtype=F32), like(2, ROWS, D), like(8 * HD, 2 * ROWS)],
        [pltpu.VMEM((8 * HD, D), BF), pltpu.SemaphoreType.DMA((8,))], "branch", 2, 2_000_000, 16,
    )(att, *pinned(rows_full))


def unit_rows(v):
    center = jnp.mean(v, axis=-1, keepdims=True)
    centered = v - center
    inverse = lax.rsqrt(jnp.mean(centered * centered, axis=-1, keepdims=True) + EPS)
    return centered * inverse, inverse


def norm_back(d, unit, inverse, gain):
    dg = d * gain
    return inverse * (dg - jnp.mean(dg, axis=-1, keepdims=True) - unit * jnp.mean(dg * unit, axis=-1, keepdims=True))


def middle_kernel(x_ref, line_ref, own_ref, got_ref, vec_ref, res_ref, n2_ref):
    for y, rows in enumerate((x_ref, line_ref)):
        res = rows[...].astype(F32) + own_ref[y] + got_ref[y].astype(F32) + vec_ref[2:3]
        if y == 0:
            res_ref[...] = res
        n2_ref[y] = (unit_rows(res)[0] * vec_ref[3:4] + vec_ref[4:5]).astype(BF)


def middle(x, line, own, got, vec):
    one, two = full(ROWS, D), full(2, ROWS, D)
    return grid_call(
        middle_kernel, 1, [one, one, two, two, full(16, D)], [one, two],
        [like(ROWS, D, dtype=F32), like(2, ROWS, D)], [], "middle", 1, 2_000_000,
    )(x, line, own, got, vec)


def after_kernel(own_ref, core_ref, got_ref, res_ref, cot_ref, vec_ref, dres_ref, dbr_ref, vg_ref):
    cot = cot_ref[...].astype(F32)
    unit, inverse = unit_rows(res_ref[...])
    dn = own_ref[...] + core_ref[0].astype(F32) + got_ref[...].astype(F32)
    dres = cot + norm_back(dn, unit, inverse, vec_ref[3:4])
    dbr = dres.astype(BF)
    dres_ref[...] = dres
    dbr_ref[...] = dbr
    sums = [dbr.astype(F32), dn * unit, dn, cot]
    for i, v in enumerate(sums):
        vg_ref[i : i + 1] = jnp.sum(v, axis=0, keepdims=True)
    vg_ref[4:8] = jnp.zeros((4, D), F32)


def after(own, core, got, res, cot, vec):
    one = full(ROWS, D)
    return grid_call(
        after_kernel, 1, [one, full(2, ROWS, D), one, one, one, full(16, D)], [one, one, full(8, D)],
        [like(ROWS, D, dtype=F32), like(ROWS, D), like(8, D, dtype=F32)], [], "after", 2, 3_000_000,
    )(own, core, got, res, cot, vec)


def branch_bwd_kernel(att_ref, own_ref, other_ref, rows_ref, grads_in, datt_ref, grads_ref, wbuf, gbuf, sem):
    copies = out_copies(rows_ref, wbuf, sem)
    for copy in copies:
        copy.start()
    d = jnp.concatenate([own_ref[...], other_ref[...]], axis=0)
    gbuf[...] = nn(att_ref[...], d).astype(BF)
    backs = [
        pltpu.make_async_copy(gbuf.at[pl.ds(48 * k, 48)], grads_ref.at[k, pl.ds(0, 48)], sem.at[8 + k]) for k in range(8)
    ]
    for back in backs:
        back.start()
    for copy in copies:
        copy.wait()
    datt_ref[...] = nt(wbuf[...], d).astype(BF)
    for back in backs:
        back.wait()


def branch_bwd(att, own, other, rows_full, grads):
    return pl.pallas_call(
        branch_bwd_kernel,
        grid=(1,),
        in_specs=[full(8 * HD, 2 * ROWS), full(ROWS, D), full(ROWS, D), HBM, HBM],
        out_specs=[full(8 * HD, 2 * ROWS), HBM],
        out_shape=[like(8 * HD, 2 * ROWS), in_hbm(8, BLOCK, D)],
        scratch_shapes=[pltpu.VMEM((8 * HD, D), BF), pltpu.VMEM((8 * HD, D), BF), pltpu.SemaphoreType.DMA((16,))],
        input_output_aliases={4: 1},
        compiler_params=params(8),
        cost_estimate=cost(3, 3_000_000),
        name="branch_bwd",
    )(att, own, other, *pinned(rows_full, grads))


TILE = 256
UNITS = FF // 4
STEPS = UNITS // TILE
FOUR = 4 * ROWS


def unit_rule():
    row = iota((D // 2, 1), 0)
    first = row // 24 * 48 + lax.rem(row, 24) // 6 * 12 + lax.rem(row, 3) * 4
    mine = lax.rem(row, 6) // 3 == lax.axis_index("yh")
    keep = jnp.where(mine, first // 4, -1) == iota((D // 2, UNITS), 1) // 4
    pick = (iota((16, UNITS), 0) == 8 + iota((16, UNITS), 1) % 4).astype(F32)
    return keep, pick


def unit_bias_kernel(small_ref, out_ref):
    keep, pick = unit_rule()
    half = pl.ds(pl.multiple_of(lax.axis_index("c") * (D // 2), 8), D // 2)
    out_ref[...] = jnp.sum(jnp.where(keep, nn(small_ref[half, :], pick), 0.0), axis=0, keepdims=True)


def unit_bias(small):
    return grid_call(
        unit_bias_kernel, 1, [full(D, 16)], full(1, UNITS), like(1, UNITS, dtype=F32), [], "unit_bias", 1, 500_000
    )(small)


def unit_bias_grad_kernel(total_ref, out_ref):
    keep, pick = unit_rule()
    out_ref[...] = nt(jnp.where(keep, jnp.broadcast_to(total_ref[...], keep.shape), 0.0), pick)


def unit_bias_grad(total):
    return grid_call(
        unit_bias_grad_kernel, 1, [full(1, UNITS)], full(D // 2, 16), like(D // 2, 16, dtype=F32), [],
        "unit_bias_grad", 1, 500_000,
    )(total)


def mlp_kernel(*refs):
    rows, cots = refs[:2], refs[2:6]
    (bias_ref, w_ref, oself, ocore, oline, dself, dcore, dline, g_ref, total_ref,
     nbuf, cbuf, up_ref, down_ref, gdbuf, gubuf, out, sems, in_sems) = refs[6:]
    j = pl.program_id(0)

    def weights(step):
        lanes, copies = pl.ds(step * TILE, TILE), []
        for z in range(8):
            for y in range(2):
                source = w_ref.at[z, pl.ds(144 + y * 48, 48), lanes]
                copies.append((source, up_ref.at[pl.ds(y * 384 + z * 48, 48), lanes]))
        for p in range(step * 8, step * 8 + 8):
            copies.append((w_ref.at[p // 3, pl.ds(48 + p % 3 * 32, 32)], down_ref.at[pl.ds(32 * p, 32)]))
        return [pltpu.make_async_copy(a, b, in_sems.at[24 * step + i]) for i, (a, b) in enumerate(copies)]

    @pl.when(j == 0)
    def _():
        for step in range(STEPS):
            for copy in weights(step):
                copy.start()
        for i in range(4):
            nbuf[i * ROWS : (i + 1) * ROWS] = rows[i % 2][i // 2]
            cbuf[i * ROWS : (i + 1) * ROWS] = cots[i][...]

    for step in range(STEPS):

        @pl.when(j == step)
        def _(step=step):
            for copy in weights(step):
                copy.wait()

    spot = pl.ds(pl.multiple_of(j * TILE, TILE), TILE)
    wu, wd = up_ref[:, spot], down_ref[spot, :]
    up = nn(nbuf[...], wu) + bias_ref[...]
    cdf = 0.5 * (1.0 + lax.erf(up * 2.0 ** (-0.5)))
    hidden = (up * cdf).astype(BF)
    dh = nt(cbuf[...], wd).astype(BF).astype(F32)
    slope = cdf + up * jnp.exp(-0.5 * up * up) * (2.0 * math.pi) ** (-0.5)
    d_up = (dh * slope).astype(BF)
    total_ref[...] = jnp.sum(d_up.astype(F32), axis=0, keepdims=True)
    gdbuf[spot, :] = tn(hidden, cbuf[...]).astype(BF)
    gu = tn(nbuf[...], d_up).astype(BF)
    for z in range(8):
        for y in range(2):
            gubuf[z, y * 48 : y * 48 + 48, spot] = gu[y * 384 + z * 48 : y * 384 + z * 48 + 48]

    def backs(step):
        copies = [
            pltpu.make_async_copy(
                gdbuf.at[pl.ds(32 * p, 32)], g_ref.at[p // 3, pl.ds(48 + p % 3 * 32, 32)], sems.at[p]
            )
            for p in range(step * 8, step * 8 + 8)
        ]
        lanes = pl.ds(step * TILE, TILE)
        target = g_ref.at[:, pl.ds(144, 96), lanes]
        return copies + [pltpu.make_async_copy(gubuf.at[:, :, lanes], target, sems.at[24 + step])]

    for step in range(STEPS):

        @pl.when(j == step)
        def _(step=step):
            for back in backs(step):
                back.start()

    out_part = nn(hidden, wd)
    dn_part = nt(d_up, wu)

    @pl.when(j == 0)
    def _():
        out[0] = out_part
        out[1] = dn_part

    @pl.when((j > 0) & (j < STEPS - 1))
    def _():
        out[0] += out_part
        out[1] += dn_part

    @pl.when(j == STEPS - 1)
    def _():
        for i, (own, core, line, part) in enumerate(
            ((oself, ocore, oline, out_part), (dself, dcore, dline, dn_part))
        ):
            whole = out[i] + part
            own[...] = whole[:ROWS]
            core[0] = whole[ROWS : 2 * ROWS].astype(BF)
            line[...] = whole[2 * ROWS : 3 * ROWS]
            core[1] = whole[3 * ROWS :].astype(BF)
        for step in range(STEPS):
            for back in backs(step):
                back.wait()


def mlp(rows, cots, bias, rows_full):
    one, two = full(ROWS, D), full(2, ROWS, D)
    parts = [like(ROWS, D, dtype=F32), like(2, ROWS, D), like(ROWS, D, dtype=F32)]
    cut = pl.BlockSpec((1, TILE), lambda j: (0, j))
    return grid_call(
        mlp_kernel,
        STEPS,
        [two] * 2 + [one] * 2 + [pl.BlockSpec((ROWS, D), lambda j: (1, 0))] * 2 + [cut, HBM],
        [one, two, one] * 2 + [HBM, cut],
        parts * 2 + [in_hbm(8, BLOCK, D), like(1, UNITS, dtype=F32)],
        [
            pltpu.VMEM((FOUR, D), BF),
            pltpu.VMEM((FOUR, D), BF),
            pltpu.VMEM((D, UNITS), BF),
            pltpu.VMEM((UNITS, D), BF),
            pltpu.VMEM((UNITS, D), BF),
            pltpu.VMEM((8, 96, UNITS), BF),
            pltpu.VMEM((2, FOUR, D), F32),
            pltpu.SemaphoreType.DMA((24 + STEPS,)),
            pltpu.SemaphoreType.DMA((24 * STEPS,)),
        ],
        "mlp",
        8,
        8_000_000,
        28,
    )(*rows, *cots, bias, *pinned(rows_full))


def join_kernel(*refs):
    n = len(refs) // 3
    for own, got, out in zip(refs[:n], refs[n : 2 * n], refs[2 * n :]):
        out[...] = (own[...].astype(F32) + got[...].astype(F32)).astype(BF)


def join_far_kernel(own, got, far0, far1):
    total = (own[...].astype(F32) + got[...].astype(F32)).astype(BF)
    far0[...] = total[:ROWS]
    far1[...] = total[ROWS:]


def join_far(own, got):
    return grid_call(
        join_far_kernel, 1, [full(BLK, D)] * 2, [full(ROWS, D)] * 2, [in_hbm(ROWS, D)] * 2, [], "join_far", 1, 1_000_000
    )(*pinned(own), got)


def join(owns, gots):
    n = len(owns)
    return grid_call(
        join_kernel, 1, [full(*v.shape) for v in owns + gots], [full(*v.shape) for v in owns],
        [in_hbm(*v.shape) for v in owns], [], f"join_{n}", 1, 5_000_000, 16,
    )(*pinned(*owns), *gots)


def deal_kernel(got_ref, sum_ref, out_ref, buf, line):
    total = got_ref[0].astype(F32)
    for z in range(1, 8):
        total = total + got_ref[z].astype(F32)
    line[...] = total
    buf[...] = jnp.zeros(buf.shape, F32)
    for b in range(8):
        for c in range(2):
            k = c * 8 + b
            buf[c * 15 : c * 15 + 3] = sum_ref[3 * k : 3 * k + 3].astype(F32)
            at = 48 + (c * 4 + b // 2) * 12
            down = sum_ref[at : at + 12].astype(F32)
            buf[c * 15 + 3 : c * 15 + 15] = jnp.where(lax.axis_index("yh") == b % 2, down, 0.0)
            for y in range(2):
                at, row = 144 + y * 48 + 3 * k, 30 + (y * 2 + c) * 3
                buf[row : row + 3] = sum_ref[at : at + 3].astype(F32)
        buf[42:45] = line[3 * b : 3 * b + 3]
        out_ref[b] = buf[...].astype(BF)


def deal(got, sums):
    return grid_call(
        deal_kernel, 1, [full(8, LINE, D), full(BLOCK, D)], full(8, SENT, D), like(8, SENT, D),
        [pltpu.VMEM((SENT, D), F32), pltpu.VMEM((LINE, D), F32)], "deal", 2, 2_000_000,
    )(got, *pinned(sums))


def share_kernel(got_ref, own_ref, core_ref, line_ref, both_ref, buf, tot):
    core0, yl0 = lax.axis_index("c") == 0, lax.axis_index("yl") == 0
    parts = [got_ref[b].astype(F32) for b in range(8)]
    for y in range(2):
        total = parts[y]
        for b in range(2 + y, 8, 2):
            total = total + parts[b]
        tot[y] = total
    both_units = tot[0] + tot[1]
    buf[...] = jnp.zeros(buf.shape, F32)
    for g in range(4):
        c = g % 2
        buf[g, 0:15] = both_units[c * 15 : c * 15 + 15]
        for y in range(2):
            buf[g, 15 + 3 * y : 18 + 3 * y] = tot[y, 30 + 3 * g : 33 + 3 * g]
        for b in range(8):
            row, lane = 21 + 3 * (b // 4), (b % 4) * WIN
            buf[g, row : row + 3, lane : lane + WIN] = parts[b][42:45, g * WIN : (g + 1) * WIN]
        buf[g, 21:24, SMALL : SMALL + 16] = both_units[42:45, g * WIN + SMALL : g * WIN + SMALL + 16]
    groups = groups_of(*(buf[g] for g in range(4)), core0, yl0)
    own_ref[...] = groups[0]
    core_ref[...] = groups[1].astype(BF)
    line_ref[...] = groups[2].astype(BF)
    both_ref[...] = groups[3].astype(BF)


def share(got):
    one = full(PACK, D)
    return grid_call(
        share_kernel, 1, [full(8, SENT, D)], [one] * 4, [like(PACK, D, dtype=F32)] + [like(PACK, D)] * 3,
        [pltpu.VMEM((4, PACK, D), F32), pltpu.VMEM((2, SENT, D), F32)], "share", 2, 2_000_000,
    )(got)


def finish_kernel(own_ref, core_ref, line_ref, both_ref, wq_ref, wu_ref, wo_ref, wd_ref, *refs):
    vectors, (buf, qbuf, cbuf) = refs[:8], refs[8:]
    core0 = lax.axis_index("c") == 0
    aligned = lax.axis_index("c") == lax.axis_index("yl")
    own, core, line, both = (r[...].astype(F32) for r in (own_ref, core_ref, line_ref, both_ref))
    cbuf[...] = jnp.zeros(cbuf.shape, F32)
    buf[0] = jnp.where(aligned, own + line, core + both)
    wo_ref[...] = buf[0, 0:3]
    wd_ref[...] = buf[0, 3:15]
    mine, theirs = own + line, core + both
    buf[0] = jnp.where(core0, mine, theirs)
    buf[1] = jnp.where(core0, theirs, mine)
    for k in range(2):
        for q in range(2):
            to = slice(q * (D // 2), (q + 1) * (D // 2))
            at = 8 * (2 * k + q)
            for y in range(2):
                cbuf[at : at + 3, y * (D // 2) : (y + 1) * (D // 2)] = buf[k, 15 + 3 * y : 18 + 3 * y, to]
        for b in range(8):
            row, lane, at = 21 + 3 * (b // 4), (b % 4) * WIN, (k * 8 + b) * HD
            for p in range(3):
                qbuf[0:3, p * D + at : p * D + at + HD] = buf[k, row : row + 3, lane + p * HD : lane + (p + 1) * HD]
    wq_ref[...] = qbuf[0:3]
    rest = cbuf[...]
    parts = []
    for _ in range(3):
        parts.append(rest.astype(BF))
        rest = rest - parts[-1].astype(F32)
    sums = nt(jnp.concatenate(parts, axis=0), unit_order())
    total = sums[0:32] + sums[32:64] + sums[64:96]
    for i in range(4):
        wu_ref[:, i * D : (i + 1) * D] = total[8 * i : 8 * i + 3]
    small = (buf[0] + buf[1])[21:24, SMALL : SMALL + 16]

    def row_of(first, stride, count):
        shape = (3, count)
        keep = iota(shape, 1) // stride == iota(shape, 0)
        total = jnp.zeros((1, count), F32)
        for k in range(stride):
            values = jnp.broadcast_to(small[:, first + k : first + k + 1], shape)
            total += jnp.sum(jnp.where(keep & (iota(shape, 1) % stride == k), values, 0.0), axis=0, keepdims=True)
        return total.reshape(count)

    for i in range(6):
        vectors[i][...] = row_of(i, 1, 3)
    vectors[6][...] = row_of(6, 2, 6)
    vectors[7][...] = row_of(8, 4, 12)


def finish(parts):
    shapes = [(3, 3 * D), (3, FF), (3, D), (12, D)] + [(3,)] * 6 + [(6,), (12,)]
    return grid_call(
        finish_kernel, 1, [full(PACK, D)] * 4, [full(*s) for s in shapes], [like(*s, dtype=F32) for s in shapes],
        [pltpu.VMEM((2, PACK, D), F32), pltpu.VMEM((8, 3 * D), F32), pltpu.VMEM((32, D), F32)], "finish", 2, 1_000_000,
    )(*parts)


AXES = ("yl", "z", "c", "x", "yh")
SEQ = ("yl", "z", "c")
BAND = ("x", "yh")
SWAP = [(0, 1), (1, 0)]
RIGHT = [(i, (i + 1) % 4) for i in range(4)]
LEFT = [(i, (i + 3) % 4) for i in range(4)]


def swap_core(v):
    return lax.ppermute(v, "c", SWAP)


def swap_yl(v):
    return lax.ppermute(v, "yl", SWAP)


def swap_yh(v):
    return lax.ppermute(v, "yh", SWAP)


def swap_both(v):
    return lax.ppermute(v, ("yl", "c"), [(0, 3), (1, 2), (2, 1), (3, 0)])


def exchange(v, axes):
    return lax.all_to_all(v, axes, 0, 0, tiled=True)


def ring_far(far0, far1):
    return lax.ppermute(far0, "x", RIGHT), lax.ppermute(far1, "x", LEFT)


def ring_add_kernel(near_ref, from_left, from_right, left_out, right_out):
    left_out[0:ROWS] = near_ref[1, 0:ROWS]
    left_out[ROWS:] = (near_ref[1, ROWS:].astype(F32) + from_right[...].astype(F32)).astype(BF)
    right_out[0:ROWS] = (near_ref[2, 0:ROWS].astype(F32) + from_left[...].astype(F32)).astype(BF)
    right_out[ROWS:] = near_ref[2, ROWS:]


def ring_add(near, from_left, from_right):
    two, one = full(BLK, D), full(ROWS, D)
    return grid_call(
        ring_add_kernel, 1, [full(3, BLK, D), one, one], [two, two], [in_hbm(BLK, D)] * 2, [], "ring_add", 1, 2_000_000
    )(*pinned(near), from_left, from_right)


def settle_kernel(near_ref, left_ref, right_ref, keep_ref, give_ref):
    first = lax.axis_index("yh") == 0
    total = near_ref[0].astype(F32) + left_ref[...].astype(F32) + right_ref[...].astype(F32)
    keep_ref[...] = jnp.where(first, total[:ROWS], total[ROWS:])
    give_ref[...] = jnp.where(first, total[ROWS:], total[:ROWS]).astype(BF)


def settle(near, left, right):
    two, one = full(BLK, D), full(ROWS, D)
    return grid_call(
        settle_kernel, 1, [full(3, BLK, D), two, two], [one, one], [like(ROWS, D, dtype=F32), like(ROWS, D)], [],
        "settle", 1, 2_000_000,
    )(*pinned(near), left, right)


def tokens_kernel(keep_ref, got_ref, res_ref, unit_ref, inv_ref, vec_ref, out_ref):
    d = keep_ref[...] + got_ref[...].astype(F32)
    out_ref[...] = (res_ref[...] + norm_back(d, unit_ref[...], inv_ref[...], vec_ref[0:1])).astype(BF)


def tokens_grad(keep, got, res, unit, inverse, vec):
    one = full(ROWS, D)
    return grid_call(
        tokens_kernel, 1, [one, one, one, one, full(ROWS, 1), full(16, D)], one, like(ROWS, D), [],
        "tokens_grad", 1, 2_000_000,
    )(keep, got, res, unit, inverse, vec)


def per_device(
    tokens, image_ids, ln1_gain, ln1_bias, w_qkv, qv_bias, w_out, out_bias,
    ln2_gain, ln2_bias, w_up, up_bias, w_down, down_bias, cotangent,
):
    first = lax.axis_index("yh") == 0
    x = tokens[0]
    cot = cotangent[0]

    pack_own, pack_other, unit, unit1, inv1 = prep(
        w_qkv, w_up, w_out, w_down, (ln1_gain, ln1_bias, out_bias, ln2_gain, ln2_bias, down_bias, qv_bias, up_bias),
        image_ids, x,
    )
    sent = spread((pack_own, swap_core(pack_other), swap_yl(pack_own), swap_both(pack_other)))
    got_yh = swap_yh(unit)
    pair = jnp.stack([jnp.where(first, unit, got_yh), jnp.where(first, got_yh, unit)])
    x_and_cot = jnp.concatenate([x, cot], axis=0)
    got, pair, x_and_cot = lax.optimization_barrier((exchange(sent, BAND), pair, x_and_cot))
    left = lax.ppermute(pair, "x", RIGHT)
    right = lax.ppermute(pair, "x", LEFT)
    block, line = collect(got)
    rows_full = lax.all_gather(block, "z", axis=0)
    far0 = lax.ppermute(left[0], "x", RIGHT)
    far1 = lax.ppermute(right[1], "x", LEFT)
    line_got = exchange(line, "z")
    token_pieces = (pair.reshape(BLK, D), left.reshape(BLK, D), right.reshape(BLK, D), far0, far1)
    other_pieces = tuple(swap_core(v) for v in token_pieces)
    line_got, line_rows, *other_pieces = lax.optimization_barrier((line_got, swap_yh(x_and_cot), *other_pieces))
    cots = (cot, swap_core(cot), line_rows, swap_core(line_rows))

    qkv, att, wide, lse, w_t, vec, small = attend_fwd(token_pieces + tuple(other_pieces), line_got)
    att, *cots = lax.optimization_barrier((att, *cots))
    branch_own, branch_send, att_c = branch(exchange(att, BAND), rows_full)
    residual, n2 = middle(x, line_rows, branch_own, swap_core(branch_send), vec)

    rows = (n2, swap_core(n2))
    o_self, o_core, o_line, d_self, d_core, d_line, grads, utotal = mlp(rows, cots, unit_bias(small), rows_full)
    d_core = swap_core(d_core)
    d_line = swap_yh((d_line + d_core[1].astype(F32)).astype(BF))
    d_line, ugrads = lax.optimization_barrier((d_line, unit_bias_grad(utotal)))
    d_res, d_branch, vgrads = after(d_self, d_core, d_line, residual, cot, vec)
    d_att, grads = branch_bwd(att_c, d_branch, swap_core(d_branch), rows_full, grads)
    grad_sum = lax.psum_scatter(grads, "z", scatter_dimension=0, tiled=True).reshape(BLOCK, D)
    d_att_all = exchange(d_att.reshape(8, HD, 2 * ROWS), BAND)
    o_core = swap_core(o_core)
    o_line = (o_line + o_core[1].astype(F32)).astype(BF)
    d_att_all, o_line = lax.optimization_barrier((d_att_all, o_line))

    own_far, own_near, other_far, other_near, line_grad = attend_bwd(
        token_pieces + tuple(other_pieces), qkv, lse, wide, d_att_all, w_t, small, vec, vgrads, ugrads
    )
    line_sum = exchange(line_grad, "z")
    d_far0, d_far1 = join_far(own_far, swap_core(other_far))
    (d_near,) = join((own_near,), (swap_core(other_near),))
    d_left, d_right = ring_add(d_near, *ring_far(d_far0, d_far1))
    line_sum, o_line = lax.optimization_barrier((line_sum, swap_yh(o_line)))
    from_left, from_right = lax.ppermute(d_right, "x", RIGHT), lax.ppermute(d_left, "x", LEFT)
    keep, give = settle(d_near, from_left, from_right)
    output = (residual + o_self + o_core[0].astype(F32) + o_line.astype(F32) + vec[5:6]).astype(BF)
    last, give, output = lax.optimization_barrier((exchange(deal(line_sum, grad_sum), BAND), swap_yh(give), output))
    d_tokens = tokens_grad(keep, give, d_res, unit1, inv1, vec)

    own, to_core, to_yl, to_both = share(last)
    done = finish((own, swap_core(to_core), swap_yl(to_yl), swap_both(to_both)))
    g_qkv, g_up, g_out, g_down, l1g, l1b, ob, l2g, l2b, db, qvb, upb = done
    return (
        output[None], d_tokens[None], l1g, l1b, g_qkv, qvb, g_out, ob, l2g, l2b, g_up, upb, g_down, db,
    )


def solution(mesh):
    fine = Mesh(mesh.devices.reshape(2, 8, 2, 4, 2), AXES)
    seq_band = P(SEQ, BAND, None)
    flat, flat2 = P(AXES), P(AXES, None)
    in_specs = (
        seq_band, P(SEQ, BAND), flat, flat, flat2, flat, flat2, flat,
        flat, flat, flat2, flat, flat2, flat, seq_band,
    )
    out_specs = (
        seq_band, seq_band, flat, flat, flat2, flat, flat2, flat,
        flat, flat, flat2, flat, flat2, flat,
    )
    return jax.shard_map(per_device, mesh=fine, in_specs=in_specs, out_specs=out_specs, check_vma=False)
```

```python
import math

import jax
import jax.numpy as jnp
from jax import lax
from jax.experimental import pallas as pl
from jax.experimental.pallas import tpu as pltpu
from jax.sharding import Mesh, PartitionSpec as P

D = 768
HEADS = 16
HD = 48
FF = 3072
LEN = 1024
ROWS = 128
BLK = 256
HALF = FF // 2
EPS = 1e-05
SCALE = HD ** (-0.5)
BF = jnp.bfloat16
F32 = jnp.float32
HBM = pl.BlockSpec(memory_space=pltpu.HBM)


def nn(a, b):
    return lax.dot_general(a, b, (((1,), (0,)), ((), ())), preferred_element_type=F32)


def nt(a, b):
    return lax.dot_general(a, b, (((1,), (1,)), ((), ())), preferred_element_type=F32)


def tn(a, b):
    return lax.dot_general(a, b, (((0,), (0,)), ((), ())), preferred_element_type=F32)


def turned(a):
    return a.astype(F32).T.astype(BF)


def params(mebi):
    return pltpu.CompilerParams(vmem_limit_bytes=mebi << 20)


def cost(micros, size):
    return pl.CostEstimate(flops=1000, bytes_accessed=1000, transcendentals=0)


def grid_call(kernel, steps, ins, outs, out_shape, scratch, name, micros, size, mebi=8):
    return pl.pallas_call(
        kernel,
        grid=(steps,),
        in_specs=ins,
        out_specs=outs,
        out_shape=out_shape,
        scratch_shapes=scratch,
        compiler_params=params(mebi),
        cost_estimate=cost(micros, size),
        name=name,
    )


def pinned(*values):
    return tuple(pltpu.with_memory_space_constraint(v, pltpu.HBM) for v in values)


def in_hbm(*shape, dtype=BF):
    return pltpu.HBM(shape, dtype)


def full(*shape):
    return pl.BlockSpec(shape, lambda i: (0,) * len(shape))


def step_block(*shape):
    return pl.BlockSpec((None,) + shape, lambda i: (i,) + (0,) * len(shape))


def iota(shape, axis):
    return lax.broadcasted_iota(jnp.int32, shape, axis)


def like(*shape, dtype=BF):
    return jax.ShapeDtypeStruct(shape, dtype)


WIN = 192
SMALL = 3 * HD
PACK = 32


def unit_order():
    source = iota((D, 1), 0)
    part = lax.rem(source, 24)
    target = part // 12 * (D // 2) + source // 96 * 48 + lax.rem(source, 96) // 24 * 12 + lax.rem(part, 12)
    return (target == iota((D, D), 1)).astype(F32).astype(BF)


def prep_kernel(*refs):
    sources, (own_ref, other_ref, rows_ref, wide_ref, inv_ref), held, (buf, cbuf, sems) = refs[:14], refs[14:19], refs[19:33], refs[33:]
    copies = [pltpu.make_async_copy(a, b, sems.at[i]) for i, (a, b) in enumerate(zip(sources, held))]
    for copy in copies:
        copy.start()
    buf[...] = jnp.zeros(buf.shape, F32)
    cbuf[...] = jnp.zeros(cbuf.shape, F32)
    order = unit_order()
    copies[13].wait()
    unit, inverse = unit_rows(held[13][...].astype(F32))
    rows_ref[...] = held[13][...]
    wide_ref[...] = unit
    inv_ref[...] = inverse
    for copy in copies[:13]:
        copy.wait()
    wq_ref, wu_ref, wo_ref, wd_ref = held[:4]
    vectors, ids_ref = held[4:12], held[12]

    def column(ref, stride, k):
        row = ref[...].astype(F32).reshape(1, ref.shape[0])
        shape = (3, ref.shape[0])
        keep = iota(shape, 1) == iota(shape, 0) * stride + k
        return jnp.sum(jnp.where(keep, jnp.broadcast_to(row, shape), 0.0), axis=1, keepdims=True)

    columns = [column(ref, 1, 0) for ref in vectors[:6]]
    columns += [column(vectors[6], 2, k) for k in range(2)]
    columns += [column(vectors[7], 4, k) for k in range(4)]
    mark = jnp.max(ids_ref[...].astype(F32), axis=1, keepdims=True)
    columns.append(jnp.broadcast_to(mark, (3, 1)))
    lanes = iota((3, 128), 1)
    small = jnp.zeros((3, 128), F32)
    for j, col in enumerate(columns):
        small = jnp.where(lanes == j, jnp.broadcast_to(col, (3, 128)), small)
    wq = wq_ref[...].astype(F32)
    for i in range(4):
        cbuf[8 * i : 8 * i + 3] = wu_ref[:, i * D : (i + 1) * D].astype(F32)
    chosen = nn(cbuf[...].astype(BF), order)
    for k in range(2):
        buf[k, 0:3] = wo_ref[...].astype(F32)
        buf[k, 3:15] = wd_ref[...].astype(F32)
        for q in range(2):
            at = 8 * (2 * k + q)
            for y in range(2):
                to = slice(q * (D // 2), (q + 1) * (D // 2))
                buf[k, 15 + 3 * y : 18 + 3 * y, to] = chosen[at : at + 3, y * (D // 2) : (y + 1) * (D // 2)]
        for b in range(8):
            row, lane, at = 21 + 3 * (b // 4), (b % 4) * WIN, (k * 8 + b) * HD
            for p in range(3):
                buf[k, row : row + 3, lane + p * HD : lane + (p + 1) * HD] = wq[:, p * D + at : p * D + at + HD]
            buf[k, row : row + 3, lane + SMALL : lane + SMALL + 16] = small[:, :16]
    core0 = lax.axis_index("c") == 0
    own_ref[...] = jnp.where(core0, buf[0], buf[1]).astype(BF)
    other_ref[...] = jnp.where(core0, buf[1], buf[0]).astype(BF)


def prep(w_qkv, w_up, w_out, w_down, vectors, ids, x):
    args = (w_qkv, w_up, w_out, w_down) + vectors + (ids, x)
    return grid_call(
        prep_kernel, 1, [HBM] * len(args), [full(PACK, D)] * 2 + [full(ROWS, D)] * 2 + [full(ROWS, 1)],
        [like(PACK, D)] * 2 + [like(ROWS, D), in_hbm(ROWS, D, dtype=F32), in_hbm(ROWS, 1, dtype=F32)],
        [pltpu.VMEM(a.shape, a.dtype) for a in args]
        + [pltpu.VMEM((2, PACK, D), F32), pltpu.VMEM((32, D), F32), pltpu.SemaphoreType.DMA((len(args),))],
        "prep", 2, 100_000,
    )(*pinned(*args))


def groups_of(own, core, line, both, core0, yl0):
    def pick(a, b, c, d):
        return jnp.where(yl0, jnp.where(core0, a, b), jnp.where(core0, c, d))

    return (
        pick(own, core, line, both),
        pick(core, own, both, line),
        pick(line, both, own, core),
        pick(both, line, core, own),
    )


SENT = 48


def spread_kernel(own_ref, core_ref, line_ref, both_ref, out_ref, buf):
    core0, yl0 = lax.axis_index("c") == 0, lax.axis_index("yl") == 0
    aligned = lax.axis_index("c") == lax.axis_index("yl")
    own, core, line, both = (r[...].astype(F32) for r in (own_ref, core_ref, line_ref, both_ref))
    same, cross = jnp.where(aligned, own, line), jnp.where(aligned, core, both)
    buf[...] = jnp.zeros(buf.shape, F32)
    buf[0:15] = jnp.where(core0, same, cross)[0:15]
    buf[15:30] = jnp.where(core0, cross, same)[0:15]
    groups = groups_of(own, core, line, both, core0, yl0)
    for b in range(8):
        y, row, lane = b % 2, 21 + 3 * (b // 4), (b % 4) * WIN
        for g in range(4):
            buf[30 + 3 * g : 33 + 3 * g] = groups[g][15 + 3 * y : 18 + 3 * y]
            buf[42:45, g * WIN : (g + 1) * WIN] = groups[g][row : row + 3, lane : lane + WIN]
        out_ref[b] = buf[...].astype(BF)


def spread(packs):
    return grid_call(
        spread_kernel, 1, [full(PACK, D)] * 4, full(8, SENT, D), like(8, SENT, D),
        [pltpu.VMEM((SENT, D), F32)], "spread", 1, 1_000_000,
    )(*packs)


BLOCK = 240
LINE = 24


def collect_kernel(got_ref, blk_ref, line_ref, buf, lbuf):
    yh = lax.axis_index("yh")
    for b in range(8):
        got = got_ref[b].astype(F32)
        for c in range(2):
            k = c * 8 + b
            buf[3 * k : 3 * k + 3] = got[c * 15 : c * 15 + 3]
            for y in range(2):
                at, row = 144 + y * 48 + 3 * k, 30 + (y * 2 + c) * 3
                buf[at : at + 3] = got[row : row + 3]
        lbuf[3 * b : 3 * b + 3] = got[42:45]
    for x in range(4):
        got = got_ref[2 * x + yh].astype(F32)
        for c in range(2):
            at = 48 + (c * 4 + x) * 12
            buf[at : at + 12] = got[c * 15 + 3 : c * 15 + 15]
    line = lbuf[...].astype(BF)
    for z in range(8):
        line_ref[z] = line
    blk_ref[...] = buf[...].astype(BF)


def collect(got):
    return grid_call(
        collect_kernel, 1, [full(8, SENT, D)], [full(BLOCK, D), full(8, LINE, D)], [in_hbm(BLOCK, D), like(8, LINE, D)],
        [pltpu.VMEM((BLOCK, D), F32), pltpu.VMEM((LINE, D), F32)], "collect", 2, 2_000_000,
    )(got)


def place_of(step):
    return lax.rem(lax.axis_index("x") + step, 4)


RING = (0, 3, 1, 2)


def head_index():
    return lax.axis_index("c") * 8 + lax.axis_index("x") * 2 + lax.axis_index("yh")


def group_rows(group):
    return pl.ds(pl.multiple_of(group * 24, 8), 24)


def pair_groups():
    at = (lax.axis_index("yl") * 8 + lax.axis_index("z")) * 2
    c = lax.axis_index("c")
    return at + c, at + 1 - c


def several_images(small_ref, seq):
    own, other = pair_groups()
    block = small_ref[group_rows(jnp.where(seq == 0, own, other)), :]
    marks = jnp.where(iota(block.shape, 1) == 12, block, 0.0)
    return jnp.max(marks) > 0.5


def piece_cols(k):
    return pl.ds(pl.multiple_of(place_of(RING[k]) * BLK, BLK), BLK)


def piece_copies(pieces, target, sems, s):
    at, copies = 0, []
    for i, piece in enumerate(pieces[5 * s : 5 * s + 5]):
        rows = piece.shape[0]
        copies.append(pltpu.make_async_copy(piece, target.at[s, pl.ds(at, rows)], sems.at[5 * s + i]))
        at += rows
    return copies


def attend_fwd_kernel(*refs):
    pieces = refs[:10]
    (line_ref, unit_hbm, qkv_hbm, att_ref, wide_hbm, lse_hbm, wt_hbm, vec_ref, small_ref,
     xbuf, ubuf, qkv_ref, wide_ref, lse_ref, wt_ref, keys_buf, wbuf, bias, sems) = refs[10:]
    seq = pl.program_id(0)

    def outgoing(s, kinds):
        pairs = ((qkv_ref, qkv_hbm), (wide_ref, wide_hbm), (lse_ref, lse_hbm), (ubuf, unit_hbm))
        return [pltpu.make_async_copy(pairs[i][0].at[s], pairs[i][1].at[s], sems.at[10 + 4 * s + i]) for i in kinds]

    @pl.when(seq == 0)
    def _():
        for s in range(2):
            for copy in piece_copies(pieces, xbuf, sems, s):
                copy.start()
        wbuf[...] = jnp.zeros(wbuf.shape, F32)
        for z in range(8):
            line = line_ref[z].astype(F32)
            for g in range(4):
                y, c = g // 2, g % 2
                at = (y * 8 + z) * 48 + c * 24
                wbuf[at : at + 24, 0:WIN] = line[:, g * WIN : (g + 1) * WIN]
        turned_w = wbuf[...].T
        wt_ref[...] = turned_w[:SMALL].astype(BF)
        pltpu.make_async_copy(wt_ref, wt_hbm, sems.at[18]).start()
        vec_ref[...] = turned_w[SMALL : SMALL + 16]
        small_ref[...] = wbuf[:, SMALL : SMALL + 16]
        head = head_index()
        expand = (iota((HD, 24), 0) // 2 == iota((HD, 24), 1)).astype(F32)
        lane = iota((HD, 16), 1) == 6 + iota((HD, 16), 0) % 2
        for part, group in ((0, head), (2, 16 + head)):
            spreads = nn(expand, small_ref[group_rows(group), :])
            col = jnp.sum(jnp.where(lane, spreads, 0.0), axis=1, keepdims=True)
            bias[part * HD : (part + 1) * HD] = col
        bias[HD : 2 * HD] = jnp.zeros((HD, 1), F32)

    gain, off = vec_ref[0:1], vec_ref[1:2]
    for s in range(2):

        @pl.when(seq == s)
        def _(s=s):
            for copy in piece_copies(pieces, xbuf, sems, s):
                copy.wait()

    for k in range(4):
        rows = slice(k * BLK, (k + 1) * BLK)
        unit = unit_rows(xbuf[seq, rows].astype(F32))[0]
        ubuf[seq, rows] = unit.astype(BF)
        normed = (unit * gain + off).astype(BF)
        qkv_ref[seq, :, piece_cols(k)] = (nt(wt_ref[...], normed) + bias[...]).astype(BF)
    for s in range(2):

        @pl.when(seq == s)
        def _(s=s):
            for copy in outgoing(s, (0, 3)):
                copy.start()

    keys_buf[...] = turned(qkv_ref[seq, HD : 2 * HD, :])

    def block(qb, keys):
        cols = slice(qb * BLK, (qb + 1) * BLK)
        vt = qkv_ref[seq, 2 * HD : 3 * HD, keys]
        s = nn(keys_buf[keys, :], qkv_ref[seq, 0:HD, cols]) * SCALE
        peak = jnp.max(s, axis=0, keepdims=True)
        e = jnp.exp(s - peak)
        total = jnp.sum(e, axis=0, keepdims=True)
        lse_ref[seq, :, cols] = peak + jnp.log(total)
        out = nn(vt, e.astype(BF)) * (1.0 / total)
        wide_ref[seq, :, cols] = out
        out = out.astype(BF)
        low, high = out[:, :ROWS], out[:, ROWS:]
        att_ref[2 * qb, 0] = low
        att_ref[2 * qb, 1] = high
        att_ref[2 * qb + 1, 0] = high
        att_ref[2 * qb + 1, 1] = low

    several = several_images(small_ref, seq)

    @pl.when(jnp.logical_not(several))
    def _():
        for qb in range(LEN // BLK):
            block(qb, slice(0, LEN))

    @pl.when(several)
    def _():
        for qb in range(LEN // BLK):
            block(qb, slice(qb * BLK, (qb + 1) * BLK))

    for s in range(2):

        @pl.when(seq == s)
        def _(s=s):
            for copy in outgoing(s, (1, 2)):
                copy.start()

    @pl.when(seq == 1)
    def _():
        pltpu.make_async_copy(wt_ref, wt_hbm, sems.at[18]).wait()
        for s in range(2):
            for copy in outgoing(s, (0, 1, 2, 3)):
                copy.wait()


def attend_fwd(pieces, line):
    return grid_call(
        attend_fwd_kernel,
        2,
        [HBM] * 10 + [full(8, LINE, D)],
        [HBM, HBM, pl.BlockSpec((8, 2, HD, ROWS), lambda i: (0, 0, 0, i)), HBM, HBM, HBM, full(16, D), full(D, 16)],
        [
            in_hbm(2, LEN, D),
            in_hbm(2, SMALL, LEN),
            like(8, 2, HD, 2 * ROWS),
            in_hbm(2, HD, LEN, dtype=F32),
            in_hbm(2, 1, LEN, dtype=F32),
            in_hbm(SMALL, D),
            like(16, D, dtype=F32),
            like(D, 16, dtype=F32),
        ],
        [
            pltpu.VMEM((2, LEN, D), BF),
            pltpu.VMEM((2, LEN, D), BF),
            pltpu.VMEM((2, SMALL, LEN), BF),
            pltpu.VMEM((2, HD, LEN), F32),
            pltpu.VMEM((2, 1, LEN), F32),
            pltpu.VMEM((SMALL, D), BF),
            pltpu.VMEM((LEN, HD), BF),
            pltpu.VMEM((D, 256), F32),
            pltpu.VMEM((SMALL, 1), F32),
            pltpu.SemaphoreType.DMA((19,)),
        ],
        "attend_fwd",
        9,
        10_000_000,
        28,
    )(*pinned(*pieces), line)


def attend_bwd_kernel(*refs):
    (unit_hbm, qkv_hbm, lse_hbm, wide_hbm, datt_ref, w_hbm, small_ref, vec_ref, vgrad_ref, ugrad_ref,
     down_far, down_near, dother_far, dother_near, out_ref,
     ubuf, qkv_ref, lse_ref, wide_ref, w_ref, dbuf,
     rows_buf, values_buf, dq_buf, dkv_buf, fbuf, acc, acc_bias, gbuf, sems) = refs
    seq = pl.program_id(0)

    def first_in():
        pairs = ((qkv_hbm, qkv_ref), (lse_hbm, lse_ref), (wide_hbm, wide_ref))
        return [pltpu.make_async_copy(a, b, sems.at[10 + i]) for i, (a, b) in enumerate(pairs)]

    def unit_in(s):
        return pltpu.make_async_copy(unit_hbm.at[s], ubuf.at[s], sems.at[s])

    def w_in():
        return pltpu.make_async_copy(w_hbm, w_ref, sems.at[13])

    def out(s):
        far, near = ((down_far, down_near), (dother_far, dother_near))[s]
        return [
            pltpu.make_async_copy(dbuf.at[s, 3], far, sems.at[14 + 2 * s]),
            pltpu.make_async_copy(dbuf.at[s, pl.ds(0, 3)], near, sems.at[15 + 2 * s]),
        ]

    @pl.when(seq == 0)
    def _():
        for copy in first_in() + [w_in()]:
            copy.start()
        for s in range(2):
            unit_in(s).start()
        for copy in first_in():
            copy.wait()

    rows_buf[:, 0 : 3 * HD] = turned(qkv_ref[seq])
    d_out = jnp.concatenate([datt_ref[b] for b in range(8)], axis=1)
    values_buf[:, 0:HD] = turned(d_out)
    delta_all = jnp.sum(d_out.astype(F32) * wide_ref[seq], axis=0, keepdims=True)
    QS, KS = 256, 256

    def scores(qb, kb):
        cols = slice(qb * QS, (qb + 1) * QS)
        keys = slice(kb * KS, (kb + 1) * KS)
        qt = qkv_ref[seq, 0:HD, cols]
        dt = d_out[:, cols]
        probs = jnp.exp(nn(rows_buf[keys, HD : 2 * HD], qt) * SCALE - lse_ref[seq, :, cols])
        ds = (probs * (nn(rows_buf[keys, 2 * HD : 3 * HD], dt) - delta_all[:, cols])).astype(BF)
        return probs.astype(BF), ds

    def products(qb, kb, probs, ds, first_q, first_k):
        cols = slice(qb * QS, (qb + 1) * QS)
        keys = slice(kb * KS, (kb + 1) * KS)
        dq = nn(qkv_ref[seq, HD : 2 * HD, keys], ds)
        dk = nn(ds, rows_buf[cols, 0:HD])
        dv = nn(probs, values_buf[cols, 0:HD])
        if first_q:
            dq_buf[:, cols] = dq
        else:
            dq_buf[:, cols] += dq
        if first_k:
            dkv_buf[keys, 0:HD] = dk
            dkv_buf[keys, HD : 2 * HD] = dv
        else:
            dkv_buf[keys, 0:HD] += dk
            dkv_buf[keys, HD : 2 * HD] += dv

    def sweep(tiles):
        seen_q, seen_k, held = set(), set(), None
        for tile in tiles + [None]:
            now = (tile, scores(*tile)) if tile else None
            if held is not None:
                (qb, kb), (probs, ds) = held
                products(qb, kb, probs, ds, qb not in seen_q, kb not in seen_k)
                seen_q.add(qb)
                seen_k.add(kb)
            held = now

    several = several_images(small_ref, seq)

    @pl.when(jnp.logical_not(several))
    def _():
        sweep([(qb, kb) for qb in range(LEN // QS) for kb in range(LEN // KS)])

    @pl.when(several)
    def _():
        for b in range(4):
            cols = slice(b * BLK, (b + 1) * BLK)
            qt = qkv_ref[seq, 0:HD, cols]
            dt = d_out[:, cols]
            probs = jnp.exp(nn(rows_buf[cols, HD : 2 * HD], qt) * SCALE - lse_ref[seq, :, cols])
            ds = (probs * (nn(rows_buf[cols, 2 * HD : 3 * HD], dt) - delta_all[:, cols])).astype(BF)
            dq_buf[:, cols] = nn(qkv_ref[seq, HD : 2 * HD, cols], ds)
            dkv_buf[cols, 0:HD] = nn(ds, rows_buf[cols, 0:HD])
            dkv_buf[cols, HD : 2 * HD] = nn(probs.astype(BF), values_buf[cols, 0:HD])

    dkv = dkv_buf[...]
    by_row = jnp.concatenate(
        [dq_buf[...].T * SCALE, dkv[:, 0:HD] * SCALE, dkv[:, HD : 2 * HD]], axis=1
    ).astype(BF)
    by_feature = turned(by_row)

    rows_buf[:, 0 : 3 * HD] = by_row
    fbuf[...] = by_feature

    @pl.when(seq == 0)
    def _():
        w_in().wait()

    for k in range(4):
        dbuf[seq, k] = nn(rows_buf[piece_cols(k), 0 : 3 * HD], w_ref[...]).astype(BF)
    for s in range(2):

        @pl.when(seq == s)
        def _(s=s):
            for copy in out(s):
                copy.start()
            unit_in(s).wait()

    gn = jnp.zeros((SMALL, D), F32)
    for k in range(4):
        gn = gn + nn(fbuf[:, piece_cols(k)], ubuf[seq, k * BLK : (k + 1) * BLK])
    gb = jnp.sum(by_feature.astype(F32), axis=1, keepdims=True)

    @pl.when(seq == 0)
    def _():
        acc[...] = gn
        acc_bias[...] = gb

    @pl.when(seq == 1)
    def _():
        w = w_ref[...].astype(F32)
        gb_all = acc_bias[...] + gb
        gn_all = acc[...] + gn
        rows = jnp.concatenate(
            [
                gn_all * vec_ref[0:1] + gb_all * vec_ref[1:2],
                jnp.sum(w * gn_all, axis=0, keepdims=True),
                jnp.sum(w * gb_all, axis=0, keepdims=True),
                vgrad_ref[0:4],
                jnp.zeros((256 - SMALL - 6, D), F32),
            ],
            axis=0,
        )
        gbuf[...] = rows.T
        head = head_index()
        fold = (iota((24, HD), 0) == iota((24, HD), 1) // 2).astype(F32)
        lane = iota((HD, 256), 1) == SMALL + 6 + iota((HD, 256), 0) % 2
        for part, group in ((0, head), (2, 16 + head)):
            spreads = jnp.where(lane, jnp.broadcast_to(gb_all[part * HD : (part + 1) * HD], (HD, 256)), 0.0)
            gbuf[group_rows(group), :] += nn(fold, spreads)
        half = pl.ds(pl.multiple_of(lax.axis_index("c") * (D // 2), 8), D // 2)
        gbuf[half, SMALL + 8 : SMALL + 12] = ugrad_ref[:, 8:12]
        for z in range(8):
            for g in range(4):
                y, c = g // 2, g % 2
                at = (y * 8 + z) * 48 + c * 24
                out_ref[z, :, g * WIN : (g + 1) * WIN] = gbuf[at : at + 24, 0:WIN].astype(BF)
        for s in range(2):
            for copy in out(s):
                copy.wait()


def attend_bwd(unit, qkv, lse, wide, datt, w_t, small, vec, vgrads, ugrads):
    return grid_call(
        attend_bwd_kernel,
        2,
        [HBM] * 4
        + [pl.BlockSpec((8, HD, ROWS), lambda i: (0, 0, i)), HBM, full(D, 16), full(16, D), full(8, D), full(D // 2, 16)],
        [HBM] * 4 + [full(8, LINE, D)],
        [in_hbm(BLK, D), in_hbm(3, BLK, D)] * 2 + [like(8, LINE, D)],
        [
            pltpu.VMEM((2, LEN, D), BF),
            pltpu.VMEM((2, SMALL, LEN), BF),
            pltpu.VMEM((2, 1, LEN), F32),
            pltpu.VMEM((2, HD, LEN), F32),
            pltpu.VMEM((SMALL, D), BF),
            pltpu.VMEM((2, 4, BLK, D), BF),
            pltpu.VMEM((LEN, SMALL), BF),
            pltpu.VMEM((LEN, HD), BF),
            pltpu.VMEM((HD, LEN), F32),
            pltpu.VMEM((LEN, 2 * HD), F32),
            pltpu.VMEM((SMALL, LEN), BF),
            pltpu.VMEM((SMALL, D), F32),
            pltpu.VMEM((SMALL, 1), F32),
            pltpu.VMEM((D, 256), F32),
            pltpu.SemaphoreType.DMA((18,)),
        ],
        "attend_bwd",
        10,
        12_000_000,
        28,
    )(*pinned(unit, qkv, lse, wide), datt, *pinned(w_t), small, vec, vgrads, ugrads)


def out_copies(rows_ref, wbuf, sem):
    return [
        pltpu.make_async_copy(rows_ref.at[k, pl.ds(0, 48)], wbuf.at[pl.ds(48 * k, 48)], sem.at[k]) for k in range(8)
    ]


def branch_kernel(att_ref, rows_ref, own_ref, send_ref, keep_ref, wbuf, sem):
    copies = out_copies(rows_ref, wbuf, sem)
    for copy in copies:
        copy.start()
    parts = [att_ref[:, y].reshape(8 * HD, 2 * ROWS) for y in range(2)]
    keep_ref[...] = parts[0]
    for copy in copies:
        copy.wait()
    for y in range(2):
        out = tn(parts[y], wbuf[...])
        own_ref[y] = out[:ROWS]
        send_ref[y] = out[ROWS:].astype(BF)


def branch(att, rows_full):
    two = full(2, ROWS, D)
    return grid_call(
        branch_kernel, 1, [full(8, 2, HD, 2 * ROWS), HBM], [two, two, full(8 * HD, 2 * ROWS)],
        [like(2, ROWS, D, dtype=F32), like(2, ROWS, D), like(8 * HD, 2 * ROWS)],
        [pltpu.VMEM((8 * HD, D), BF), pltpu.SemaphoreType.DMA((8,))], "branch", 2, 2_000_000, 16,
    )(att, *pinned(rows_full))


def unit_rows(v):
    center = jnp.mean(v, axis=-1, keepdims=True)
    centered = v - center
    inverse = lax.rsqrt(jnp.mean(centered * centered, axis=-1, keepdims=True) + EPS)
    return centered * inverse, inverse


def norm_back(d, unit, inverse, gain):
    dg = d * gain
    return inverse * (dg - jnp.mean(dg, axis=-1, keepdims=True) - unit * jnp.mean(dg * unit, axis=-1, keepdims=True))


def middle_kernel(x_ref, line_ref, own_ref, got_ref, vec_ref, res_ref, n2_ref):
    for y, rows in enumerate((x_ref, line_ref)):
        res = rows[...].astype(F32) + own_ref[y] + got_ref[y].astype(F32) + vec_ref[2:3]
        if y == 0:
            res_ref[...] = res
        n2_ref[y] = (unit_rows(res)[0] * vec_ref[3:4] + vec_ref[4:5]).astype(BF)


def middle(x, line, own, got, vec):
    one, two = full(ROWS, D), full(2, ROWS, D)
    return grid_call(
        middle_kernel, 1, [one, one, two, two, full(16, D)], [one, two],
        [like(ROWS, D, dtype=F32), like(2, ROWS, D)], [], "middle", 1, 2_000_000,
    )(x, line, own, got, vec)


def after_kernel(own_ref, core_ref, got_ref, res_ref, cot_ref, vec_ref, dres_ref, dbr_ref, vg_ref):
    cot = cot_ref[...].astype(F32)
    unit, inverse = unit_rows(res_ref[...])
    dn = own_ref[...] + core_ref[0].astype(F32) + got_ref[...].astype(F32)
    dres = cot + norm_back(dn, unit, inverse, vec_ref[3:4])
    dbr = dres.astype(BF)
    dres_ref[...] = dres
    dbr_ref[...] = dbr
    sums = [dbr.astype(F32), dn * unit, dn, cot]
    for i, v in enumerate(sums):
        vg_ref[i : i + 1] = jnp.sum(v, axis=0, keepdims=True)
    vg_ref[4:8] = jnp.zeros((4, D), F32)


def after(own, core, got, res, cot, vec):
    one = full(ROWS, D)
    return grid_call(
        after_kernel, 1, [one, full(2, ROWS, D), one, one, one, full(16, D)], [one, one, full(8, D)],
        [like(ROWS, D, dtype=F32), like(ROWS, D), like(8, D, dtype=F32)], [], "after", 2, 3_000_000,
    )(own, core, got, res, cot, vec)


def branch_bwd_kernel(att_ref, own_ref, other_ref, rows_ref, grads_in, datt_ref, grads_ref, wbuf, gbuf, sem):
    copies = out_copies(rows_ref, wbuf, sem)
    for copy in copies:
        copy.start()
    d = jnp.concatenate([own_ref[...], other_ref[...]], axis=0)
    gbuf[...] = nn(att_ref[...], d).astype(BF)
    backs = [
        pltpu.make_async_copy(gbuf.at[pl.ds(48 * k, 48)], grads_ref.at[k, pl.ds(0, 48)], sem.at[8 + k]) for k in range(8)
    ]
    for back in backs:
        back.start()
    for copy in copies:
        copy.wait()
    datt_ref[...] = nt(wbuf[...], d).astype(BF)
    for back in backs:
        back.wait()


def branch_bwd(att, own, other, rows_full, grads):
    return pl.pallas_call(
        branch_bwd_kernel,
        grid=(1,),
        in_specs=[full(8 * HD, 2 * ROWS), full(ROWS, D), full(ROWS, D), HBM, HBM],
        out_specs=[full(8 * HD, 2 * ROWS), HBM],
        out_shape=[like(8 * HD, 2 * ROWS), in_hbm(8, BLOCK, D)],
        scratch_shapes=[pltpu.VMEM((8 * HD, D), BF), pltpu.VMEM((8 * HD, D), BF), pltpu.SemaphoreType.DMA((16,))],
        input_output_aliases={4: 1},
        compiler_params=params(8),
        cost_estimate=cost(3, 3_000_000),
        name="branch_bwd",
    )(att, own, other, *pinned(rows_full, grads))


TILE = 256
UNITS = FF // 4
STEPS = UNITS // TILE
FOUR = 4 * ROWS


def unit_rule():
    row = iota((D // 2, 1), 0)
    first = row // 24 * 48 + lax.rem(row, 24) // 6 * 12 + lax.rem(row, 3) * 4
    mine = lax.rem(row, 6) // 3 == lax.axis_index("yh")
    keep = jnp.where(mine, first // 4, -1) == iota((D // 2, UNITS), 1) // 4
    pick = (iota((16, UNITS), 0) == 8 + iota((16, UNITS), 1) % 4).astype(F32)
    return keep, pick


def unit_bias_kernel(small_ref, out_ref):
    keep, pick = unit_rule()
    half = pl.ds(pl.multiple_of(lax.axis_index("c") * (D // 2), 8), D // 2)
    out_ref[...] = jnp.sum(jnp.where(keep, nn(small_ref[half, :], pick), 0.0), axis=0, keepdims=True)


def unit_bias(small):
    return grid_call(
        unit_bias_kernel, 1, [full(D, 16)], full(1, UNITS), like(1, UNITS, dtype=F32), [], "unit_bias", 1, 500_000
    )(small)


def unit_bias_grad_kernel(total_ref, out_ref):
    keep, pick = unit_rule()
    out_ref[...] = nt(jnp.where(keep, jnp.broadcast_to(total_ref[...], keep.shape), 0.0), pick)


def unit_bias_grad(total):
    return grid_call(
        unit_bias_grad_kernel, 1, [full(1, UNITS)], full(D // 2, 16), like(D // 2, 16, dtype=F32), [],
        "unit_bias_grad", 1, 500_000,
    )(total)


def mlp_kernel(*refs):
    rows, cots = refs[:2], refs[2:6]
    (bias_ref, w_ref, oself, ocore, oline, dself, dcore, dline, g_ref, total_ref,
     nbuf, cbuf, up_ref, down_ref, gdbuf, gubuf, out, sems, in_sems) = refs[6:]
    j = pl.program_id(0)

    def weights(step):
        lanes, copies = pl.ds(step * TILE, TILE), []
        for z in range(8):
            for y in range(2):
                source = w_ref.at[z, pl.ds(144 + y * 48, 48), lanes]
                copies.append((source, up_ref.at[pl.ds(y * 384 + z * 48, 48), lanes]))
        for p in range(step * 8, step * 8 + 8):
            copies.append((w_ref.at[p // 3, pl.ds(48 + p % 3 * 32, 32)], down_ref.at[pl.ds(32 * p, 32)]))
        return [pltpu.make_async_copy(a, b, in_sems.at[24 * step + i]) for i, (a, b) in enumerate(copies)]

    @pl.when(j == 0)
    def _():
        for step in range(STEPS):
            for copy in weights(step):
                copy.start()
        for i in range(4):
            nbuf[i * ROWS : (i + 1) * ROWS] = rows[i % 2][i // 2]
            cbuf[i * ROWS : (i + 1) * ROWS] = cots[i][...]

    for step in range(STEPS):

        @pl.when(j == step)
        def _(step=step):
            for copy in weights(step):
                copy.wait()

    spot = pl.ds(pl.multiple_of(j * TILE, TILE), TILE)
    wu, wd = up_ref[:, spot], down_ref[spot, :]
    up = nn(nbuf[...], wu) + bias_ref[...]
    cdf = 0.5 * (1.0 + lax.erf(up * 2.0 ** (-0.5)))
    hidden = (up * cdf).astype(BF)
    dh = nt(cbuf[...], wd).astype(BF).astype(F32)
    slope = cdf + up * jnp.exp(-0.5 * up * up) * (2.0 * math.pi) ** (-0.5)
    d_up = (dh * slope).astype(BF)
    total_ref[...] = jnp.sum(d_up.astype(F32), axis=0, keepdims=True)
    gdbuf[spot, :] = tn(hidden, cbuf[...]).astype(BF)
    gu = tn(nbuf[...], d_up).astype(BF)
    for z in range(8):
        for y in range(2):
            gubuf[z, y * 48 : y * 48 + 48, spot] = gu[y * 384 + z * 48 : y * 384 + z * 48 + 48]

    def backs(step):
        copies = [
            pltpu.make_async_copy(
                gdbuf.at[pl.ds(32 * p, 32)], g_ref.at[p // 3, pl.ds(48 + p % 3 * 32, 32)], sems.at[p]
            )
            for p in range(step * 8, step * 8 + 8)
        ]
        lanes = pl.ds(step * TILE, TILE)
        target = g_ref.at[:, pl.ds(144, 96), lanes]
        return copies + [pltpu.make_async_copy(gubuf.at[:, :, lanes], target, sems.at[24 + step])]

    for step in range(STEPS):

        @pl.when(j == step)
        def _(step=step):
            for back in backs(step):
                back.start()

    out_part = nn(hidden, wd)
    dn_part = nt(d_up, wu)

    @pl.when(j == 0)
    def _():
        out[0] = out_part
        out[1] = dn_part

    @pl.when((j > 0) & (j < STEPS - 1))
    def _():
        out[0] += out_part
        out[1] += dn_part

    @pl.when(j == STEPS - 1)
    def _():
        for i, (own, core, line, part) in enumerate(
            ((oself, ocore, oline, out_part), (dself, dcore, dline, dn_part))
        ):
            whole = out[i] + part
            own[...] = whole[:ROWS]
            core[0] = whole[ROWS : 2 * ROWS].astype(BF)
            line[...] = whole[2 * ROWS : 3 * ROWS]
            core[1] = whole[3 * ROWS :].astype(BF)
        for step in range(STEPS):
            for back in backs(step):
                back.wait()


def mlp(rows, cots, bias, rows_full):
    one, two = full(ROWS, D), full(2, ROWS, D)
    parts = [like(ROWS, D, dtype=F32), like(2, ROWS, D), like(ROWS, D, dtype=F32)]
    cut = pl.BlockSpec((1, TILE), lambda j: (0, j))
    return grid_call(
        mlp_kernel,
        STEPS,
        [two] * 2 + [one] * 2 + [pl.BlockSpec((ROWS, D), lambda j: (1, 0))] * 2 + [cut, HBM],
        [one, two, one] * 2 + [HBM, cut],
        parts * 2 + [in_hbm(8, BLOCK, D), like(1, UNITS, dtype=F32)],
        [
            pltpu.VMEM((FOUR, D), BF),
            pltpu.VMEM((FOUR, D), BF),
            pltpu.VMEM((D, UNITS), BF),
            pltpu.VMEM((UNITS, D), BF),
            pltpu.VMEM((UNITS, D), BF),
            pltpu.VMEM((8, 96, UNITS), BF),
            pltpu.VMEM((2, FOUR, D), F32),
            pltpu.SemaphoreType.DMA((24 + STEPS,)),
            pltpu.SemaphoreType.DMA((24 * STEPS,)),
        ],
        "mlp",
        8,
        8_000_000,
        28,
    )(*rows, *cots, bias, *pinned(rows_full))


def join_kernel(*refs):
    n = len(refs) // 3
    for own, got, out in zip(refs[:n], refs[n : 2 * n], refs[2 * n :]):
        out[...] = (own[...].astype(F32) + got[...].astype(F32)).astype(BF)


def join_far_kernel(own, got, far0, far1):
    total = (own[...].astype(F32) + got[...].astype(F32)).astype(BF)
    far0[...] = total[:ROWS]
    far1[...] = total[ROWS:]


def join_far(own, got):
    return grid_call(
        join_far_kernel, 1, [full(BLK, D)] * 2, [full(ROWS, D)] * 2, [in_hbm(ROWS, D)] * 2, [], "join_far", 1, 1_000_000
    )(*pinned(own), got)


def join(owns, gots):
    n = len(owns)
    return grid_call(
        join_kernel, 1, [full(*v.shape) for v in owns + gots], [full(*v.shape) for v in owns],
        [in_hbm(*v.shape) for v in owns], [], f"join_{n}", 1, 5_000_000, 16,
    )(*pinned(*owns), *gots)


def deal_kernel(got_ref, sum_ref, out_ref, buf, line):
    total = got_ref[0].astype(F32)
    for z in range(1, 8):
        total = total + got_ref[z].astype(F32)
    line[...] = total
    buf[...] = jnp.zeros(buf.shape, F32)
    for b in range(8):
        for c in range(2):
            k = c * 8 + b
            buf[c * 15 : c * 15 + 3] = sum_ref[3 * k : 3 * k + 3].astype(F32)
            at = 48 + (c * 4 + b // 2) * 12
            down = sum_ref[at : at + 12].astype(F32)
            buf[c * 15 + 3 : c * 15 + 15] = jnp.where(lax.axis_index("yh") == b % 2, down, 0.0)
            for y in range(2):
                at, row = 144 + y * 48 + 3 * k, 30 + (y * 2 + c) * 3
                buf[row : row + 3] = sum_ref[at : at + 3].astype(F32)
        buf[42:45] = line[3 * b : 3 * b + 3]
        out_ref[b] = buf[...].astype(BF)


def deal(got, sums):
    return grid_call(
        deal_kernel, 1, [full(8, LINE, D), full(BLOCK, D)], full(8, SENT, D), like(8, SENT, D),
        [pltpu.VMEM((SENT, D), F32), pltpu.VMEM((LINE, D), F32)], "deal", 2, 2_000_000,
    )(got, *pinned(sums))


def share_kernel(got_ref, own_ref, core_ref, line_ref, both_ref, buf, tot):
    core0, yl0 = lax.axis_index("c") == 0, lax.axis_index("yl") == 0
    parts = [got_ref[b].astype(F32) for b in range(8)]
    for y in range(2):
        total = parts[y]
        for b in range(2 + y, 8, 2):
            total = total + parts[b]
        tot[y] = total
    both_units = tot[0] + tot[1]
    buf[...] = jnp.zeros(buf.shape, F32)
    for g in range(4):
        c = g % 2
        buf[g, 0:15] = both_units[c * 15 : c * 15 + 15]
        for y in range(2):
            buf[g, 15 + 3 * y : 18 + 3 * y] = tot[y, 30 + 3 * g : 33 + 3 * g]
        for b in range(8):
            row, lane = 21 + 3 * (b // 4), (b % 4) * WIN
            buf[g, row : row + 3, lane : lane + WIN] = parts[b][42:45, g * WIN : (g + 1) * WIN]
        buf[g, 21:24, SMALL : SMALL + 16] = both_units[42:45, g * WIN + SMALL : g * WIN + SMALL + 16]
    groups = groups_of(*(buf[g] for g in range(4)), core0, yl0)
    own_ref[...] = groups[0]
    core_ref[...] = groups[1].astype(BF)
    line_ref[...] = groups[2].astype(BF)
    both_ref[...] = groups[3].astype(BF)


def share(got):
    one = full(PACK, D)
    return grid_call(
        share_kernel, 1, [full(8, SENT, D)], [one] * 4, [like(PACK, D, dtype=F32)] + [like(PACK, D)] * 3,
        [pltpu.VMEM((4, PACK, D), F32), pltpu.VMEM((2, SENT, D), F32)], "share", 2, 2_000_000,
    )(got)


def finish_kernel(own_ref, core_ref, line_ref, both_ref, wq_ref, wu_ref, wo_ref, wd_ref, *refs):
    vectors, (buf, qbuf, cbuf) = refs[:8], refs[8:]
    core0 = lax.axis_index("c") == 0
    aligned = lax.axis_index("c") == lax.axis_index("yl")
    own, core, line, both = (r[...].astype(F32) for r in (own_ref, core_ref, line_ref, both_ref))
    cbuf[...] = jnp.zeros(cbuf.shape, F32)
    buf[0] = jnp.where(aligned, own + line, core + both)
    wo_ref[...] = buf[0, 0:3]
    wd_ref[...] = buf[0, 3:15]
    mine, theirs = own + line, core + both
    buf[0] = jnp.where(core0, mine, theirs)
    buf[1] = jnp.where(core0, theirs, mine)
    for k in range(2):
        for q in range(2):
            to = slice(q * (D // 2), (q + 1) * (D // 2))
            at = 8 * (2 * k + q)
            for y in range(2):
                cbuf[at : at + 3, y * (D // 2) : (y + 1) * (D // 2)] = buf[k, 15 + 3 * y : 18 + 3 * y, to]
        for b in range(8):
            row, lane, at = 21 + 3 * (b // 4), (b % 4) * WIN, (k * 8 + b) * HD
            for p in range(3):
                qbuf[0:3, p * D + at : p * D + at + HD] = buf[k, row : row + 3, lane + p * HD : lane + (p + 1) * HD]
    wq_ref[...] = qbuf[0:3]
    rest = cbuf[...]
    parts = []
    for _ in range(3):
        parts.append(rest.astype(BF))
        rest = rest - parts[-1].astype(F32)
    sums = nt(jnp.concatenate(parts, axis=0), unit_order())
    total = sums[0:32] + sums[32:64] + sums[64:96]
    for i in range(4):
        wu_ref[:, i * D : (i + 1) * D] = total[8 * i : 8 * i + 3]
    small = (buf[0] + buf[1])[21:24, SMALL : SMALL + 16]

    def row_of(first, stride, count):
        shape = (3, count)
        keep = iota(shape, 1) // stride == iota(shape, 0)
        total = jnp.zeros((1, count), F32)
        for k in range(stride):
            values = jnp.broadcast_to(small[:, first + k : first + k + 1], shape)
            total += jnp.sum(jnp.where(keep & (iota(shape, 1) % stride == k), values, 0.0), axis=0, keepdims=True)
        return total.reshape(count)

    for i in range(6):
        vectors[i][...] = row_of(i, 1, 3)
    vectors[6][...] = row_of(6, 2, 6)
    vectors[7][...] = row_of(8, 4, 12)


def finish(parts):
    shapes = [(3, 3 * D), (3, FF), (3, D), (12, D)] + [(3,)] * 6 + [(6,), (12,)]
    return grid_call(
        finish_kernel, 1, [full(PACK, D)] * 4, [full(*s) for s in shapes], [like(*s, dtype=F32) for s in shapes],
        [pltpu.VMEM((2, PACK, D), F32), pltpu.VMEM((8, 3 * D), F32), pltpu.VMEM((32, D), F32)], "finish", 2, 1_000_000,
    )(*parts)


AXES = ("yl", "z", "c", "x", "yh")
SEQ = ("yl", "z", "c")
BAND = ("x", "yh")
SWAP = [(0, 1), (1, 0)]
RIGHT = [(i, (i + 1) % 4) for i in range(4)]
LEFT = [(i, (i + 3) % 4) for i in range(4)]


def swap_core(v):
    return lax.ppermute(v, "c", SWAP)


def swap_yl(v):
    return lax.ppermute(v, "yl", SWAP)


def swap_yh(v):
    return lax.ppermute(v, "yh", SWAP)


def swap_both(v):
    return lax.ppermute(v, ("yl", "c"), [(0, 3), (1, 2), (2, 1), (3, 0)])


def exchange(v, axes):
    return lax.all_to_all(v, axes, 0, 0, tiled=True)


def ring_far(far0, far1):
    return lax.ppermute(far0, "x", RIGHT), lax.ppermute(far1, "x", LEFT)


def ring_add_kernel(near_ref, from_left, from_right, left_out, right_out):
    left_out[0:ROWS] = near_ref[1, 0:ROWS]
    left_out[ROWS:] = (near_ref[1, ROWS:].astype(F32) + from_right[...].astype(F32)).astype(BF)
    right_out[0:ROWS] = (near_ref[2, 0:ROWS].astype(F32) + from_left[...].astype(F32)).astype(BF)
    right_out[ROWS:] = near_ref[2, ROWS:]


def ring_add(near, from_left, from_right):
    two, one = full(BLK, D), full(ROWS, D)
    return grid_call(
        ring_add_kernel, 1, [full(3, BLK, D), one, one], [two, two], [in_hbm(BLK, D)] * 2, [], "ring_add", 1, 2_000_000
    )(*pinned(near), from_left, from_right)


def settle_kernel(near_ref, left_ref, right_ref, keep_ref, give_ref):
    first = lax.axis_index("yh") == 0
    total = near_ref[0].astype(F32) + left_ref[...].astype(F32) + right_ref[...].astype(F32)
    keep_ref[...] = jnp.where(first, total[:ROWS], total[ROWS:])
    give_ref[...] = jnp.where(first, total[ROWS:], total[:ROWS]).astype(BF)


def settle(near, left, right):
    two, one = full(BLK, D), full(ROWS, D)
    return grid_call(
        settle_kernel, 1, [full(3, BLK, D), two, two], [one, one], [like(ROWS, D, dtype=F32), like(ROWS, D)], [],
        "settle", 1, 2_000_000,
    )(*pinned(near), left, right)


def tokens_kernel(keep_ref, got_ref, res_ref, unit_ref, inv_ref, vec_ref, out_ref):
    d = keep_ref[...] + got_ref[...].astype(F32)
    out_ref[...] = (res_ref[...] + norm_back(d, unit_ref[...], inv_ref[...], vec_ref[0:1])).astype(BF)


def tokens_grad(keep, got, res, unit, inverse, vec):
    one = full(ROWS, D)
    return grid_call(
        tokens_kernel, 1, [one, one, one, one, full(ROWS, 1), full(16, D)], one, like(ROWS, D), [],
        "tokens_grad", 1, 2_000_000,
    )(keep, got, res, unit, inverse, vec)


def per_device(
    tokens, image_ids, ln1_gain, ln1_bias, w_qkv, qv_bias, w_out, out_bias,
    ln2_gain, ln2_bias, w_up, up_bias, w_down, down_bias, cotangent,
):
    first = lax.axis_index("yh") == 0
    x = tokens[0]
    cot = cotangent[0]

    pack_own, pack_other, rows, unit1, inv1 = prep(
        w_qkv, w_up, w_out, w_down, (ln1_gain, ln1_bias, out_bias, ln2_gain, ln2_bias, down_bias, qv_bias, up_bias),
        image_ids, x,
    )
    sent = spread((pack_own, swap_core(pack_other), swap_yl(pack_own), swap_both(pack_other)))
    got_yh = swap_yh(rows)
    pair = jnp.stack([jnp.where(first, rows, got_yh), jnp.where(first, got_yh, rows)])
    x_and_cot = jnp.concatenate([x, cot], axis=0)
    got, pair, x_and_cot = lax.optimization_barrier((exchange(sent, BAND), pair, x_and_cot))
    left = lax.ppermute(pair, "x", RIGHT)
    right = lax.ppermute(pair, "x", LEFT)
    block, line = collect(got)
    rows_full = lax.all_gather(block, "z", axis=0)
    far0 = lax.ppermute(left[0], "x", RIGHT)
    far1 = lax.ppermute(right[1], "x", LEFT)
    line_got = exchange(line, "z")
    token_pieces = (pair.reshape(BLK, D), left.reshape(BLK, D), right.reshape(BLK, D), far0, far1)
    other_pieces = tuple(swap_core(v) for v in token_pieces)
    line_got, line_rows, *other_pieces = lax.optimization_barrier((line_got, swap_yh(x_and_cot), *other_pieces))
    cots = (cot, swap_core(cot), line_rows, swap_core(line_rows))

    unit, qkv, att, wide, lse, w_t, vec, small = attend_fwd(token_pieces + tuple(other_pieces), line_got)
    att, *cots = lax.optimization_barrier((att, *cots))
    branch_own, branch_send, att_c = branch(exchange(att, BAND), rows_full)
    residual, n2 = middle(x, line_rows, branch_own, swap_core(branch_send), vec)

    rows = (n2, swap_core(n2))
    o_self, o_core, o_line, d_self, d_core, d_line, grads, utotal = mlp(rows, cots, unit_bias(small), rows_full)
    d_core = swap_core(d_core)
    d_line = swap_yh((d_line + d_core[1].astype(F32)).astype(BF))
    d_line, ugrads = lax.optimization_barrier((d_line, unit_bias_grad(utotal)))
    d_res, d_branch, vgrads = after(d_self, d_core, d_line, residual, cot, vec)
    d_att, grads = branch_bwd(att_c, d_branch, swap_core(d_branch), rows_full, grads)
    grad_sum = lax.psum_scatter(grads, "z", scatter_dimension=0, tiled=True).reshape(BLOCK, D)
    d_att_all = exchange(d_att.reshape(8, HD, 2 * ROWS), BAND)
    o_core = swap_core(o_core)
    o_line = (o_line + o_core[1].astype(F32)).astype(BF)
    d_att_all, o_line = lax.optimization_barrier((d_att_all, o_line))

    own_far, own_near, other_far, other_near, line_grad = attend_bwd(
        unit, qkv, lse, wide, d_att_all, w_t, small, vec, vgrads, ugrads
    )
    line_sum = exchange(line_grad, "z")
    d_far0, d_far1 = join_far(own_far, swap_core(other_far))
    (d_near,) = join((own_near,), (swap_core(other_near),))
    d_left, d_right = ring_add(d_near, *ring_far(d_far0, d_far1))
    line_sum, o_line = lax.optimization_barrier((line_sum, swap_yh(o_line)))
    from_left, from_right = lax.ppermute(d_right, "x", RIGHT), lax.ppermute(d_left, "x", LEFT)
    keep, give = settle(d_near, from_left, from_right)
    output = (residual + o_self + o_core[0].astype(F32) + o_line.astype(F32) + vec[5:6]).astype(BF)
    last, give, output = lax.optimization_barrier((exchange(deal(line_sum, grad_sum), BAND), swap_yh(give), output))
    d_tokens = tokens_grad(keep, give, d_res, unit1, inv1, vec)

    own, to_core, to_yl, to_both = share(last)
    done = finish((own, swap_core(to_core), swap_yl(to_yl), swap_both(to_both)))
    g_qkv, g_up, g_out, g_down, l1g, l1b, ob, l2g, l2b, db, qvb, upb = done
    return (
        output[None], d_tokens[None], l1g, l1b, g_qkv, qvb, g_out, ob, l2g, l2b, g_up, upb, g_down, db,
    )


def solution(mesh):
    fine = Mesh(mesh.devices.reshape(2, 8, 2, 4, 2), AXES)
    seq_band = P(SEQ, BAND, None)
    flat, flat2 = P(AXES), P(AXES, None)
    in_specs = (
        seq_band, P(SEQ, BAND), flat, flat, flat2, flat, flat2, flat,
        flat, flat, flat2, flat, flat2, flat, seq_band,
    )
    out_specs = (
        seq_band, seq_band, flat, flat, flat2, flat, flat2, flat,
        flat, flat, flat2, flat, flat2, flat,
    )
    return jax.shard_map(per_device, mesh=fine, in_specs=in_specs, out_specs=out_specs, check_vma=False)
```

```python
import math

import jax
import jax.numpy as jnp
from jax import lax
from jax.experimental import pallas as pl
from jax.experimental.pallas import tpu as pltpu
from jax.sharding import Mesh, PartitionSpec as P

D = 768
HEADS = 16
HD = 48
FF = 3072
LEN = 1024
ROWS = 128
BLK = 256
HALF = FF // 2
EPS = 1e-05
SCALE = HD ** (-0.5)
BF = jnp.bfloat16
F32 = jnp.float32
HBM = pl.BlockSpec(memory_space=pltpu.HBM)


def nn(a, b):
    return lax.dot_general(a, b, (((1,), (0,)), ((), ())), preferred_element_type=F32)


def nt(a, b):
    return lax.dot_general(a, b, (((1,), (1,)), ((), ())), preferred_element_type=F32)


def tn(a, b):
    return lax.dot_general(a, b, (((0,), (0,)), ((), ())), preferred_element_type=F32)


def turned(a):
    return a.astype(F32).T.astype(BF)


def params(mebi):
    return pltpu.CompilerParams(vmem_limit_bytes=mebi << 20)


def cost(micros, size):
    return pl.CostEstimate(flops=1000, bytes_accessed=1000, transcendentals=0)


def grid_call(kernel, steps, ins, outs, out_shape, scratch, name, micros, size, mebi=8):
    return pl.pallas_call(
        kernel,
        grid=(steps,),
        in_specs=ins,
        out_specs=outs,
        out_shape=out_shape,
        scratch_shapes=scratch,
        compiler_params=params(mebi),
        cost_estimate=cost(micros, size),
        name=name,
    )


def pinned(*values):
    return tuple(pltpu.with_memory_space_constraint(v, pltpu.HBM) for v in values)


def in_hbm(*shape, dtype=BF):
    return pltpu.HBM(shape, dtype)


def full(*shape):
    return pl.BlockSpec(shape, lambda i: (0,) * len(shape))


def step_block(*shape):
    return pl.BlockSpec((None,) + shape, lambda i: (i,) + (0,) * len(shape))


def iota(shape, axis):
    return lax.broadcasted_iota(jnp.int32, shape, axis)


def like(*shape, dtype=BF):
    return jax.ShapeDtypeStruct(shape, dtype)


WIN = 192
SMALL = 3 * HD
PACK = 32


def unit_order():
    source = iota((D, 1), 0)
    part = lax.rem(source, 24)
    target = part // 12 * (D // 2) + source // 96 * 48 + lax.rem(source, 96) // 24 * 12 + lax.rem(part, 12)
    return (target == iota((D, D), 1)).astype(F32).astype(BF)


def prep_kernel(*refs):
    sources, (own_ref, other_ref, rows_ref, wide_ref, inv_ref), held, (buf, cbuf, sems) = refs[:14], refs[14:19], refs[19:33], refs[33:]
    copies = [pltpu.make_async_copy(a, b, sems.at[i]) for i, (a, b) in enumerate(zip(sources, held))]
    for copy in copies:
        copy.start()
    buf[...] = jnp.zeros(buf.shape, F32)
    cbuf[...] = jnp.zeros(cbuf.shape, F32)
    order = unit_order()
    copies[13].wait()
    unit, inverse = unit_rows(held[13][...].astype(F32))
    rows_ref[...] = held[13][...]
    wide_ref[...] = unit
    inv_ref[...] = inverse
    for copy in copies[:13]:
        copy.wait()
    wq_ref, wu_ref, wo_ref, wd_ref = held[:4]
    vectors, ids_ref = held[4:12], held[12]

    def column(ref, stride, k):
        row = ref[...].astype(F32).reshape(1, ref.shape[0])
        shape = (3, ref.shape[0])
        keep = iota(shape, 1) == iota(shape, 0) * stride + k
        return jnp.sum(jnp.where(keep, jnp.broadcast_to(row, shape), 0.0), axis=1, keepdims=True)

    columns = [column(ref, 1, 0) for ref in vectors[:6]]
    columns += [column(vectors[6], 2, k) for k in range(2)]
    columns += [column(vectors[7], 4, k) for k in range(4)]
    mark = jnp.max(ids_ref[...].astype(F32), axis=1, keepdims=True)
    columns.append(jnp.broadcast_to(mark, (3, 1)))
    lanes = iota((3, 128), 1)
    small = jnp.zeros((3, 128), F32)
    for j, col in enumerate(columns):
        small = jnp.where(lanes == j, jnp.broadcast_to(col, (3, 128)), small)
    wq = wq_ref[...].astype(F32)
    for i in range(4):
        cbuf[8 * i : 8 * i + 3] = wu_ref[:, i * D : (i + 1) * D].astype(F32)
    chosen = nn(cbuf[...].astype(BF), order)
    for k in range(2):
        buf[k, 0:3] = wo_ref[...].astype(F32)
        buf[k, 3:15] = wd_ref[...].astype(F32)
        for q in range(2):
            at = 8 * (2 * k + q)
            for y in range(2):
                to = slice(q * (D // 2), (q + 1) * (D // 2))
                buf[k, 15 + 3 * y : 18 + 3 * y, to] = chosen[at : at + 3, y * (D // 2) : (y + 1) * (D // 2)]
        for b in range(8):
            row, lane, at = 21 + 3 * (b // 4), (b % 4) * WIN, (k * 8 + b) * HD
            for p in range(3):
                buf[k, row : row + 3, lane + p * HD : lane + (p + 1) * HD] = wq[:, p * D + at : p * D + at + HD]
            buf[k, row : row + 3, lane + SMALL : lane + SMALL + 16] = small[:, :16]
    core0 = lax.axis_index("c") == 0
    own_ref[...] = jnp.where(core0, buf[0], buf[1]).astype(BF)
    other_ref[...] = jnp.where(core0, buf[1], buf[0]).astype(BF)


def prep(w_qkv, w_up, w_out, w_down, vectors, ids, x):
    args = (w_qkv, w_up, w_out, w_down) + vectors + (ids, x)
    return grid_call(
        prep_kernel, 1, [HBM] * len(args), [full(PACK, D)] * 2 + [full(ROWS, D)] * 2 + [full(ROWS, 1)],
        [like(PACK, D)] * 2 + [like(ROWS, D), in_hbm(ROWS, D, dtype=F32), in_hbm(ROWS, 1, dtype=F32)],
        [pltpu.VMEM(a.shape, a.dtype) for a in args]
        + [pltpu.VMEM((2, PACK, D), F32), pltpu.VMEM((32, D), F32), pltpu.SemaphoreType.DMA((len(args),))],
        "prep", 2, 100_000,
    )(*pinned(*args))


def groups_of(own, core, line, both, core0, yl0):
    def pick(a, b, c, d):
        return jnp.where(yl0, jnp.where(core0, a, b), jnp.where(core0, c, d))

    return (
        pick(own, core, line, both),
        pick(core, own, both, line),
        pick(line, both, own, core),
        pick(both, line, core, own),
    )


SENT = 48


def spread_kernel(own_ref, core_ref, line_ref, both_ref, out_ref, buf):
    core0, yl0 = lax.axis_index("c") == 0, lax.axis_index("yl") == 0
    aligned = lax.axis_index("c") == lax.axis_index("yl")
    own, core, line, both = (r[...].astype(F32) for r in (own_ref, core_ref, line_ref, both_ref))
    same, cross = jnp.where(aligned, own, line), jnp.where(aligned, core, both)
    buf[...] = jnp.zeros(buf.shape, F32)
    buf[0:15] = jnp.where(core0, same, cross)[0:15]
    buf[15:30] = jnp.where(core0, cross, same)[0:15]
    groups = groups_of(own, core, line, both, core0, yl0)
    for b in range(8):
        y, row, lane = b % 2, 21 + 3 * (b // 4), (b % 4) * WIN
        for g in range(4):
            buf[30 + 3 * g : 33 + 3 * g] = groups[g][15 + 3 * y : 18 + 3 * y]
            buf[42:45, g * WIN : (g + 1) * WIN] = groups[g][row : row + 3, lane : lane + WIN]
        out_ref[b] = buf[...].astype(BF)


def spread(packs):
    return grid_call(
        spread_kernel, 1, [full(PACK, D)] * 4, full(8, SENT, D), like(8, SENT, D),
        [pltpu.VMEM((SENT, D), F32)], "spread", 1, 1_000_000,
    )(*packs)


BLOCK = 240
LINE = 24


def collect_kernel(got_ref, blk_ref, line_ref, buf, lbuf):
    yh = lax.axis_index("yh")
    for b in range(8):
        got = got_ref[b].astype(F32)
        for c in range(2):
            k = c * 8 + b
            buf[3 * k : 3 * k + 3] = got[c * 15 : c * 15 + 3]
            for y in range(2):
                at, row = 144 + y * 48 + 3 * k, 30 + (y * 2 + c) * 3
                buf[at : at + 3] = got[row : row + 3]
        lbuf[3 * b : 3 * b + 3] = got[42:45]
    for x in range(4):
        got = got_ref[2 * x + yh].astype(F32)
        for c in range(2):
            at = 48 + (c * 4 + x) * 12
            buf[at : at + 12] = got[c * 15 + 3 : c * 15 + 15]
    line = lbuf[...].astype(BF)
    for z in range(8):
        line_ref[z] = line
    blk_ref[...] = buf[...].astype(BF)


def collect(got):
    return grid_call(
        collect_kernel, 1, [full(8, SENT, D)], [full(BLOCK, D), full(8, LINE, D)], [in_hbm(BLOCK, D), like(8, LINE, D)],
        [pltpu.VMEM((BLOCK, D), F32), pltpu.VMEM((LINE, D), F32)], "collect", 2, 2_000_000,
    )(got)


def place_of(step):
    return lax.rem(lax.axis_index("x") + step, 4)


RING = (0, 3, 1, 2)


def head_index():
    return lax.axis_index("c") * 8 + lax.axis_index("x") * 2 + lax.axis_index("yh")


def group_rows(group):
    return pl.ds(pl.multiple_of(group * 24, 8), 24)


def pair_groups():
    at = (lax.axis_index("yl") * 8 + lax.axis_index("z")) * 2
    c = lax.axis_index("c")
    return at + c, at + 1 - c


def several_images(small_ref, seq):
    own, other = pair_groups()
    block = small_ref[group_rows(jnp.where(seq == 0, own, other)), :]
    marks = jnp.where(iota(block.shape, 1) == 12, block, 0.0)
    return jnp.max(marks) > 0.5


def piece_cols(k):
    return pl.ds(pl.multiple_of(place_of(RING[k]) * BLK, BLK), BLK)


def piece_copies(pieces, target, sems, s):
    at, copies = 0, []
    for i, piece in enumerate(pieces[5 * s : 5 * s + 5]):
        rows = piece.shape[0]
        copies.append(pltpu.make_async_copy(piece, target.at[s, pl.ds(at, rows)], sems.at[5 * s + i]))
        at += rows
    return copies


def attend_fwd_kernel(*refs):
    pieces = refs[:10]
    (line_ref, unit_hbm, qkv_hbm, att_ref, wide_hbm, lse_hbm, wt_hbm, vec_ref, small_ref,
     xbuf, ubuf, qkv_ref, wide_ref, lse_ref, wt_ref, keys_buf, wbuf, bias, sems) = refs[10:]
    seq = pl.program_id(0)

    def outgoing(s, kinds):
        pairs = ((qkv_ref, qkv_hbm), (wide_ref, wide_hbm), (lse_ref, lse_hbm), (ubuf, unit_hbm))
        return [pltpu.make_async_copy(pairs[i][0].at[s], pairs[i][1].at[s], sems.at[10 + 4 * s + i]) for i in kinds]

    @pl.when(seq == 0)
    def _():
        for s in range(2):
            for copy in piece_copies(pieces, xbuf, sems, s):
                copy.start()
        wbuf[...] = jnp.zeros(wbuf.shape, F32)
        for z in range(8):
            line = line_ref[z].astype(F32)
            for g in range(4):
                y, c = g // 2, g % 2
                at = (y * 8 + z) * 48 + c * 24
                wbuf[at : at + 24, 0:WIN] = line[:, g * WIN : (g + 1) * WIN]
        turned_w = wbuf[...].T
        wt_ref[...] = turned_w[:SMALL].astype(BF)
        pltpu.make_async_copy(wt_ref, wt_hbm, sems.at[18]).start()
        vec_ref[...] = turned_w[SMALL : SMALL + 16]
        small_ref[...] = wbuf[:, SMALL : SMALL + 16]
        head = head_index()
        expand = (iota((HD, 24), 0) // 2 == iota((HD, 24), 1)).astype(F32)
        lane = iota((HD, 16), 1) == 6 + iota((HD, 16), 0) % 2
        for part, group in ((0, head), (2, 16 + head)):
            spreads = nn(expand, small_ref[group_rows(group), :])
            col = jnp.sum(jnp.where(lane, spreads, 0.0), axis=1, keepdims=True)
            bias[part * HD : (part + 1) * HD] = col
        bias[HD : 2 * HD] = jnp.zeros((HD, 1), F32)

    gain, off = vec_ref[0:1], vec_ref[1:2]
    for s in range(2):

        @pl.when(seq == s)
        def _(s=s):
            for copy in piece_copies(pieces, xbuf, sems, s):
                copy.wait()

    for k in range(4):
        rows = slice(k * BLK, (k + 1) * BLK)
        unit = unit_rows(xbuf[seq, rows].astype(F32))[0]
        ubuf[seq, rows] = unit.astype(BF)
        normed = (unit * gain + off).astype(BF)
        qkv_ref[seq, :, piece_cols(k)] = (nt(wt_ref[...], normed) + bias[...]).astype(BF)
    for s in range(2):

        @pl.when(seq == s)
        def _(s=s):
            for copy in outgoing(s, (0, 3)):
                copy.start()

    keys_buf[...] = turned(qkv_ref[seq, HD : 2 * HD, :])

    def block(qb, keys):
        cols = slice(qb * BLK, (qb + 1) * BLK)
        vt = qkv_ref[seq, 2 * HD : 3 * HD, keys]
        s = nn(keys_buf[keys, :], qkv_ref[seq, 0:HD, cols]) * SCALE
        peak = jnp.max(s, axis=0, keepdims=True)
        e = jnp.exp(s - peak)
        total = jnp.sum(e, axis=0, keepdims=True)
        lse_ref[seq, :, cols] = peak + jnp.log(total)
        out = nn(vt, e.astype(BF)) * (1.0 / total)
        wide_ref[seq, :, cols] = out
        out = out.astype(BF)
        low, high = out[:, :ROWS], out[:, ROWS:]
        att_ref[2 * qb, 0] = low
        att_ref[2 * qb, 1] = high
        att_ref[2 * qb + 1, 0] = high
        att_ref[2 * qb + 1, 1] = low

    several = several_images(small_ref, seq)

    @pl.when(jnp.logical_not(several))
    def _():
        for qb in range(LEN // BLK):
            block(qb, slice(0, LEN))

    @pl.when(several)
    def _():
        for qb in range(LEN // BLK):
            block(qb, slice(qb * BLK, (qb + 1) * BLK))

    for s in range(2):

        @pl.when(seq == s)
        def _(s=s):
            for copy in outgoing(s, (1, 2)):
                copy.start()

    @pl.when(seq == 1)
    def _():
        pltpu.make_async_copy(wt_ref, wt_hbm, sems.at[18]).wait()
        for s in range(2):
            for copy in outgoing(s, (0, 1, 2, 3)):
                copy.wait()


def attend_fwd(pieces, line):
    return grid_call(
        attend_fwd_kernel,
        2,
        [HBM] * 10 + [full(8, LINE, D)],
        [HBM, HBM, pl.BlockSpec((8, 2, HD, ROWS), lambda i: (0, 0, 0, i)), HBM, HBM, HBM, full(16, D), full(D, 16)],
        [
            in_hbm(2, LEN, D),
            in_hbm(2, SMALL, LEN),
            like(8, 2, HD, 2 * ROWS),
            in_hbm(2, HD, LEN, dtype=F32),
            in_hbm(2, 1, LEN, dtype=F32),
            in_hbm(SMALL, D),
            like(16, D, dtype=F32),
            like(D, 16, dtype=F32),
        ],
        [
            pltpu.VMEM((2, LEN, D), BF),
            pltpu.VMEM((2, LEN, D), BF),
            pltpu.VMEM((2, SMALL, LEN), BF),
            pltpu.VMEM((2, HD, LEN), F32),
            pltpu.VMEM((2, 1, LEN), F32),
            pltpu.VMEM((SMALL, D), BF),
            pltpu.VMEM((LEN, HD), BF),
            pltpu.VMEM((D, 256), F32),
            pltpu.VMEM((SMALL, 1), F32),
            pltpu.SemaphoreType.DMA((19,)),
        ],
        "attend_fwd",
        9,
        10_000_000,
        28,
    )(*pinned(*pieces), line)


def attend_bwd_kernel(*refs):
    (unit_hbm, qkv_hbm, lse_hbm, wide_hbm, datt_ref, w_hbm, small_ref, vec_ref, vgrad_ref, ugrad_ref,
     down_far, down_near, dother_far, dother_near, out_ref,
     ubuf, qkv_ref, lse_ref, wide_ref, w_ref, dbuf,
     rows_buf, values_buf, dq_buf, dkv_buf, fbuf, acc, acc_bias, gbuf, sems) = refs
    seq = pl.program_id(0)

    def first_in():
        pairs = ((qkv_hbm, qkv_ref), (lse_hbm, lse_ref), (wide_hbm, wide_ref))
        return [pltpu.make_async_copy(a, b, sems.at[10 + i]) for i, (a, b) in enumerate(pairs)]

    def unit_in(s):
        return pltpu.make_async_copy(unit_hbm.at[s], ubuf.at[s], sems.at[s])

    def w_in():
        return pltpu.make_async_copy(w_hbm, w_ref, sems.at[13])

    def out(s):
        far, near = ((down_far, down_near), (dother_far, dother_near))[s]
        return [
            pltpu.make_async_copy(dbuf.at[s, 3], far, sems.at[14 + 2 * s]),
            pltpu.make_async_copy(dbuf.at[s, pl.ds(0, 3)], near, sems.at[15 + 2 * s]),
        ]

    @pl.when(seq == 0)
    def _():
        for copy in first_in() + [w_in()]:
            copy.start()
        for s in range(2):
            unit_in(s).start()
        for copy in first_in():
            copy.wait()

    rows_buf[:, 0 : 3 * HD] = turned(qkv_ref[seq])
    d_out = jnp.concatenate([datt_ref[b] for b in range(8)], axis=1)
    values_buf[:, 0:HD] = turned(d_out)
    delta_all = jnp.sum(d_out.astype(F32) * wide_ref[seq], axis=0, keepdims=True)
    QS, KS = 256, 256

    def scores(qb, kb):
        cols = slice(qb * QS, (qb + 1) * QS)
        keys = slice(kb * KS, (kb + 1) * KS)
        qt = qkv_ref[seq, 0:HD, cols]
        dt = d_out[:, cols]
        probs = jnp.exp(nn(rows_buf[keys, HD : 2 * HD], qt) * SCALE - lse_ref[seq, :, cols])
        ds = (probs * (nn(rows_buf[keys, 2 * HD : 3 * HD], dt) - delta_all[:, cols])).astype(BF)
        return probs.astype(BF), ds

    def products(qb, kb, probs, ds, first_q, first_k):
        cols = slice(qb * QS, (qb + 1) * QS)
        keys = slice(kb * KS, (kb + 1) * KS)
        dq = nn(qkv_ref[seq, HD : 2 * HD, keys], ds)
        dk = nn(ds, rows_buf[cols, 0:HD])
        dv = nn(probs, values_buf[cols, 0:HD])
        if first_q:
            dq_buf[:, cols] = dq
        else:
            dq_buf[:, cols] += dq
        if first_k:
            dkv_buf[keys, 0:HD] = dk
            dkv_buf[keys, HD : 2 * HD] = dv
        else:
            dkv_buf[keys, 0:HD] += dk
            dkv_buf[keys, HD : 2 * HD] += dv

    def sweep(tiles):
        seen_q, seen_k, held = set(), set(), None
        for tile in tiles + [None]:
            now = (tile, scores(*tile)) if tile else None
            if held is not None:
                (qb, kb), (probs, ds) = held
                products(qb, kb, probs, ds, qb not in seen_q, kb not in seen_k)
                seen_q.add(qb)
                seen_k.add(kb)
            held = now

    several = several_images(small_ref, seq)

    @pl.when(jnp.logical_not(several))
    def _():
        sweep([(qb, kb) for qb in range(LEN // QS) for kb in range(LEN // KS)])

    @pl.when(several)
    def _():
        for b in range(4):
            cols = slice(b * BLK, (b + 1) * BLK)
            qt = qkv_ref[seq, 0:HD, cols]
            dt = d_out[:, cols]
            probs = jnp.exp(nn(rows_buf[cols, HD : 2 * HD], qt) * SCALE - lse_ref[seq, :, cols])
            ds = (probs * (nn(rows_buf[cols, 2 * HD : 3 * HD], dt) - delta_all[:, cols])).astype(BF)
            dq_buf[:, cols] = nn(qkv_ref[seq, HD : 2 * HD, cols], ds)
            dkv_buf[cols, 0:HD] = nn(ds, rows_buf[cols, 0:HD])
            dkv_buf[cols, HD : 2 * HD] = nn(probs.astype(BF), values_buf[cols, 0:HD])

    dkv = dkv_buf[...]
    by_row = jnp.concatenate(
        [dq_buf[...].T * SCALE, dkv[:, 0:HD] * SCALE, dkv[:, HD : 2 * HD]], axis=1
    ).astype(BF)
    by_feature = turned(by_row)

    rows_buf[:, 0 : 3 * HD] = by_row
    fbuf[...] = by_feature

    @pl.when(seq == 0)
    def _():
        w_in().wait()

    for k in range(4):
        dbuf[seq, k] = nn(rows_buf[piece_cols(k), 0 : 3 * HD], w_ref[...]).astype(BF)
    for s in range(2):

        @pl.when(seq == s)
        def _(s=s):
            for copy in out(s):
                copy.start()
            unit_in(s).wait()

    gn = jnp.zeros((SMALL, D), F32)
    for k in range(4):
        gn = gn + nn(fbuf[:, piece_cols(k)], ubuf[seq, k * BLK : (k + 1) * BLK])
    gb = jnp.sum(by_feature.astype(F32), axis=1, keepdims=True)

    @pl.when(seq == 0)
    def _():
        acc[...] = gn
        acc_bias[...] = gb

    @pl.when(seq == 1)
    def _():
        w = w_ref[...].astype(F32)
        gb_all = acc_bias[...] + gb
        gn_all = acc[...] + gn
        rows = jnp.concatenate(
            [
                gn_all * vec_ref[0:1] + gb_all * vec_ref[1:2],
                jnp.sum(w * gn_all, axis=0, keepdims=True),
                jnp.sum(w * gb_all, axis=0, keepdims=True),
                vgrad_ref[0:4],
                jnp.zeros((256 - SMALL - 6, D), F32),
            ],
            axis=0,
        )
        gbuf[...] = rows.T
        head = head_index()
        fold = (iota((24, HD), 0) == iota((24, HD), 1) // 2).astype(F32)
        lane = iota((HD, 256), 1) == SMALL + 6 + iota((HD, 256), 0) % 2
        for part, group in ((0, head), (2, 16 + head)):
            spreads = jnp.where(lane, jnp.broadcast_to(gb_all[part * HD : (part + 1) * HD], (HD, 256)), 0.0)
            gbuf[group_rows(group), :] += nn(fold, spreads)
        half = pl.ds(pl.multiple_of(lax.axis_index("c") * (D // 2), 8), D // 2)
        gbuf[half, SMALL + 8 : SMALL + 12] = ugrad_ref[:, 8:12]
        for z in range(8):
            for g in range(4):
                y, c = g // 2, g % 2
                at = (y * 8 + z) * 48 + c * 24
                out_ref[z, :, g * WIN : (g + 1) * WIN] = gbuf[at : at + 24, 0:WIN].astype(BF)
        for s in range(2):
            for copy in out(s):
                copy.wait()


def attend_bwd(unit, qkv, lse, wide, datt, w_t, small, vec, vgrads, ugrads):
    return grid_call(
        attend_bwd_kernel,
        2,
        [HBM] * 4
        + [pl.BlockSpec((8, HD, ROWS), lambda i: (0, 0, i)), HBM, full(D, 16), full(16, D), full(8, D), full(D // 2, 16)],
        [HBM] * 4 + [full(8, LINE, D)],
        [in_hbm(BLK, D), in_hbm(3, BLK, D)] * 2 + [like(8, LINE, D)],
        [
            pltpu.VMEM((2, LEN, D), BF),
            pltpu.VMEM((2, SMALL, LEN), BF),
            pltpu.VMEM((2, 1, LEN), F32),
            pltpu.VMEM((2, HD, LEN), F32),
            pltpu.VMEM((SMALL, D), BF),
            pltpu.VMEM((2, 4, BLK, D), BF),
            pltpu.VMEM((LEN, SMALL), BF),
            pltpu.VMEM((LEN, HD), BF),
            pltpu.VMEM((HD, LEN), F32),
            pltpu.VMEM((LEN, 2 * HD), F32),
            pltpu.VMEM((SMALL, LEN), BF),
            pltpu.VMEM((SMALL, D), F32),
            pltpu.VMEM((SMALL, 1), F32),
            pltpu.VMEM((D, 256), F32),
            pltpu.SemaphoreType.DMA((18,)),
        ],
        "attend_bwd",
        10,
        12_000_000,
        28,
    )(*pinned(unit, qkv, lse, wide), datt, *pinned(w_t), small, vec, vgrads, ugrads)


def out_copies(rows_ref, wbuf, sem):
    return [
        pltpu.make_async_copy(rows_ref.at[k, pl.ds(0, 48)], wbuf.at[pl.ds(48 * k, 48)], sem.at[k]) for k in range(8)
    ]


def branch_kernel(att_ref, rows_ref, own_ref, send_ref, keep_ref, wbuf, sem):
    copies = out_copies(rows_ref, wbuf, sem)
    for copy in copies:
        copy.start()
    parts = [att_ref[:, y].reshape(8 * HD, 2 * ROWS) for y in range(2)]
    keep_ref[...] = parts[0]
    for copy in copies:
        copy.wait()
    for y in range(2):
        out = tn(parts[y], wbuf[...])
        own_ref[y] = out[:ROWS]
        send_ref[y] = out[ROWS:].astype(BF)


def branch(att, rows_full):
    two = full(2, ROWS, D)
    return grid_call(
        branch_kernel, 1, [full(8, 2, HD, 2 * ROWS), HBM], [two, two, full(8 * HD, 2 * ROWS)],
        [like(2, ROWS, D, dtype=F32), like(2, ROWS, D), like(8 * HD, 2 * ROWS)],
        [pltpu.VMEM((8 * HD, D), BF), pltpu.SemaphoreType.DMA((8,))], "branch", 2, 2_000_000, 16,
    )(att, *pinned(rows_full))


def unit_rows(v):
    center = jnp.mean(v, axis=-1, keepdims=True)
    centered = v - center
    inverse = lax.rsqrt(jnp.mean(centered * centered, axis=-1, keepdims=True) + EPS)
    return centered * inverse, inverse


def norm_back(d, unit, inverse, gain):
    dg = d * gain
    return inverse * (dg - jnp.mean(dg, axis=-1, keepdims=True) - unit * jnp.mean(dg * unit, axis=-1, keepdims=True))


def middle_kernel(x_ref, line_ref, own_ref, got_ref, vec_ref, res_ref, n2_ref):
    for y, rows in enumerate((x_ref, line_ref)):
        res = rows[...].astype(F32) + own_ref[y] + got_ref[y].astype(F32) + vec_ref[2:3]
        if y == 0:
            res_ref[...] = res
        n2_ref[y] = (unit_rows(res)[0] * vec_ref[3:4] + vec_ref[4:5]).astype(BF)


def middle(x, line, own, got, vec):
    one, two = full(ROWS, D), full(2, ROWS, D)
    return grid_call(
        middle_kernel, 1, [one, one, two, two, full(16, D)], [one, two],
        [like(ROWS, D, dtype=F32), like(2, ROWS, D)], [], "middle", 1, 2_000_000,
    )(x, line, own, got, vec)


def after_kernel(own_ref, core_ref, got_ref, res_ref, cot_ref, vec_ref, dres_ref, dbr_ref, vg_ref):
    cot = cot_ref[...].astype(F32)
    unit, inverse = unit_rows(res_ref[...])
    dn = own_ref[...] + core_ref[0].astype(F32) + got_ref[...].astype(F32)
    dres = cot + norm_back(dn, unit, inverse, vec_ref[3:4])
    dbr = dres.astype(BF)
    dres_ref[...] = dres
    dbr_ref[...] = dbr
    sums = [dbr.astype(F32), dn * unit, dn, cot]
    for i, v in enumerate(sums):
        vg_ref[i : i + 1] = jnp.sum(v, axis=0, keepdims=True)
    vg_ref[4:8] = jnp.zeros((4, D), F32)


def after(own, core, got, res, cot, vec):
    one = full(ROWS, D)
    return grid_call(
        after_kernel, 1, [one, full(2, ROWS, D), one, one, one, full(16, D)], [one, one, full(8, D)],
        [like(ROWS, D, dtype=F32), like(ROWS, D), like(8, D, dtype=F32)], [], "after", 2, 3_000_000,
    )(own, core, got, res, cot, vec)


def branch_bwd_kernel(att_ref, own_ref, other_ref, rows_ref, grads_in, datt_ref, grads_ref, wbuf, gbuf, sem):
    copies = out_copies(rows_ref, wbuf, sem)
    for copy in copies:
        copy.start()
    d = jnp.concatenate([own_ref[...], other_ref[...]], axis=0)
    gbuf[...] = nn(att_ref[...], d).astype(BF)
    backs = [
        pltpu.make_async_copy(gbuf.at[pl.ds(48 * k, 48)], grads_ref.at[k, pl.ds(0, 48)], sem.at[8 + k]) for k in range(8)
    ]
    for back in backs:
        back.start()
    for copy in copies:
        copy.wait()
    datt_ref[...] = nt(wbuf[...], d).astype(BF)
    for back in backs:
        back.wait()


def branch_bwd(att, own, other, rows_full, grads):
    return pl.pallas_call(
        branch_bwd_kernel,
        grid=(1,),
        in_specs=[full(8 * HD, 2 * ROWS), full(ROWS, D), full(ROWS, D), HBM, HBM],
        out_specs=[full(8 * HD, 2 * ROWS), HBM],
        out_shape=[like(8 * HD, 2 * ROWS), in_hbm(8, BLOCK, D)],
        scratch_shapes=[pltpu.VMEM((8 * HD, D), BF), pltpu.VMEM((8 * HD, D), BF), pltpu.SemaphoreType.DMA((16,))],
        input_output_aliases={4: 1},
        compiler_params=params(8),
        cost_estimate=cost(3, 3_000_000),
        name="branch_bwd",
    )(att, own, other, *pinned(rows_full, grads))


TILE = 256
UNITS = FF // 4
STEPS = UNITS // TILE
FOUR = 4 * ROWS


def unit_rule():
    row = iota((D // 2, 1), 0)
    first = row // 24 * 48 + lax.rem(row, 24) // 6 * 12 + lax.rem(row, 3) * 4
    mine = lax.rem(row, 6) // 3 == lax.axis_index("yh")
    keep = jnp.where(mine, first // 4, -1) == iota((D // 2, UNITS), 1) // 4
    pick = (iota((16, UNITS), 0) == 8 + iota((16, UNITS), 1) % 4).astype(F32)
    return keep, pick


def unit_bias_kernel(small_ref, out_ref):
    keep, pick = unit_rule()
    half = pl.ds(pl.multiple_of(lax.axis_index("c") * (D // 2), 8), D // 2)
    out_ref[...] = jnp.sum(jnp.where(keep, nn(small_ref[half, :], pick), 0.0), axis=0, keepdims=True)


def unit_bias(small):
    return grid_call(
        unit_bias_kernel, 1, [full(D, 16)], full(1, UNITS), like(1, UNITS, dtype=F32), [], "unit_bias", 1, 500_000
    )(small)


def unit_bias_grad_kernel(total_ref, out_ref):
    keep, pick = unit_rule()
    out_ref[...] = nt(jnp.where(keep, jnp.broadcast_to(total_ref[...], keep.shape), 0.0), pick)


def unit_bias_grad(total):
    return grid_call(
        unit_bias_grad_kernel, 1, [full(1, UNITS)], full(D // 2, 16), like(D // 2, 16, dtype=F32), [],
        "unit_bias_grad", 1, 500_000,
    )(total)


def mlp_kernel(*refs):
    rows, cots = refs[:2], refs[2:6]
    (bias_ref, w_ref, oself, ocore, oline, dself, dcore, dline, g_ref, total_ref,
     nbuf, cbuf, up_ref, down_ref, gdbuf, gubuf, out, sems, in_sems) = refs[6:]
    j = pl.program_id(0)

    def weights(step):
        lanes, copies = pl.ds(step * TILE, TILE), []
        for z in range(8):
            for y in range(2):
                source = w_ref.at[z, pl.ds(144 + y * 48, 48), lanes]
                copies.append((source, up_ref.at[pl.ds(y * 384 + z * 48, 48), lanes]))
        for p in range(step * 8, step * 8 + 8):
            copies.append((w_ref.at[p // 3, pl.ds(48 + p % 3 * 32, 32)], down_ref.at[pl.ds(32 * p, 32)]))
        return [pltpu.make_async_copy(a, b, in_sems.at[24 * step + i]) for i, (a, b) in enumerate(copies)]

    @pl.when(j == 0)
    def _():
        for step in range(STEPS):
            for copy in weights(step):
                copy.start()
        for i in range(4):
            nbuf[i * ROWS : (i + 1) * ROWS] = rows[i % 2][i // 2]
            cbuf[i * ROWS : (i + 1) * ROWS] = cots[i][...]

    for step in range(STEPS):

        @pl.when(j == step)
        def _(step=step):
            for copy in weights(step):
                copy.wait()

    spot = pl.ds(pl.multiple_of(j * TILE, TILE), TILE)
    wu, wd = up_ref[:, spot], down_ref[spot, :]
    up = nn(nbuf[...], wu) + bias_ref[...]
    cdf = 0.5 * (1.0 + lax.erf(up * 2.0 ** (-0.5)))
    hidden = (up * cdf).astype(BF)
    dh = nt(cbuf[...], wd).astype(BF).astype(F32)
    slope = cdf + up * jnp.exp(-0.5 * up * up) * (2.0 * math.pi) ** (-0.5)
    d_up = (dh * slope).astype(BF)
    total_ref[...] = jnp.sum(d_up.astype(F32), axis=0, keepdims=True)
    gdbuf[spot, :] = tn(hidden, cbuf[...]).astype(BF)
    gu = tn(nbuf[...], d_up).astype(BF)
    for z in range(8):
        for y in range(2):
            gubuf[z, y * 48 : y * 48 + 48, spot] = gu[y * 384 + z * 48 : y * 384 + z * 48 + 48]

    def backs(step):
        copies = [
            pltpu.make_async_copy(
                gdbuf.at[pl.ds(32 * p, 32)], g_ref.at[p // 3, pl.ds(48 + p % 3 * 32, 32)], sems.at[p]
            )
            for p in range(step * 8, step * 8 + 8)
        ]
        lanes = pl.ds(step * TILE, TILE)
        target = g_ref.at[:, pl.ds(144, 96), lanes]
        return copies + [pltpu.make_async_copy(gubuf.at[:, :, lanes], target, sems.at[24 + step])]

    for step in range(STEPS):

        @pl.when(j == step)
        def _(step=step):
            for back in backs(step):
                back.start()

    out_part = nn(hidden, wd)
    dn_part = nt(d_up, wu)

    @pl.when(j == 0)
    def _():
        out[0] = out_part
        out[1] = dn_part

    @pl.when((j > 0) & (j < STEPS - 1))
    def _():
        out[0] += out_part
        out[1] += dn_part

    @pl.when(j == STEPS - 1)
    def _():
        for i, (own, core, line, part) in enumerate(
            ((oself, ocore, oline, out_part), (dself, dcore, dline, dn_part))
        ):
            whole = out[i] + part
            own[...] = whole[:ROWS]
            core[0] = whole[ROWS : 2 * ROWS].astype(BF)
            line[...] = whole[2 * ROWS : 3 * ROWS]
            core[1] = whole[3 * ROWS :].astype(BF)
        for step in range(STEPS):
            for back in backs(step):
                back.wait()


def mlp(rows, cots, bias, rows_full):
    one, two = full(ROWS, D), full(2, ROWS, D)
    parts = [like(ROWS, D, dtype=F32), like(2, ROWS, D), like(ROWS, D, dtype=F32)]
    cut = pl.BlockSpec((1, TILE), lambda j: (0, j))
    return grid_call(
        mlp_kernel,
        STEPS,
        [two] * 2 + [one] * 2 + [pl.BlockSpec((ROWS, D), lambda j: (1, 0))] * 2 + [cut, HBM],
        [one, two, one] * 2 + [HBM, cut],
        parts * 2 + [in_hbm(8, BLOCK, D), like(1, UNITS, dtype=F32)],
        [
            pltpu.VMEM((FOUR, D), BF),
            pltpu.VMEM((FOUR, D), BF),
            pltpu.VMEM((D, UNITS), BF),
            pltpu.VMEM((UNITS, D), BF),
            pltpu.VMEM((UNITS, D), BF),
            pltpu.VMEM((8, 96, UNITS), BF),
            pltpu.VMEM((2, FOUR, D), F32),
            pltpu.SemaphoreType.DMA((24 + STEPS,)),
            pltpu.SemaphoreType.DMA((24 * STEPS,)),
        ],
        "mlp",
        8,
        8_000_000,
        28,
    )(*rows, *cots, bias, *pinned(rows_full))


def join_kernel(*refs):
    n = len(refs) // 3
    for own, got, out in zip(refs[:n], refs[n : 2 * n], refs[2 * n :]):
        out[...] = (own[...].astype(F32) + got[...].astype(F32)).astype(BF)


def join_far_kernel(own, got, far0, far1):
    total = (own[...].astype(F32) + got[...].astype(F32)).astype(BF)
    far0[...] = total[:ROWS]
    far1[...] = total[ROWS:]


def join_far(own, got):
    return grid_call(
        join_far_kernel, 1, [full(BLK, D)] * 2, [full(ROWS, D)] * 2, [in_hbm(ROWS, D)] * 2, [], "join_far", 1, 1_000_000
    )(*pinned(own), got)


def join(owns, gots):
    n = len(owns)
    return grid_call(
        join_kernel, 1, [full(*v.shape) for v in owns + gots], [full(*v.shape) for v in owns],
        [in_hbm(*v.shape) for v in owns], [], f"join_{n}", 1, 5_000_000, 16,
    )(*pinned(*owns), *gots)


def deal_kernel(got_ref, sum_ref, out_ref, buf, line):
    total = got_ref[0].astype(F32)
    for z in range(1, 8):
        total = total + got_ref[z].astype(F32)
    line[...] = total
    buf[...] = jnp.zeros(buf.shape, F32)
    for b in range(8):
        for c in range(2):
            k = c * 8 + b
            buf[c * 15 : c * 15 + 3] = sum_ref[3 * k : 3 * k + 3].astype(F32)
            at = 48 + (c * 4 + b // 2) * 12
            down = sum_ref[at : at + 12].astype(F32)
            buf[c * 15 + 3 : c * 15 + 15] = jnp.where(lax.axis_index("yh") == b % 2, down, 0.0)
            for y in range(2):
                at, row = 144 + y * 48 + 3 * k, 30 + (y * 2 + c) * 3
                buf[row : row + 3] = sum_ref[at : at + 3].astype(F32)
        buf[42:45] = line[3 * b : 3 * b + 3]
        out_ref[b] = buf[...].astype(BF)


def deal(got, sums):
    return grid_call(
        deal_kernel, 1, [full(8, LINE, D), full(BLOCK, D)], full(8, SENT, D), like(8, SENT, D),
        [pltpu.VMEM((SENT, D), F32), pltpu.VMEM((LINE, D), F32)], "deal", 2, 2_000_000,
    )(got, *pinned(sums))


def share_kernel(got_ref, own_ref, core_ref, line_ref, both_ref, buf, tot):
    core0, yl0 = lax.axis_index("c") == 0, lax.axis_index("yl") == 0
    parts = [got_ref[b].astype(F32) for b in range(8)]
    for y in range(2):
        total = parts[y]
        for b in range(2 + y, 8, 2):
            total = total + parts[b]
        tot[y] = total
    both_units = tot[0] + tot[1]
    buf[...] = jnp.zeros(buf.shape, F32)
    for g in range(4):
        c = g % 2
        buf[g, 0:15] = both_units[c * 15 : c * 15 + 15]
        for y in range(2):
            buf[g, 15 + 3 * y : 18 + 3 * y] = tot[y, 30 + 3 * g : 33 + 3 * g]
        for b in range(8):
            row, lane = 21 + 3 * (b // 4), (b % 4) * WIN
            buf[g, row : row + 3, lane : lane + WIN] = parts[b][42:45, g * WIN : (g + 1) * WIN]
        buf[g, 21:24, SMALL : SMALL + 16] = both_units[42:45, g * WIN + SMALL : g * WIN + SMALL + 16]
    groups = groups_of(*(buf[g] for g in range(4)), core0, yl0)
    own_ref[...] = groups[0]
    core_ref[...] = groups[1].astype(BF)
    line_ref[...] = groups[2].astype(BF)
    both_ref[...] = groups[3].astype(BF)


def share(got):
    one = full(PACK, D)
    return grid_call(
        share_kernel, 1, [full(8, SENT, D)], [one] * 4, [like(PACK, D, dtype=F32)] + [like(PACK, D)] * 3,
        [pltpu.VMEM((4, PACK, D), F32), pltpu.VMEM((2, SENT, D), F32)], "share", 2, 2_000_000,
    )(got)


def finish_kernel(own_ref, core_ref, line_ref, both_ref, wq_ref, wu_ref, wo_ref, wd_ref, *refs):
    vectors, (buf, qbuf, cbuf) = refs[:8], refs[8:]
    core0 = lax.axis_index("c") == 0
    aligned = lax.axis_index("c") == lax.axis_index("yl")
    own, core, line, both = (r[...].astype(F32) for r in (own_ref, core_ref, line_ref, both_ref))
    cbuf[...] = jnp.zeros(cbuf.shape, F32)
    buf[0] = jnp.where(aligned, own + line, core + both)
    wo_ref[...] = buf[0, 0:3]
    wd_ref[...] = buf[0, 3:15]
    mine, theirs = own + line, core + both
    buf[0] = jnp.where(core0, mine, theirs)
    buf[1] = jnp.where(core0, theirs, mine)
    for k in range(2):
        for q in range(2):
            to = slice(q * (D // 2), (q + 1) * (D // 2))
            at = 8 * (2 * k + q)
            for y in range(2):
                cbuf[at : at + 3, y * (D // 2) : (y + 1) * (D // 2)] = buf[k, 15 + 3 * y : 18 + 3 * y, to]
        for b in range(8):
            row, lane, at = 21 + 3 * (b // 4), (b % 4) * WIN, (k * 8 + b) * HD
            for p in range(3):
                qbuf[0:3, p * D + at : p * D + at + HD] = buf[k, row : row + 3, lane + p * HD : lane + (p + 1) * HD]
    wq_ref[...] = qbuf[0:3]
    rest = cbuf[...]
    parts = []
    for _ in range(3):
        parts.append(rest.astype(BF))
        rest = rest - parts[-1].astype(F32)
    sums = nt(jnp.concatenate(parts, axis=0), unit_order())
    total = sums[0:32] + sums[32:64] + sums[64:96]
    for i in range(4):
        wu_ref[:, i * D : (i + 1) * D] = total[8 * i : 8 * i + 3]
    small = (buf[0] + buf[1])[21:24, SMALL : SMALL + 16]

    def row_of(first, stride, count):
        shape = (3, count)
        keep = iota(shape, 1) // stride == iota(shape, 0)
        total = jnp.zeros((1, count), F32)
        for k in range(stride):
            values = jnp.broadcast_to(small[:, first + k : first + k + 1], shape)
            total += jnp.sum(jnp.where(keep & (iota(shape, 1) % stride == k), values, 0.0), axis=0, keepdims=True)
        return total.reshape(count)

    for i in range(6):
        vectors[i][...] = row_of(i, 1, 3)
    vectors[6][...] = row_of(6, 2, 6)
    vectors[7][...] = row_of(8, 4, 12)


def finish(parts):
    shapes = [(3, 3 * D), (3, FF), (3, D), (12, D)] + [(3,)] * 6 + [(6,), (12,)]
    return grid_call(
        finish_kernel, 1, [full(PACK, D)] * 4, [full(*s) for s in shapes], [like(*s, dtype=F32) for s in shapes],
        [pltpu.VMEM((2, PACK, D), F32), pltpu.VMEM((8, 3 * D), F32), pltpu.VMEM((32, D), F32)], "finish", 2, 1_000_000,
    )(*parts)


AXES = ("yl", "z", "c", "x", "yh")
SEQ = ("yl", "z", "c")
BAND = ("x", "yh")
SWAP = [(0, 1), (1, 0)]
RIGHT = [(i, (i + 1) % 4) for i in range(4)]
LEFT = [(i, (i + 3) % 4) for i in range(4)]


def swap_core(v):
    return lax.ppermute(v, "c", SWAP)


def swap_yl(v):
    return lax.ppermute(v, "yl", SWAP)


def swap_yh(v):
    return lax.ppermute(v, "yh", SWAP)


def swap_both(v):
    return lax.ppermute(v, ("yl", "c"), [(0, 3), (1, 2), (2, 1), (3, 0)])


def exchange(v, axes):
    return lax.all_to_all(v, axes, 0, 0, tiled=True)


def ring_far(far0, far1):
    return lax.ppermute(far0, "x", RIGHT), lax.ppermute(far1, "x", LEFT)


def ring_add_kernel(near_ref, from_left, from_right, left_out, right_out):
    left_out[0:ROWS] = near_ref[1, 0:ROWS]
    left_out[ROWS:] = (near_ref[1, ROWS:].astype(F32) + from_right[...].astype(F32)).astype(BF)
    right_out[0:ROWS] = (near_ref[2, 0:ROWS].astype(F32) + from_left[...].astype(F32)).astype(BF)
    right_out[ROWS:] = near_ref[2, ROWS:]


def ring_add(near, from_left, from_right):
    two, one = full(BLK, D), full(ROWS, D)
    return grid_call(
        ring_add_kernel, 1, [full(3, BLK, D), one, one], [two, two], [in_hbm(BLK, D)] * 2, [], "ring_add", 1, 2_000_000
    )(*pinned(near), from_left, from_right)


def settle_kernel(near_ref, left_ref, right_ref, keep_ref, give_ref):
    first = lax.axis_index("yh") == 0
    total = near_ref[0].astype(F32) + left_ref[...].astype(F32) + right_ref[...].astype(F32)
    keep_ref[...] = jnp.where(first, total[:ROWS], total[ROWS:])
    give_ref[...] = jnp.where(first, total[ROWS:], total[:ROWS]).astype(BF)


def settle(near, left, right):
    two, one = full(BLK, D), full(ROWS, D)
    return grid_call(
        settle_kernel, 1, [full(3, BLK, D), two, two], [one, one], [like(ROWS, D, dtype=F32), like(ROWS, D)], [],
        "settle", 1, 2_000_000,
    )(*pinned(near), left, right)


def tokens_kernel(keep_ref, got_ref, res_ref, unit_ref, inv_ref, vec_ref, out_ref):
    d = keep_ref[...] + got_ref[...].astype(F32)
    out_ref[...] = (res_ref[...] + norm_back(d, unit_ref[...], inv_ref[...], vec_ref[0:1])).astype(BF)


def tokens_grad(keep, got, res, unit, inverse, vec):
    one = full(ROWS, D)
    return grid_call(
        tokens_kernel, 1, [one, one, one, one, full(ROWS, 1), full(16, D)], one, like(ROWS, D), [],
        "tokens_grad", 1, 2_000_000,
    )(keep, got, *pinned(res, unit, inverse), vec)


def per_device(
    tokens, image_ids, ln1_gain, ln1_bias, w_qkv, qv_bias, w_out, out_bias,
    ln2_gain, ln2_bias, w_up, up_bias, w_down, down_bias, cotangent,
):
    first = lax.axis_index("yh") == 0
    x = tokens[0]
    cot = cotangent[0]

    pack_own, pack_other, rows, unit1, inv1 = prep(
        w_qkv, w_up, w_out, w_down, (ln1_gain, ln1_bias, out_bias, ln2_gain, ln2_bias, down_bias, qv_bias, up_bias),
        image_ids, x,
    )
    sent = spread((pack_own, swap_core(pack_other), swap_yl(pack_own), swap_both(pack_other)))
    got_yh = swap_yh(rows)
    pair = jnp.stack([jnp.where(first, rows, got_yh), jnp.where(first, got_yh, rows)])
    x_and_cot = jnp.concatenate([x, cot], axis=0)
    got, pair, x_and_cot = lax.optimization_barrier((exchange(sent, BAND), pair, x_and_cot))
    left = lax.ppermute(pair, "x", RIGHT)
    right = lax.ppermute(pair, "x", LEFT)
    block, line = collect(got)
    rows_full = lax.all_gather(block, "z", axis=0)
    far0 = lax.ppermute(left[0], "x", RIGHT)
    far1 = lax.ppermute(right[1], "x", LEFT)
    line_got = exchange(line, "z")
    token_pieces = (pair.reshape(BLK, D), left.reshape(BLK, D), right.reshape(BLK, D), far0, far1)
    other_pieces = tuple(swap_core(v) for v in token_pieces)
    line_got, line_rows, *other_pieces = lax.optimization_barrier((line_got, swap_yh(x_and_cot), *other_pieces))
    cots = (cot, swap_core(cot), line_rows, swap_core(line_rows))

    unit, qkv, att, wide, lse, w_t, vec, small = attend_fwd(token_pieces + tuple(other_pieces), line_got)
    att, *cots = lax.optimization_barrier((att, *cots))
    branch_own, branch_send, att_c = branch(exchange(att, BAND), rows_full)
    residual, n2 = middle(x, line_rows, branch_own, swap_core(branch_send), vec)

    rows = (n2, swap_core(n2))
    o_self, o_core, o_line, d_self, d_core, d_line, grads, utotal = mlp(rows, cots, unit_bias(small), rows_full)
    d_core = swap_core(d_core)
    d_line = swap_yh((d_line + d_core[1].astype(F32)).astype(BF))
    d_line, ugrads = lax.optimization_barrier((d_line, unit_bias_grad(utotal)))
    d_res, d_branch, vgrads = after(d_self, d_core, d_line, residual, cot, vec)
    d_att, grads = branch_bwd(att_c, d_branch, swap_core(d_branch), rows_full, grads)
    grad_sum = lax.psum_scatter(grads, "z", scatter_dimension=0, tiled=True).reshape(BLOCK, D)
    d_att_all = exchange(d_att.reshape(8, HD, 2 * ROWS), BAND)
    o_core = swap_core(o_core)
    o_line = (o_line + o_core[1].astype(F32)).astype(BF)

    own_far, own_near, other_far, other_near, line_grad = attend_bwd(
        unit, qkv, lse, wide, d_att_all, w_t, small, vec, vgrads, ugrads
    )
    line_sum = exchange(line_grad, "z")
    d_far0, d_far1 = join_far(own_far, swap_core(other_far))
    (d_near,) = join((own_near,), (swap_core(other_near),))
    d_left, d_right = ring_add(d_near, *ring_far(d_far0, d_far1))
    line_sum, o_line = lax.optimization_barrier((line_sum, swap_yh(o_line)))
    from_left, from_right = lax.ppermute(d_right, "x", RIGHT), lax.ppermute(d_left, "x", LEFT)
    keep, give = settle(d_near, from_left, from_right)
    output = (residual + o_self + o_core[0].astype(F32) + o_line.astype(F32) + vec[5:6]).astype(BF)
    last, give, output = lax.optimization_barrier((exchange(deal(line_sum, grad_sum), BAND), swap_yh(give), output))
    d_tokens = tokens_grad(keep, give, d_res, unit1, inv1, vec)

    own, to_core, to_yl, to_both = share(last)
    done = finish((own, swap_core(to_core), swap_yl(to_yl), swap_both(to_both)))
    g_qkv, g_up, g_out, g_down, l1g, l1b, ob, l2g, l2b, db, qvb, upb = done
    return (
        output[None], d_tokens[None], l1g, l1b, g_qkv, qvb, g_out, ob, l2g, l2b, g_up, upb, g_down, db,
    )


def solution(mesh):
    fine = Mesh(mesh.devices.reshape(2, 8, 2, 4, 2), AXES)
    seq_band = P(SEQ, BAND, None)
    flat, flat2 = P(AXES), P(AXES, None)
    in_specs = (
        seq_band, P(SEQ, BAND), flat, flat, flat2, flat, flat2, flat,
        flat, flat, flat2, flat, flat2, flat, seq_band,
    )
    out_specs = (
        seq_band, seq_band, flat, flat, flat2, flat, flat2, flat,
        flat, flat, flat2, flat, flat2, flat,
    )
    return jax.shard_map(per_device, mesh=fine, in_specs=in_specs, out_specs=out_specs, check_vma=False)
```
